32 devices in a mesh: dp: 4 (over x, core), blk: 8 (over z, y).
Axes of the slice: x: 2, y: 2, z: 4, core: 2. Of those that a mesh axis runs over, the one named last changes fastest.
Arguments:
- frames: bfloat16 [4, 1024, 768], P('dp', 'blk'), may hold values from -6 to 6
- segment: int32 [4, 1024], P('dp', 'blk'), may hold values from -1 to 16, as said below
- conv_weight: bfloat16 [768, 48, 128], replicated, may hold values from -0.078125 to 0.078125
- conv_bias: bfloat16 [768], replicated, may hold values from -1.5 to 1.5
- qkv_weight: bfloat16 [768, 2304], replicated, may hold values from -0.21875 to 0.21875
- qv_bias: bfloat16 [1536], replicated, may hold values from -1.5 to 1.5
- out_weight: bfloat16 [768, 768], replicated, may hold values from -0.875 to 0.875
- out_bias: bfloat16 [768], replicated, may hold values from -1.5 to 1.5
- norm1_gain: bfloat16 [768], replicated, may hold values from 0.25 to 1.75
- norm1_bias: bfloat16 [768], replicated, may hold values from -1.5 to 1.5
- ffn_in: bfloat16 [768, 3072], replicated, may hold values from -0.21875 to 0.21875
- ffn_in_bias: bfloat16 [3072], replicated, may hold values from -1.5 to 1.5
- ffn_out: bfloat16 [3072, 768], replicated, may hold values from -0.109375 to 0.109375
- ffn_out_bias: bfloat16 [768], replicated, may hold values from -1.5 to 1.5
- norm2_gain: bfloat16 [768], replicated, may hold values from 0.25 to 1.75
- norm2_bias: bfloat16 [768], replicated, may hold values from -1.5 to 1.5
- cotangent: bfloat16 [4, 1024, 768], P('dp', 'blk'), may hold values from -6 to 6
Outputs:
- layer_out: bfloat16 [4, 1024, 768], P('dp', 'blk')
- frames_grad: bfloat16 [4, 1024, 768], P('dp', 'blk')
- conv_weight_grad: float32 [768, 48, 128], P('blk')
- conv_bias_grad: float32 [768], P('blk')
- qkv_weight_grad: float32 [768, 2304], P('blk')
- qv_bias_grad: float32 [1536], P('blk')
- out_weight_grad: float32 [768, 768], P('blk')
- out_bias_grad: float32 [768], P('blk')
- norm1_gain_grad: float32 [768], P('blk')
- norm1_bias_grad: float32 [768], P('blk')
- ffn_in_grad: float32 [768, 3072], P('blk')
- ffn_in_bias_grad: float32 [3072], P('blk')
- ffn_out_grad: float32 [3072, 768], P('blk')
- ffn_out_bias_grad: float32 [768], P('blk')
- norm2_gain_grad: float32 [768], P('blk')
- norm2_bias_grad: float32 [768], P('blk')
The draws below stay inside these ranges and needn't reach their ends.
Inputs may be any that keep to these rules, and one draw needn't show every extreme that they name: `segment`: in each row the frames of a clip are consecutive and clips are numbered 0, 1, 2, ... in order; padding frames, if any, close the row. At least one row holds a clip that starts in the row's first 128 frames and ends in its last 128.
All inputs are finite; a program needn't handle non-finite values.
Results may differ from the reference program's by a relative error of at most 0.02.
Values may be sent and summed in bfloat16 or wider, within the bound.
A program may use at most 320 MiB of HBM per device.

```python
import math
from functools import partial
import jax
import jax.numpy as jnp
from jax import lax

D = 768
HEADS = 12
HEAD_DIM = 64
FF = 3072
GROUPS = 16
KERNEL = 128
BLK_TOK = 128
ROWS_DEV = 1
FRAMES = 1024
ROWS = 4
N_DP = 4


def draw_segment(key, part):
    key = jax.random.fold_in(key, 11)
    len_key, pad_key, pick_key, head_key, tail_key, flip_key = jax.random.split(key, 6)
    clip_lens = jax.random.randint(len_key, (ROWS, 16), FRAMES // 32, FRAMES // 24 + 1)
    clip_ends = jnp.cumsum(clip_lens, axis=1)
    positions = jnp.arange(FRAMES, dtype=jnp.int32)
    drawn = jnp.sum((clip_ends[:, None, :] <= positions[None, :, None]).astype(jnp.int32), axis=2)
    row_fill = FRAMES - jax.random.randint(pad_key, (ROWS, 1), 0, FRAMES // 4)
    head_len = jax.random.randint(head_key, (ROWS, 1), 1, BLK_TOK // 2 + 1)
    long_fill = FRAMES - jax.random.randint(tail_key, (ROWS, 1), 1, BLK_TOK // 2 + 1)
    spanning = (positions[None, :] >= head_len).astype(jnp.int32)
    chosen = jax.random.randint(pick_key, (N_DP,), 0, ROWS_DEV)
    flip = jax.random.randint(flip_key, (), 0, 2)
    row_ids = jnp.arange(ROWS, dtype=jnp.int32)
    group_ids = row_ids // ROWS_DEV
    alternate = jnp.logical_or((group_ids + flip) % 2 == 0, ROWS_DEV > 1)
    is_long = jnp.logical_and(row_ids % ROWS_DEV == chosen[group_ids], alternate)[:, None]
    row_end = jnp.where(is_long, long_fill, row_fill)
    clip_ids = jnp.where(is_long, spanning, drawn)
    return jnp.where(positions[None, :] < row_end, clip_ids, -1).astype(jnp.int32)


def block_levels(own_key, dims, shards, smallest, top_value):
    factor_of, own = 1.0, jax.random.fold_in(own_key, 6)
    for dim, parts in shards:
        steps = jnp.exp(jax.random.uniform(jax.random.fold_in(own, dim), (parts,), jnp.float32, smallest / len(shards), top_value / len(shards)))
        factor_of = factor_of * jnp.repeat(steps, dims[dim] // parts).reshape([-1 if axis == dim else 1 for axis in range(len(dims))])
    return factor_of


def gaussian(key, extent, deviation, bound, cuts=(), kind=jnp.bfloat16):
    level = block_levels(key, extent, cuts, -0.22, 0.18) if cuts else 1.0
    array = jax.random.normal(key, extent, jnp.float32) * deviation * level
    return jnp.minimum(jnp.maximum(array, -bound), bound).astype(kind)


def setup_inputs(seed: int = 0) -> dict:
    seeds = jax.random.split(jax.random.key(seed), 18)
    return {
        "frames": gaussian(seeds[0], (ROWS, FRAMES, D), 1.0, 6.0, ((0, 4), (1, 8))),
        "segment": draw_segment(jax.random.fold_in(seeds[17], 71), 0),
        "conv_weight": gaussian(seeds[2], (D, D // GROUPS, KERNEL), ((D // GROUPS) * KERNEL) ** -0.5, 0.078125),
        "conv_bias": gaussian(seeds[3], (D,), 0.3, 1.5),
        "qkv_weight": gaussian(seeds[4], (D, 3 * D), D ** -0.5, 0.21875),
        "qv_bias": gaussian(seeds[5], (2 * D,), 0.3, 1.5),
        "out_weight": gaussian(seeds[6], (D, D), (D // 16) ** -0.5, 0.875),
        "out_bias": gaussian(seeds[7], (D,), 0.3, 1.5),
        "norm1_gain": jnp.clip(1.0 + 0.15 * jax.random.normal(seeds[8], (D,), jnp.float32), 0.25, 1.75).astype(jnp.bfloat16),
        "norm1_bias": gaussian(seeds[9], (D,), 0.3, 1.5),
        "ffn_in": gaussian(seeds[10], (D, FF), D ** -0.5, 0.21875),
        "ffn_in_bias": gaussian(seeds[11], (FF,), 0.3, 1.5),
        "ffn_out": gaussian(seeds[12], (FF, D), FF ** -0.5, 0.109375),
        "ffn_out_bias": gaussian(seeds[13], (D,), 0.3, 1.5),
        "norm2_gain": jnp.clip(1.0 + 0.15 * jax.random.normal(seeds[14], (D,), jnp.float32), 0.25, 1.75).astype(jnp.bfloat16),
        "norm2_bias": gaussian(seeds[15], (D,), 0.3, 1.5),
        "cotangent": gaussian(seeds[16], (ROWS, FRAMES, D), 1.0, 6.0, ((0, 4), (1, 8))),
    }


@jax.custom_vjp
def low(v):
    return lax.optimization_barrier(v.astype(jnp.bfloat16)).astype(jnp.float32)

@jax.custom_vjp
def low_back(v):
    return v

def low_keep(v):
    return (low(v), None)

def low_pass(kept, grad):
    return (grad,)

def back_keep(v):
    return (v, None)

def back_low(kept, grad):
    return (low(grad),)
low.defvjp(low_keep, low_pass)
low_back.defvjp(back_keep, back_low)
EPS = 1e-05
HIGH = lax.Precision.HIGHEST
ROOT_HALF = 0.7071067811865476

def gelu_value(signal):
    return 0.5 * signal * (1.0 + lax.erf(signal * ROOT_HALF))

def layer_norm(signal, gain_vec, shift_vec):
    average = lax.optimization_barrier(jnp.mean(signal, axis=-1, keepdims=True))
    centred = signal - average
    spread = lax.optimization_barrier(jnp.mean(centred * centred, axis=-1, keepdims=True))
    return centred * lax.rsqrt(spread + EPS) * gain_vec + shift_vec

def attend_block(query_blk, qseg_blk, key_row, value_row, seg_row, score_scale):
    scores = jnp.einsum('qhc,khc->hqk', query_blk, key_row, precision=HIGH) * score_scale
    scores = low_back(scores)
    same_seg = (qseg_blk[:, None] == seg_row[None, :])[None]
    masked_scores = jnp.where(same_seg, scores, -1e+30)
    weights_f = low(jax.nn.softmax(masked_scores, axis=-1))
    return jnp.einsum('hqk,khc->qhc', weights_f, value_row, precision=HIGH)

def attend_rows(queries, keys, values, segment):
    row_count, frame_count = segment.shape
    block_rows = math.gcd(frame_count, 512)
    block_count = frame_count // block_rows
    attend = jax.checkpoint(partial(attend_block, score_scale=HEAD_DIM ** (-0.5)))

    def one_row(row_args):
        query_row, key_row, value_row, seg_row = row_args
        query_blocks = query_row.reshape(block_count, block_rows, HEADS, HEAD_DIM)
        seg_blocks = seg_row.reshape(block_count, block_rows)

        def one_block(block_args):
            return attend(block_args[0], block_args[1], key_row, value_row, seg_row)
        outputs = lax.map(one_block, (query_blocks, seg_blocks))
        return outputs.reshape(frame_count, HEADS * HEAD_DIM)
    return lax.map(one_row, (queries, keys, values, segment))

def forward(frames_f, is_valid, segment, conv_weight, conv_bias, qkv_weight, qv_bias, out_weight, out_bias, norm1_gain, norm1_bias, ffn_in, ffn_in_bias, ffn_out, ffn_out_bias, norm2_gain, norm2_bias):
    row_count, frame_count, model_width = frames_f.shape
    masked = frames_f * is_valid[..., None]
    conv_out = lax.conv_general_dilated(masked, conv_weight, (1,), [(KERNEL // 2, KERNEL // 2 - 1)], dimension_numbers=('NWC', 'OIW', 'NWC'), feature_group_count=GROUPS, precision=HIGH)
    pre_conv = low_back(conv_out + conv_bias)
    mixed_in = frames_f + gelu_value(pre_conv)
    mixed_low = low(mixed_in)
    zero_bias = jnp.zeros((model_width,), jnp.float32)
    full_bias = jnp.concatenate([qv_bias[:model_width], zero_bias, qv_bias[model_width:]])
    project = jnp.einsum('rtd,de->rte', mixed_low, qkv_weight, precision=HIGH) + full_bias
    project = low(low_back(project))
    queries = project[..., :model_width].reshape(row_count, frame_count, HEADS, HEAD_DIM)
    keys = project[..., model_width:2 * model_width].reshape(row_count, frame_count, HEADS, HEAD_DIM)
    values = project[..., 2 * model_width:].reshape(row_count, frame_count, HEADS, HEAD_DIM)
    attended = low(low_back(attend_rows(queries, keys, values, segment)))
    branch = low_back(jnp.einsum('rte,ed->rtd', attended, out_weight, precision=HIGH) + out_bias)
    hidden = layer_norm(mixed_in + branch, norm1_gain, norm1_bias)
    ffn_pre = low_back(jnp.einsum('rtd,df->rtf', low(hidden), ffn_in, precision=HIGH) + ffn_in_bias)
    ffn_act = low(gelu_value(ffn_pre))
    ffn_branch = low_back(jnp.einsum('rtf,fd->rtd', ffn_act, ffn_out, precision=HIGH) + ffn_out_bias)
    return layer_norm(hidden + ffn_branch, norm2_gain, norm2_bias)

def reference(frames, segment, conv_weight, conv_bias, qkv_weight, qv_bias, out_weight, out_bias, norm1_gain, norm1_bias, ffn_in, ffn_in_bias, ffn_out, ffn_out_bias, norm2_gain, norm2_bias, cotangent):
    is_valid = (segment >= 0).astype(jnp.float32)

    def wrapped(frames_f, conv_w, conv_b, qkv_w, qv_b, out_w, out_b, gain_one, shift_one, in_w, in_b, out_w2, out_b2, gain_two, shift_two):
        return forward(frames_f, is_valid, segment, conv_w, conv_b, qkv_w, qv_b, out_w, out_b, gain_one, shift_one, in_w, in_b, out_w2, out_b2, gain_two, shift_two)
    result, pullback = jax.vjp(wrapped, frames.astype(jnp.float32), conv_weight.astype(jnp.float32), conv_bias.astype(jnp.float32), qkv_weight.astype(jnp.float32), qv_bias.astype(jnp.float32), out_weight.astype(jnp.float32), out_bias.astype(jnp.float32), norm1_gain.astype(jnp.float32), norm1_bias.astype(jnp.float32), ffn_in.astype(jnp.float32), ffn_in_bias.astype(jnp.float32), ffn_out.astype(jnp.float32), ffn_out_bias.astype(jnp.float32), norm2_gain.astype(jnp.float32), norm2_bias.astype(jnp.float32))
    gradients = pullback(cotangent.astype(jnp.float32))
    return (result.astype(jnp.bfloat16), gradients[0].astype(jnp.bfloat16), gradients[1], gradients[2], gradients[3], gradients[4], gradients[5], gradients[6], gradients[7], gradients[8], gradients[9], gradients[10], gradients[11], gradients[12], gradients[13], gradients[14])
```

```python
import functools
import math

import jax
import jax.numpy as jnp
from jax import lax
from jax.experimental import pallas as pl
from jax.experimental.pallas import tpu as pltpu
from jax.sharding import PartitionSpec as P

HEADS = 12
GROUPS = 16


EPS = 1e-05
ROOT_HALF = 0.7071067811865476
DENSITY_CONST = 0.3989422804014327


def with_halo(x, sides, width):
    for axis, dim in sides:
        size, length = (lax.axis_size(axis), x.shape[dim])
        up = [(i, (i + 1) % size) for i in range(size - 1)]
        down = [(j, i) for i, j in up]
        last = lax.slice_in_dim(x, length - width, length, axis=dim)
        initial = lax.slice_in_dim(x, 0, width, axis=dim)
        before = lax.ppermute(last, axis, up)
        after = lax.ppermute(initial, axis, down)
        x = jnp.concatenate([before, x, after], axis=dim)
    return x


def from_behind(value, axis, steps):
    count = lax.axis_size(axis)
    pairs = [(source, (source + steps) % count) for source in range(count)]
    return lax.ppermute(value, axis, pairs)


def gelu_value(signal):
    return 0.5 * signal * (1.0 + lax.erf(signal * ROOT_HALF))


def gelu_slope(signal):
    return (
        0.5 * (1.0 + lax.erf(signal * ROOT_HALF))
        + signal * jnp.exp(-0.5 * signal * signal) * DENSITY_CONST
    )


def norm_forward(signal, gain_vec, shift_vec):
    average = jnp.mean(signal, axis=-1, keepdims=True)
    centred = signal - average
    inv_std = lax.rsqrt(jnp.mean(centred * centred, axis=-1, keepdims=True) + EPS)
    normed = centred * inv_std
    return (normed * gain_vec + shift_vec, normed, inv_std)


def norm_backward(grad_in, normed, inv_std, gain_vec):
    scaled = grad_in * gain_vec
    result = inv_std * (
        scaled
        - jnp.mean(scaled, axis=-1, keepdims=True)
        - normed * jnp.mean(scaled * normed, axis=-1, keepdims=True)
    )
    return (result, jnp.sum(grad_in * normed, axis=0), jnp.sum(grad_in, axis=0))


def block_grads(
    query_h, dout_h, query_seg, log_tot, row_delta, key_h, value_h, key_seg, score_scale
):
    scores = (
        jnp.einsum("rqhc,rkhc->rhqk", query_h, key_h, preferred_element_type=jnp.float32)
        * score_scale
    )
    same_seg = (query_seg[:, :, None] == key_seg[:, None, :])[:, None]
    weights_f = jnp.where(same_seg, jnp.exp(scores - log_tot[..., None]), 0.0)
    grad_prob = jnp.einsum("rqhc,rkhc->rhqk", dout_h, value_h, preferred_element_type=jnp.float32)
    grad_score = (weights_f * (grad_prob - row_delta[..., None])).astype(jnp.bfloat16)
    query_part = score_scale * jnp.einsum(
        "rhqk,rkhc->rqhc", grad_score, key_h, preferred_element_type=jnp.float32
    )
    key_part = score_scale * jnp.einsum(
        "rhqk,rqhc->rkhc", grad_score, query_h, preferred_element_type=jnp.float32
    )
    value_part = jnp.einsum(
        "rhqk,rqhc->rkhc",
        weights_f.astype(jnp.bfloat16),
        dout_h,
        preferred_element_type=jnp.float32,
    )
    return (query_part, key_part, value_part)


def ring_shards(
    frames,
    segment,
    conv_weight,
    conv_bias,
    qkv_weight,
    qv_bias,
    out_weight,
    out_bias,
    norm1_gain,
    norm1_bias,
    ffn_in,
    ffn_in_bias,
    ffn_out,
    ffn_out_bias,
    norm2_gain,
    norm2_bias,
    cotangent,
):
    row_count, block_len, model_width = frames.shape
    token_count = row_count * block_len
    group_width = conv_weight.shape[1]
    kernel = conv_weight.shape[2]
    half_kernel = kernel // 2
    head_dim = model_width // HEADS
    score_scale = head_dim ** (-0.5)
    cycle_len = lax.axis_size("blk")
    is_valid = segment >= 0
    masked = jnp.where(is_valid[..., None], frames, jnp.zeros_like(frames))
    padded = with_halo(masked, (("blk", 1),), half_kernel)
    conv_out = lax.conv_general_dilated(
        padded,
        conv_weight,
        (1,),
        "VALID",
        dimension_numbers=("NWC", "OIW", "NWC"),
        feature_group_count=GROUPS,
        preferred_element_type=jnp.float32,
    )
    pre_conv = conv_out[:, :block_len].reshape(token_count, model_width) + conv_bias.astype(
        jnp.float32
    )
    mixed_in = frames.reshape(token_count, model_width).astype(jnp.float32) + gelu_value(pre_conv)
    mixed_low = mixed_in.astype(jnp.bfloat16)
    pair_bias = qv_bias.astype(jnp.float32)
    zero_bias = jnp.zeros((model_width,), jnp.float32)
    full_bias = jnp.concatenate([pair_bias[:model_width], zero_bias, pair_bias[model_width:]])
    project = (
        jnp.dot(mixed_low, qkv_weight, preferred_element_type=jnp.float32) + full_bias
    ).astype(jnp.bfloat16)
    project = project.reshape(row_count, block_len, 3 * model_width)
    query_heads = project[..., :model_width].reshape(row_count, block_len, HEADS, head_dim)
    keys_local = project[..., model_width : 2 * model_width]
    values_local = project[..., 2 * model_width :]
    key_heads = keys_local.reshape(row_count, block_len, HEADS, head_dim)
    value_heads = values_local.reshape(row_count, block_len, HEADS, head_dim)
    query_seg = segment.astype(jnp.bfloat16)
    start_carry = (
        jnp.full((row_count, HEADS, block_len), -1e30, jnp.float32),
        jnp.zeros((row_count, HEADS, block_len), jnp.float32),
        jnp.zeros((row_count, HEADS, block_len, head_dim), jnp.float32),
    )
    key_piece = lax.all_gather(keys_local, "blk", axis=1, tiled=True)
    value_piece = lax.all_gather(values_local, "blk", axis=1, tiled=True)
    seg_piece = lax.all_gather(query_seg, "blk", axis=1, tiled=True)
    piece_len = key_piece.shape[1]
    block_size = math.gcd(piece_len, 512)

    def one_block(block_index, inner_carry):
        running_max, denominator, numerator = inner_carry
        offset = block_index * block_size
        key_block = lax.dynamic_slice_in_dim(key_piece, offset, block_size, 1).reshape(
            row_count, block_size, HEADS, head_dim
        )
        value_block = lax.dynamic_slice_in_dim(value_piece, offset, block_size, 1).reshape(
            row_count, block_size, HEADS, head_dim
        )
        seg_block = lax.dynamic_slice_in_dim(seg_piece, offset, block_size, 1)
        scores = (
            jnp.einsum(
                "rqhc,rkhc->rhqk", query_heads, key_block, preferred_element_type=jnp.float32
            )
            * score_scale
        )
        same_seg = (query_seg[:, :, None] == seg_block[:, None, :])[:, None]
        masked_scores = jnp.where(same_seg, scores, -1e30)
        new_max = jnp.maximum(running_max, jnp.max(masked_scores, axis=-1))
        weights_f = jnp.where(same_seg, jnp.exp(masked_scores - new_max[..., None]), 0.0)
        rescale = jnp.exp(running_max - new_max)
        denominator = denominator * rescale + jnp.sum(weights_f, axis=-1)
        numerator = numerator * rescale[..., None] + jnp.einsum(
            "rhqk,rkhc->rhqc",
            weights_f.astype(jnp.bfloat16),
            value_block,
            preferred_element_type=jnp.float32,
        )
        return (new_max, denominator, numerator)

    running_max, denominator, numerator = lax.fori_loop(
        0, piece_len // block_size, one_block, start_carry
    )
    log_total = running_max + jnp.log(denominator)
    attended_heads = (numerator / denominator[..., None]).transpose(0, 2, 1, 3)
    attended = attended_heads.reshape(token_count, model_width)
    attn_low = attended.astype(jnp.bfloat16)
    branch = jnp.dot(attn_low, out_weight, preferred_element_type=jnp.float32) + out_bias.astype(
        jnp.float32
    )
    gain_one = norm1_gain.astype(jnp.float32)
    hidden_norm, normed_one, inv_one = norm_forward(
        mixed_in + branch, gain_one, norm1_bias.astype(jnp.float32)
    )
    hidden_low = hidden_norm.astype(jnp.bfloat16)
    ffn_pre = jnp.dot(hidden_low, ffn_in, preferred_element_type=jnp.float32) + ffn_in_bias.astype(
        jnp.float32
    )
    ffn_act = gelu_value(ffn_pre).astype(jnp.bfloat16)
    ffn_branch = jnp.dot(
        ffn_act, ffn_out, preferred_element_type=jnp.float32
    ) + ffn_out_bias.astype(jnp.float32)
    gain_two = norm2_gain.astype(jnp.float32)
    layer_out, normed_two, inv_two = norm_forward(
        hidden_norm + ffn_branch, gain_two, norm2_bias.astype(jnp.float32)
    )
    grad_top = cotangent.reshape(token_count, model_width).astype(jnp.float32)
    grad_second, norm2_gain_grad, norm2_bias_grad = norm_backward(
        grad_top, normed_two, inv_two, gain_two
    )
    grad_branch_two = grad_second.astype(jnp.bfloat16)
    ffn_out_grad = jnp.einsum(
        "nf,nd->fd", ffn_act, grad_branch_two, preferred_element_type=jnp.float32
    )
    ffn_out_bias_grad = jnp.sum(grad_branch_two.astype(jnp.float32), axis=0)
    grad_act = jnp.einsum("nd,fd->nf", grad_branch_two, ffn_out, preferred_element_type=jnp.float32)
    grad_pre = (grad_act * gelu_slope(ffn_pre)).astype(jnp.bfloat16)
    ffn_in_grad = jnp.einsum("nd,nf->df", hidden_low, grad_pre, preferred_element_type=jnp.float32)
    ffn_in_bias_grad = jnp.sum(grad_pre.astype(jnp.float32), axis=0)
    grad_hidden = grad_second + jnp.einsum(
        "nf,df->nd", grad_pre, ffn_in, preferred_element_type=jnp.float32
    )
    grad_first, norm1_gain_grad, norm1_bias_grad = norm_backward(
        grad_hidden, normed_one, inv_one, gain_one
    )
    grad_branch = grad_first.astype(jnp.bfloat16)
    out_weight_grad = jnp.einsum(
        "ne,nd->ed", attn_low, grad_branch, preferred_element_type=jnp.float32
    )
    out_bias_grad = jnp.sum(grad_branch.astype(jnp.float32), axis=0)
    grad_att = jnp.einsum("nd,ed->ne", grad_branch, out_weight, preferred_element_type=jnp.float32)
    grad_heads = grad_att.astype(jnp.bfloat16).reshape(row_count, block_len, HEADS, head_dim)
    row_delta = jnp.einsum("rqhc,rqhc->rhq", grad_heads.astype(jnp.float32), attended_heads)
    zero_heads = jnp.zeros((row_count, block_len, HEADS, head_dim), jnp.float32)

    def key_step(carried):
        key_block, value_block, seg_block, key_grad, value_grad, query_grad = carried
        query_part, key_part, value_part = block_grads(
            query_heads,
            grad_heads,
            query_seg,
            log_total,
            row_delta,
            key_block,
            value_block,
            seg_block,
            score_scale,
        )
        query_grad = query_grad + query_part
        key_grad = key_grad + key_part
        value_grad = value_grad + value_part
        key_block, value_block, seg_block = from_behind(
            (key_block, value_block, seg_block), "blk", 1
        )
        key_grad, value_grad = (
            from_behind(key_grad.astype(jnp.bfloat16), "blk", 1).astype(key_grad.dtype),
            from_behind(value_grad.astype(jnp.bfloat16), "blk", 1).astype(value_grad.dtype),
        )
        return (key_block, value_block, seg_block, key_grad, value_grad, query_grad)

    def four_steps(turn_index, carried):
        for repeat in range(4):
            carried = key_step(carried)
        return carried

    final_state = lax.fori_loop(
        0,
        cycle_len // 4,
        four_steps,
        (key_heads, value_heads, query_seg, zero_heads, zero_heads, zero_heads),
    )
    key_grad, value_grad, query_grad = (final_state[3], final_state[4], final_state[5])
    grad_project = jnp.concatenate(
        [
            query_grad.reshape(token_count, model_width),
            key_grad.reshape(token_count, model_width),
            value_grad.reshape(token_count, model_width),
        ],
        axis=1,
    ).astype(jnp.bfloat16)
    qkv_weight_grad = jnp.einsum(
        "nd,ne->de", mixed_low, grad_project, preferred_element_type=jnp.float32
    )
    bias_sums = jnp.sum(grad_project.astype(jnp.float32), axis=0)
    qv_bias_grad = jnp.concatenate([bias_sums[:model_width], bias_sums[2 * model_width :]])
    grad_mixed = grad_first + jnp.einsum(
        "ne,de->nd", grad_project, qkv_weight, preferred_element_type=jnp.float32
    )
    grad_conv = (grad_mixed * gelu_slope(pre_conv)).astype(jnp.bfloat16)
    conv_bias_grad = jnp.sum(grad_conv.astype(jnp.float32), axis=0)
    grad_conv_rows = grad_conv.reshape(row_count, block_len, model_width)
    grad_padded = with_halo(grad_conv_rows, (("blk", 1),), half_kernel)
    flipped = conv_weight.reshape(GROUPS, group_width, group_width, kernel).transpose(0, 2, 1, 3)
    flipped = flipped.reshape(model_width, group_width, kernel)[:, :, ::-1]
    back_conv = lax.conv_general_dilated(
        grad_padded,
        flipped,
        (1,),
        "VALID",
        dimension_numbers=("NWC", "OIW", "NWC"),
        feature_group_count=GROUPS,
        preferred_element_type=jnp.float32,
    )[:, 1:]
    frames_grad = (
        grad_mixed.reshape(row_count, block_len, model_width)
        + jnp.where(is_valid[..., None], back_conv, 0.0)
    ).astype(jnp.bfloat16)
    conv_weight_grad = lax.conv_general_dilated(
        padded,
        grad_conv_rows,
        (1,),
        "VALID",
        dimension_numbers=("CWN", "IWO", "CNW"),
        batch_group_count=GROUPS,
        preferred_element_type=jnp.float32,
    )[:, :, :kernel]
    (
        conv_weight_part,
        conv_bias_part,
        qkv_weight_part,
        qv_bias_part,
        out_weight_part,
        out_bias_part,
        gain_one_part,
        shift_one_part,
        ffn_in_part,
        ffn_in_bias_part,
        ffn_out_part,
        ffn_out_bias_part,
        gain_two_part,
        shift_two_part,
    ) = (
        lax.psum_scatter(conv_weight_grad, "blk", scatter_dimension=0, tiled=True),
        lax.psum_scatter(conv_bias_grad, "blk", scatter_dimension=0, tiled=True),
        lax.psum_scatter(qkv_weight_grad, "blk", scatter_dimension=0, tiled=True),
        lax.psum_scatter(qv_bias_grad, "blk", scatter_dimension=0, tiled=True),
        lax.psum_scatter(out_weight_grad, "blk", scatter_dimension=0, tiled=True),
        lax.psum_scatter(out_bias_grad, "blk", scatter_dimension=0, tiled=True),
        lax.psum_scatter(norm1_gain_grad, "blk", scatter_dimension=0, tiled=True),
        lax.psum_scatter(norm1_bias_grad, "blk", scatter_dimension=0, tiled=True),
        lax.psum_scatter(ffn_in_grad, "blk", scatter_dimension=0, tiled=True),
        lax.psum_scatter(ffn_in_bias_grad, "blk", scatter_dimension=0, tiled=True),
        lax.psum_scatter(ffn_out_grad, "blk", scatter_dimension=0, tiled=True),
        lax.psum_scatter(ffn_out_bias_grad, "blk", scatter_dimension=0, tiled=True),
        lax.psum_scatter(norm2_gain_grad, "blk", scatter_dimension=0, tiled=True),
        lax.psum_scatter(norm2_bias_grad, "blk", scatter_dimension=0, tiled=True),
    )
    totals = (
        lax.psum(conv_weight_part.astype(jnp.bfloat16), "dp").astype(jnp.float32),
        lax.psum(conv_bias_part.astype(jnp.bfloat16), "dp").astype(jnp.float32),
        lax.psum(qkv_weight_part.astype(jnp.bfloat16), "dp").astype(jnp.float32),
        lax.psum(qv_bias_part.astype(jnp.bfloat16), "dp").astype(jnp.float32),
        lax.psum(out_weight_part.astype(jnp.bfloat16), "dp").astype(jnp.float32),
        lax.psum(out_bias_part.astype(jnp.bfloat16), "dp").astype(jnp.float32),
        lax.psum(gain_one_part.astype(jnp.bfloat16), "dp").astype(jnp.float32),
        lax.psum(shift_one_part.astype(jnp.bfloat16), "dp").astype(jnp.float32),
        lax.psum(ffn_in_part.astype(jnp.bfloat16), "dp").astype(jnp.float32),
        lax.psum(ffn_in_bias_part.astype(jnp.bfloat16), "dp").astype(jnp.float32),
        lax.psum(ffn_out_part.astype(jnp.bfloat16), "dp").astype(jnp.float32),
        lax.psum(ffn_out_bias_part.astype(jnp.bfloat16), "dp").astype(jnp.float32),
        lax.psum(gain_two_part.astype(jnp.bfloat16), "dp").astype(jnp.float32),
        lax.psum(shift_two_part.astype(jnp.bfloat16), "dp").astype(jnp.float32),
    )
    return (
        layer_out.reshape(row_count, block_len, model_width).astype(jnp.bfloat16),
        frames_grad,
        totals[0],
        totals[1],
        totals[2],
        totals[3],
        totals[4],
        totals[5],
        totals[6],
        totals[7],
        totals[8],
        totals[9],
        totals[10],
        totals[11],
        totals[12],
        totals[13],
    )


MESH = pl.DeviceIdType.MESH
LANES = 128
TAP_STEP = 16
VMEM = pl.BlockSpec(memory_space=pltpu.VMEM)


def peer(me, step, count):
    return lax.rem(me + step, count)


def greet(me, count):
    barrier = pltpu.get_barrier_semaphore()
    for step in range(1, count):
        pl.semaphore_signal(
            barrier, inc=1, device_id={"blk": peer(me, step, count)}, device_id_type=MESH
        )
    pl.semaphore_wait(barrier, count - 1)


def remote(src, dst, send_sem, recv_sem, target):
    copy = pltpu.make_async_remote_copy(
        src_ref=src,
        dst_ref=dst,
        send_sem=send_sem,
        recv_sem=recv_sem,
        device_id={"blk": target},
        device_id_type=MESH,
    )
    copy.start()
    return copy


def lane_block(index):
    return pl.ds(pl.multiple_of(index * LANES, LANES), LANES)


def row_block(index, size):
    return pl.ds(pl.multiple_of(index * size, size), size)


def swap_blocks(tiles, width):
    count = len(tiles)
    lane = lax.broadcasted_iota(jnp.int32, tiles[0].shape, 1) // width
    tiles = list(tiles)
    step = count // 2
    while step:
        low = (lane & step) == 0
        for u in range(count):
            if u & step == 0:
                one, two = tiles[u], tiles[u + step]
                tiles[u] = jnp.where(low, one, pltpu.roll(two, step * width, 1))
                tiles[u + step] = jnp.where(low, pltpu.roll(one, LANES - step * width, 1), two)
        step //= 2
    return tiles


def spread_taps(source, offset, direction, stage_ref, out_ref):
    rows, length = source.shape
    blocks = out_ref.shape[1] // LANES
    for tap in range(TAP_STEP):
        shift = (length - offset - direction * tap) % length
        moved = pltpu.roll(source, shift, 1)
        for block in range(blocks):
            stage_ref[block, pl.ds(tap, rows, stride=TAP_STEP), :] = moved[
                :, block * LANES : (block + 1) * LANES
            ]
    for block in range(blocks):
        out_ref[:, block * LANES : (block + 1) * LANES] = stage_ref[block].astype(jnp.bfloat16)


def conv_forward_kernel(
    count,
    frames_ref,
    seg_ref,
    weight_ref,
    pre_ref,
    column_ref,
    segs_ref,
    turned_ref,
    result_ref,
    back_ref,
    stage_ref,
    taps_ref,
    mix_ref,
    send_one,
    recv_one,
    send_two,
    recv_two,
    send_seg,
    recv_seg,
):
    me = lax.axis_index("blk")
    groups, width = weight_ref.shape[0], weight_ref.shape[1]
    channels = groups * width
    steps = LANES // TAP_STEP
    length = count * LANES
    valid = (seg_ref[...] >= 0).astype(jnp.float32)
    turned_ref[...] = (frames_ref[...].astype(jnp.float32).T * valid).astype(jnp.bfloat16)
    greet(me, count)
    copies = []
    for step in range(1, count):
        target = peer(me, step, count)
        copies.append(
            remote(
                turned_ref.at[row_block(target, channels), :],
                column_ref.at[:, lane_block(me + 1)],
                send_one.at[step],
                recv_one.at[step],
                target,
            )
        )
        copies.append(
            remote(seg_ref, segs_ref.at[me], send_seg.at[step], recv_seg.at[step], target)
        )
    column_ref[:, lane_block(me + 1)] = turned_ref[row_block(me, channels), :]
    column_ref[:, :LANES] = jnp.zeros((channels, LANES), jnp.bfloat16)
    column_ref[:, length + LANES :] = jnp.zeros((channels, LANES), jnp.bfloat16)
    segs_ref[me] = seg_ref[...]
    for group in range(groups):
        for block in range(width // steps):
            tiles = [
                weight_ref[group, block * steps + u].astype(jnp.float32) for u in range(steps)
            ]
            for a, tile in enumerate(swap_blocks(tiles, TAP_STEP)):
                mix_ref[
                    group, a * width : (a + 1) * width, block * LANES : (block + 1) * LANES
                ] = tile.astype(jnp.bfloat16)
    for copy in copies:
        copy.wait()
    for group in range(groups):
        rows = slice(group * width, (group + 1) * width)
        source = column_ref[rows, :].astype(jnp.float32)
        spread_taps(source, LANES // 2, 1, stage_ref, taps_ref)
        product = jnp.dot(mix_ref[group], taps_ref[...], preferred_element_type=jnp.float32)
        total = product[:width, :length]
        span = product.shape[1]
        for a in range(1, steps):
            part = pltpu.roll(
                product[a * width : (a + 1) * width, :], span - a * TAP_STEP, 1
            )
            total = total + part[:, :length]
        result_ref[rows, :] = total
    copies = []
    for step in range(1, count):
        target = peer(me, step, count)
        copies.append(
            remote(
                result_ref.at[:, lane_block(target)],
                back_ref.at[row_block(me, channels), :],
                send_two.at[step],
                recv_two.at[step],
                target,
            )
        )
    back_ref[row_block(me, channels), :] = result_ref[:, lane_block(me)]
    for copy in copies:
        copy.wait()
    pre_ref[...] = back_ref[...].T


def conv_forward(frames, seg, weight, count):
    tokens, features = frames.shape
    groups, width, _, kernel = weight.shape
    channels = groups * width
    length = count * LANES
    span = length + LANES
    rows = width * TAP_STEP
    steps = kernel // TAP_STEP
    sems = [pltpu.SemaphoreType.DMA((count,)) for _ in range(6)]
    return pl.pallas_call(
        functools.partial(conv_forward_kernel, count),
        out_shape=(
            jax.ShapeDtypeStruct((tokens, features), jnp.float32),
            jax.ShapeDtypeStruct((channels, span + LANES), jnp.bfloat16),
            jax.ShapeDtypeStruct((count, 1, LANES), jnp.int32),
        ),
        in_specs=[VMEM] * 3,
        out_specs=(VMEM,) * 3,
        scratch_shapes=[
            pltpu.VMEM((features, tokens), jnp.bfloat16),
            pltpu.VMEM((channels, length), jnp.float32),
            pltpu.VMEM((features, tokens), jnp.float32),
            pltpu.VMEM((span // LANES, rows, LANES), jnp.float32),
            pltpu.VMEM((rows, span), jnp.bfloat16),
            pltpu.VMEM((groups, steps * width, rows), jnp.bfloat16),
        ]
        + sems,
        compiler_params=pltpu.CompilerParams(
            collective_id=0, has_side_effects=True, vmem_limit_bytes=48 * 2**20
        ),
        name="conv_forward",
    )(frames, seg, weight)


def conv_backward_kernel(
    count,
    grad_ref,
    column_ref,
    weight_ref,
    back_ref,
    dweight_ref,
    turned_ref,
    gcol_ref,
    result_ref,
    home_ref,
    stage_ref,
    taps_ref,
    mix_ref,
    shifted_ref,
    send_one,
    recv_one,
    send_two,
    recv_two,
):
    me = lax.axis_index("blk")
    channels, width = weight_ref.shape[0], weight_ref.shape[1]
    groups = channels // width
    steps = LANES // TAP_STEP
    length = count * LANES
    turned_ref[...] = grad_ref[...].astype(jnp.float32).T.astype(jnp.bfloat16)
    greet(me, count)
    copies = []
    for step in range(1, count):
        target = peer(me, step, count)
        copies.append(
            remote(
                turned_ref.at[row_block(target, channels), :],
                gcol_ref.at[:, lane_block(me + 1)],
                send_one.at[step],
                recv_one.at[step],
                target,
            )
        )
    gcol_ref[:, lane_block(me + 1)] = turned_ref[row_block(me, channels), :]
    gcol_ref[:, :LANES] = jnp.zeros((channels, LANES), jnp.bfloat16)
    gcol_ref[:, length + LANES :] = jnp.zeros((channels, LANES), jnp.bfloat16)
    for group in range(groups):
        for block in range(width // steps):
            tiles = [
                weight_ref[group * width + block * steps + u].astype(jnp.float32)
                for u in range(steps)
            ]
            for a, tile in enumerate(swap_blocks(tiles, TAP_STEP)):
                mix_ref[
                    group, a * width : (a + 1) * width, block * LANES : (block + 1) * LANES
                ] = tile.astype(jnp.bfloat16)
    span = taps_ref.shape[2]
    for group in range(groups):
        rows = slice(group * width, (group + 1) * width)
        source = column_ref[rows, :].astype(jnp.float32)
        for a in range(steps):
            moved = pltpu.roll(source, (span + LANES - a * TAP_STEP) % (span + LANES), 1)
            shifted_ref[group, a * width : (a + 1) * width, :] = moved[:, :span].astype(
                jnp.bfloat16
            )
    for copy in copies:
        copy.wait()
    for group in range(groups):
        rows = slice(group * width, (group + 1) * width)
        source = gcol_ref[rows, :].astype(jnp.float32)
        spread_taps(source, LANES // 2, -1, stage_ref, taps_ref.at[group])
        product = jnp.dot(mix_ref[group], taps_ref[group], preferred_element_type=jnp.float32)
        total = product[:width, LANES:]
        for a in range(1, steps):
            part = pltpu.roll(product[a * width : (a + 1) * width, :], a * TAP_STEP, 1)
            total = total + part[:, LANES:]
        result_ref[rows, :] = total
    copies = []
    for step in range(1, count):
        target = peer(me, step, count)
        copies.append(
            remote(
                result_ref.at[:, lane_block(target)],
                home_ref.at[row_block(me, channels), :],
                send_two.at[step],
                recv_two.at[step],
                target,
            )
        )
    home_ref[row_block(me, channels), :] = result_ref[:, lane_block(me)]
    for group in range(groups):
        grad = lax.dot_general(
            shifted_ref[group],
            taps_ref[group],
            (((1,), (1,)), ((), ())),
            preferred_element_type=jnp.float32,
        )
        for block in range(width // steps):
            tiles = [
                grad[a * width : (a + 1) * width, block * LANES : (block + 1) * LANES]
                for a in range(steps)
            ]
            for u, tile in enumerate(swap_blocks(tiles, TAP_STEP)):
                dweight_ref[group * width + block * steps + u] = tile.astype(dweight_ref.dtype)
    for copy in copies:
        copy.wait()
    back_ref[...] = home_ref[...].T


def conv_backward(grad, column, weight, count):
    tokens, features = grad.shape
    channels, width, kernel = weight.shape
    groups = channels // width
    length = count * LANES
    span = length + LANES
    rows = width * TAP_STEP
    steps = kernel // TAP_STEP
    sems = [pltpu.SemaphoreType.DMA((count,)) for _ in range(4)]
    return pl.pallas_call(
        functools.partial(conv_backward_kernel, count),
        out_shape=(
            jax.ShapeDtypeStruct((tokens, features), jnp.float32),
            jax.ShapeDtypeStruct(weight.shape, jnp.bfloat16),
        ),
        in_specs=[VMEM] * 3,
        out_specs=(VMEM,) * 2,
        scratch_shapes=[
            pltpu.VMEM((features, tokens), jnp.bfloat16),
            pltpu.VMEM((channels, span + LANES), jnp.bfloat16),
            pltpu.VMEM((channels, length), jnp.float32),
            pltpu.VMEM((features, tokens), jnp.float32),
            pltpu.VMEM((span // LANES, rows, LANES), jnp.float32),
            pltpu.VMEM((groups, rows, span), jnp.bfloat16),
            pltpu.VMEM((groups, steps * width, rows), jnp.bfloat16),
            pltpu.VMEM((groups, steps * width, span), jnp.bfloat16),
        ]
        + sems,
        compiler_params=pltpu.CompilerParams(
            collective_id=1, has_side_effects=True, vmem_limit_bytes=48 * 2**20
        ),
        name="conv_backward",
    )(grad, column, weight)


def query_span(index, size):
    return pl.ds(pl.multiple_of(index * size, size), size)


def same_clip(column_ref, seg_row):
    column = column_ref[...]
    parts = [
        column == seg_row[:, start : start + LANES]
        for start in range(0, seg_row.shape[1], LANES)
    ]
    return jnp.concatenate(parts, axis=1)


def clip_column(count, segs_ref, column_ref):
    for block in range(count):
        row = segs_ref[block].astype(jnp.float32)
        column_ref[block * LANES : (block + 1) * LANES, :] = jnp.broadcast_to(
            row, (LANES, LANES)
        ).T


def clip_row(segs_ref, first, size):
    parts = [segs_ref[first + i].astype(jnp.float32) for i in range(size // LANES)]
    return jnp.concatenate(parts, axis=1)


def attend_forward_kernel(
    count,
    head_dim,
    project_ref,
    segs_ref,
    out_ref,
    main_ref,
    extra_ref,
    att_main_ref,
    att_extra_ref,
    lse_main_ref,
    lse_extra_ref,
    turned_ref,
    low_main_ref,
    low_extra_ref,
    home_ref,
    column_ref,
    send_one,
    recv_one,
    send_two,
    recv_two,
    send_three,
    recv_three,
    send_four,
    recv_four,
):
    me = lax.axis_index("blk")
    features = project_ref.shape[1] // 3
    length = count * LANES
    half = count // 2
    scale = head_dim ** (-0.5)
    for part in range(3):
        block = project_ref[:, part * features : (part + 1) * features].astype(jnp.float32)
        block = block * scale if part == 0 else block
        turned_ref[part] = block.T.astype(jnp.bfloat16)
    greet(me, count)
    copies = []
    for step in range(1, count):
        target = peer(me, step, count)
        copies.append(
            remote(
                turned_ref.at[:, row_block(target, head_dim), :],
                main_ref.at[:, :, lane_block(me)],
                send_one.at[step],
                recv_one.at[step],
                target,
            )
        )
        copies.append(
            remote(
                turned_ref.at[:, row_block(count + target // 2, head_dim), :],
                extra_ref.at[:, :, lane_block(me)],
                send_two.at[step],
                recv_two.at[step],
                target,
            )
        )
    main_ref[:, :, lane_block(me)] = turned_ref[:, row_block(me, head_dim), :]
    extra_ref[:, :, lane_block(me)] = turned_ref[:, row_block(count + me // 2, head_dim), :]
    clip_column(count, segs_ref, column_ref)
    for copy in copies:
        copy.wait()

    def attend(held_ref, start, seg_row, att_ref, low_ref, lse_ref, place, low_place):
        size = seg_row.shape[1]
        queries = held_ref[0, :, start]
        scores = lax.dot_general(
            held_ref[1], queries, (((0,), (0,)), ((), ())), preferred_element_type=jnp.float32
        )
        scores = jnp.where(same_clip(column_ref, seg_row), scores, -1e30)
        top = jnp.max(scores, axis=0, keepdims=True)
        weights = jnp.exp(scores - top)
        total = jnp.sum(weights, axis=0, keepdims=True)
        mixed = jnp.dot(
            held_ref[2], weights.astype(jnp.bfloat16), preferred_element_type=jnp.float32
        )
        mixed = mixed / total
        att_ref[:, place] = mixed
        low_ref[:, low_place] = mixed.astype(jnp.bfloat16)
        lse_ref[:, place] = top + jnp.log(total)

    size = 2 * LANES
    for block in range(length // size):
        span = slice(block * size, (block + 1) * size)
        row = clip_row(segs_ref, block * 2, size)
        attend(main_ref, span, row, att_main_ref, low_main_ref, lse_main_ref, span, span)
    side = lax.rem(me, 2)
    for block in range(half * LANES // size):
        index = side * (half * LANES // size) + block
        span = query_span(index, size)
        row = clip_row(segs_ref, index * 2, size)
        place = slice(block * size, (block + 1) * size)
        attend(extra_ref, span, row, att_extra_ref, low_extra_ref, lse_extra_ref, place, span)

    own_rows = row_block(me, head_dim)
    extra_rows = row_block(count + me // 2, head_dim)
    copies, sides = [], []
    for step in range(1, count):
        target = peer(me, step, count)
        source = peer(me, count - step, count)
        copies.append(
            remote(
                low_main_ref.at[:, lane_block(target)],
                home_ref.at[own_rows, :],
                send_three.at[step],
                recv_three.at[step],
                target,
            )
        )
        copy = pltpu.make_async_remote_copy(
            src_ref=low_extra_ref.at[:, lane_block(target)],
            dst_ref=home_ref.at[extra_rows, :],
            send_sem=send_four.at[step],
            recv_sem=recv_four.at[step],
            device_id={"blk": target},
            device_id_type=MESH,
        )
        sends = target // half == side
        comes = me // half == lax.rem(source, 2)
        pl.when(sends)(copy.start)
        sides.append((sends, comes, copy))
    home_ref[own_rows, :] = low_main_ref[:, lane_block(me)]

    @pl.when(me // half == side)
    def _():
        home_ref[extra_rows, :] = low_extra_ref[:, lane_block(me)]

    for copy in copies:
        copy.wait()
    for sends, comes, copy in sides:
        pl.when(sends)(copy.wait_send)
        pl.when(comes)(copy.wait_recv)
    out_ref[...] = home_ref[...].astype(jnp.float32).T.astype(jnp.bfloat16)


def attend_forward(project, segs, count, head_dim):
    tokens, wide = project.shape
    features = wide // 3
    length = count * LANES
    part = length // 2
    sems = [pltpu.SemaphoreType.DMA((count,)) for _ in range(8)]
    return pl.pallas_call(
        functools.partial(attend_forward_kernel, count, head_dim),
        out_shape=(
            jax.ShapeDtypeStruct((tokens, features), jnp.bfloat16),
            jax.ShapeDtypeStruct((3, head_dim, length), jnp.bfloat16),
            jax.ShapeDtypeStruct((3, head_dim, length), jnp.bfloat16),
            jax.ShapeDtypeStruct((head_dim, length), jnp.float32),
            jax.ShapeDtypeStruct((head_dim, part), jnp.float32),
            jax.ShapeDtypeStruct((1, length), jnp.float32),
            jax.ShapeDtypeStruct((1, part), jnp.float32),
        ),
        in_specs=[VMEM] * 2,
        out_specs=(VMEM,) * 7,
        scratch_shapes=[
            pltpu.VMEM((3, features, tokens), jnp.bfloat16),
            pltpu.VMEM((head_dim, length), jnp.bfloat16),
            pltpu.VMEM((head_dim, length), jnp.bfloat16),
            pltpu.VMEM((features, tokens), jnp.bfloat16),
            pltpu.VMEM((length, LANES), jnp.float32),
        ]
        + sems,
        compiler_params=pltpu.CompilerParams(
            collective_id=2, has_side_effects=True, vmem_limit_bytes=48 * 2**20
        ),
        name="attend_forward",
    )(project, segs)


def attend_backward_kernel(
    count,
    head_dim,
    grad_ref,
    segs_ref,
    main_ref,
    extra_ref,
    att_main_ref,
    att_extra_ref,
    lse_main_ref,
    lse_extra_ref,
    out_ref,
    turned_ref,
    gmain_ref,
    gextra_ref,
    dmain_ref,
    dextra_ref,
    home_ref,
    part_ref,
    column_ref,
    send_one,
    recv_one,
    send_two,
    recv_two,
    send_three,
    recv_three,
    send_four,
    recv_four,
    send_five,
    recv_five,
):
    me = lax.axis_index("blk")
    features = grad_ref.shape[1]
    length = count * LANES
    half = count // 2
    extras = half * head_dim
    scale = head_dim ** (-0.5)
    turned_ref[...] = grad_ref[...].astype(jnp.float32).T.astype(jnp.bfloat16)
    greet(me, count)
    copies = []
    for step in range(1, count):
        target = peer(me, step, count)
        copies.append(
            remote(
                turned_ref.at[row_block(target, head_dim), :],
                gmain_ref.at[:, lane_block(me)],
                send_one.at[step],
                recv_one.at[step],
                target,
            )
        )
        copies.append(
            remote(
                turned_ref.at[row_block(count + target // 2, head_dim), :],
                gextra_ref.at[:, lane_block(me)],
                send_two.at[step],
                recv_two.at[step],
                target,
            )
        )
    gmain_ref[:, lane_block(me)] = turned_ref[row_block(me, head_dim), :]
    gextra_ref[:, lane_block(me)] = turned_ref[row_block(count + me // 2, head_dim), :]
    clip_column(count, segs_ref, column_ref)
    for copy in copies:
        copy.wait()

    def attend(held_ref, grad_from, start, seg_row, att, lse):
        queries = held_ref[0, :, start]
        grads = grad_from[:, start]
        scores = lax.dot_general(
            held_ref[1], queries, (((0,), (0,)), ((), ())), preferred_element_type=jnp.float32
        )
        scores = jnp.where(same_clip(column_ref, seg_row), scores, -1e30)
        weights = jnp.exp(scores - lse)
        grad_prob = lax.dot_general(
            held_ref[2], grads, (((0,), (0,)), ((), ())), preferred_element_type=jnp.float32
        )
        delta = jnp.sum(grads.astype(jnp.float32) * att, axis=0, keepdims=True)
        grad_score = (weights * (grad_prob - delta)).astype(jnp.bfloat16)
        dquery = jnp.dot(held_ref[1], grad_score, preferred_element_type=jnp.float32) * scale
        dkey = lax.dot_general(
            queries, grad_score, (((1,), (1,)), ((), ())), preferred_element_type=jnp.float32
        )
        dvalue = lax.dot_general(
            grads,
            weights.astype(jnp.bfloat16),
            (((1,), (1,)), ((), ())),
            preferred_element_type=jnp.float32,
        )
        return dquery, dkey, dvalue

    size = 2 * LANES
    side = lax.rem(me, 2)
    dkey = dvalue = None
    for block in range(half * LANES // size):
        index = side * (half * LANES // size) + block
        span = query_span(index, size)
        place = slice(block * size, (block + 1) * size)
        row = clip_row(segs_ref, index * 2, size)
        dquery, key_part, value_part = attend(
            extra_ref, gextra_ref, span, row, att_extra_ref[:, place], lse_extra_ref[:, place]
        )
        dextra_ref[0, :, span] = dquery.astype(jnp.bfloat16)
        dkey = key_part if dkey is None else dkey + key_part
        dvalue = value_part if dvalue is None else dvalue + value_part
    dextra_ref[1] = dkey.astype(jnp.bfloat16)
    dextra_ref[2] = dvalue.astype(jnp.bfloat16)

    own_rows = row_block(me, head_dim)
    extra_rows = row_block(count + me // 2, head_dim)
    part_rows = row_block(me // 2, head_dim)
    copies, sides = [], []
    for step in range(1, count):
        target = peer(me, step, count)
        source = peer(me, count - step, count)
        copies.append(
            remote(
                dextra_ref.at[1:3, :, lane_block(target)],
                part_ref.at[side, :, part_rows, :],
                send_three.at[step],
                recv_three.at[step],
                target,
            )
        )
        copy = pltpu.make_async_remote_copy(
            src_ref=dextra_ref.at[0, :, lane_block(target)],
            dst_ref=home_ref.at[0, extra_rows, :],
            send_sem=send_four.at[step],
            recv_sem=recv_four.at[step],
            device_id={"blk": target},
            device_id_type=MESH,
        )
        sends = target // half == side
        comes = me // half == lax.rem(source, 2)
        pl.when(sends)(copy.start)
        sides.append((sends, comes, copy))
    part_ref[side, :, part_rows, :] = dextra_ref[1:3, :, lane_block(me)]

    @pl.when(me // half == side)
    def _():
        home_ref[0, extra_rows, :] = dextra_ref[0, :, lane_block(me)]

    dkey = dvalue = None
    for block in range(length // size):
        span = slice(block * size, (block + 1) * size)
        row = clip_row(segs_ref, block * 2, size)
        dquery, key_part, value_part = attend(
            main_ref, gmain_ref, span, row, att_main_ref[:, span], lse_main_ref[:, span]
        )
        dmain_ref[0, :, span] = dquery.astype(jnp.bfloat16)
        dkey = key_part if dkey is None else dkey + key_part
        dvalue = value_part if dvalue is None else dvalue + value_part
    dmain_ref[1] = dkey.astype(jnp.bfloat16)
    dmain_ref[2] = dvalue.astype(jnp.bfloat16)
    for step in range(1, count):
        target = peer(me, step, count)
        copies.append(
            remote(
                dmain_ref.at[:, :, lane_block(target)],
                home_ref.at[:, own_rows, :],
                send_five.at[step],
                recv_five.at[step],
                target,
            )
        )
    home_ref[:, own_rows, :] = dmain_ref[:, :, lane_block(me)]
    for copy in copies:
        copy.wait()
    for sends, comes, copy in sides:
        pl.when(sends)(copy.wait_send)
        pl.when(comes)(copy.wait_recv)
    first = features - extras
    for which in range(2):
        total = part_ref[0, which].astype(jnp.float32) + part_ref[1, which].astype(jnp.float32)
        home_ref[1 + which, first:, :] = total.astype(jnp.bfloat16)
    for part in range(3):
        out_ref[:, part * features : (part + 1) * features] = (
            home_ref[part].astype(jnp.float32).T.astype(jnp.bfloat16)
        )


def attend_backward(grad, segs, kept, count, head_dim):
    tokens, features = grad.shape
    length = count * LANES
    extras = count // 2 * head_dim
    sems = [pltpu.SemaphoreType.DMA((count,)) for _ in range(10)]
    return pl.pallas_call(
        functools.partial(attend_backward_kernel, count, head_dim),
        out_shape=jax.ShapeDtypeStruct((tokens, 3 * features), jnp.bfloat16),
        in_specs=[VMEM] * 8,
        out_specs=VMEM,
        scratch_shapes=[
            pltpu.VMEM((features, tokens), jnp.bfloat16),
            pltpu.VMEM((head_dim, length), jnp.bfloat16),
            pltpu.VMEM((head_dim, length), jnp.bfloat16),
            pltpu.VMEM((3, head_dim, length), jnp.bfloat16),
            pltpu.VMEM((3, head_dim, length), jnp.bfloat16),
            pltpu.VMEM((3, features, tokens), jnp.bfloat16),
            pltpu.VMEM((2, 2, extras, tokens), jnp.bfloat16),
            pltpu.VMEM((length, LANES), jnp.float32),
        ]
        + sems,
        compiler_params=pltpu.CompilerParams(
            collective_id=3, has_side_effects=True, vmem_limit_bytes=48 * 2**20
        ),
        name="attend_backward",
    )(grad, segs, *kept)


def shards(sizes, *arrays):
    frames, segment, conv_weight = arrays[:3]
    row_count, block_len, model_width = frames.shape
    group_width, kernel = conv_weight.shape[1:]
    count = sizes["blk"]
    head_dim = model_width // HEADS
    channels = model_width // count
    fits = (
        row_count == 1
        and block_len == LANES
        and kernel == LANES
        and channels % group_width == 0
        and group_width % TAP_STEP == 0
        and count % 4 == 0
        and 2 * HEADS == 3 * count
        and head_dim % TAP_STEP == 0
    )
    if fits:
        return swap_shards(count, *arrays)
    return ring_shards(*arrays)


def swap_shards(
    count,
    frames,
    segment,
    conv_weight,
    conv_bias,
    qkv_weight,
    qv_bias,
    out_weight,
    out_bias,
    norm1_gain,
    norm1_bias,
    ffn_in,
    ffn_in_bias,
    ffn_out,
    ffn_out_bias,
    norm2_gain,
    norm2_bias,
    cotangent,
):
    _, tokens, width = frames.shape
    group_width = conv_weight.shape[1]
    channels = width // count
    head_dim = width // HEADS
    me = lax.axis_index("blk")
    frames = frames[0]
    own_weight = lax.dynamic_slice_in_dim(conv_weight, me * channels, channels, 0)
    turned_weight = own_weight.reshape(-1, group_width, *conv_weight.shape[1:])
    turned_weight = turned_weight.transpose(0, 2, 1, 3)
    conv_out, column, segs = conv_forward(frames, segment, turned_weight, count)
    pre_conv = conv_out + conv_bias.astype(jnp.float32)
    mixed_in = frames.astype(jnp.float32) + gelu_value(pre_conv)
    mixed_low = mixed_in.astype(jnp.bfloat16)
    pair_bias = qv_bias.astype(jnp.float32)
    zero_bias = jnp.zeros((width,), jnp.float32)
    full_bias = jnp.concatenate([pair_bias[:width], zero_bias, pair_bias[width:]])
    project = (
        jnp.dot(mixed_low, qkv_weight, preferred_element_type=jnp.float32) + full_bias
    ).astype(jnp.bfloat16)
    attn_low, *kept = attend_forward(project, segs, count, head_dim)
    branch = jnp.dot(attn_low, out_weight, preferred_element_type=jnp.float32) + out_bias.astype(
        jnp.float32
    )
    gain_one = norm1_gain.astype(jnp.float32)
    hidden_norm, normed_one, inv_one = norm_forward(
        mixed_in + branch, gain_one, norm1_bias.astype(jnp.float32)
    )
    hidden_low = hidden_norm.astype(jnp.bfloat16)
    ffn_pre = jnp.dot(hidden_low, ffn_in, preferred_element_type=jnp.float32) + ffn_in_bias.astype(
        jnp.float32
    )
    ffn_act = gelu_value(ffn_pre).astype(jnp.bfloat16)
    ffn_branch = jnp.dot(
        ffn_act, ffn_out, preferred_element_type=jnp.float32
    ) + ffn_out_bias.astype(jnp.float32)
    gain_two = norm2_gain.astype(jnp.float32)
    layer_out, normed_two, inv_two = norm_forward(
        hidden_norm + ffn_branch, gain_two, norm2_bias.astype(jnp.float32)
    )
    grad_top = cotangent[0].astype(jnp.float32)
    grad_second, norm2_gain_grad, norm2_bias_grad = norm_backward(
        grad_top, normed_two, inv_two, gain_two
    )
    grad_branch_two = grad_second.astype(jnp.bfloat16)
    ffn_out_grad = jnp.einsum(
        "nf,nd->fd", ffn_act, grad_branch_two, preferred_element_type=jnp.float32
    )
    ffn_out_bias_grad = jnp.sum(grad_branch_two.astype(jnp.float32), axis=0)
    grad_act = jnp.einsum("nd,fd->nf", grad_branch_two, ffn_out, preferred_element_type=jnp.float32)
    grad_pre = (grad_act * gelu_slope(ffn_pre)).astype(jnp.bfloat16)
    ffn_in_grad = jnp.einsum("nd,nf->df", hidden_low, grad_pre, preferred_element_type=jnp.float32)
    ffn_in_bias_grad = jnp.sum(grad_pre.astype(jnp.float32), axis=0)
    grad_hidden = grad_second + jnp.einsum(
        "nf,df->nd", grad_pre, ffn_in, preferred_element_type=jnp.float32
    )
    grad_first, norm1_gain_grad, norm1_bias_grad = norm_backward(
        grad_hidden, normed_one, inv_one, gain_one
    )
    grad_branch = grad_first.astype(jnp.bfloat16)
    out_weight_grad = jnp.einsum(
        "ne,nd->ed", attn_low, grad_branch, preferred_element_type=jnp.float32
    )
    out_bias_grad = jnp.sum(grad_branch.astype(jnp.float32), axis=0)
    grad_att = jnp.einsum(
        "nd,ed->ne", grad_branch, out_weight, preferred_element_type=jnp.float32
    ).astype(jnp.bfloat16)
    grad_project = attend_backward(grad_att, segs, kept, count, head_dim)
    qkv_weight_grad = jnp.einsum(
        "nd,ne->de", mixed_low, grad_project, preferred_element_type=jnp.float32
    )
    bias_sums = jnp.sum(grad_project.astype(jnp.float32), axis=0)
    qv_bias_grad = jnp.concatenate([bias_sums[:width], bias_sums[2 * width :]])
    grad_mixed = grad_first + jnp.einsum(
        "ne,de->nd", grad_project, qkv_weight, preferred_element_type=jnp.float32
    )
    grad_conv = (grad_mixed * gelu_slope(pre_conv)).astype(jnp.bfloat16)
    conv_bias_grad = jnp.sum(grad_conv.astype(jnp.float32), axis=0)
    back_conv, conv_weight_grad = conv_backward(grad_conv, column, own_weight, count)
    is_valid = segment.reshape(tokens, 1) >= 0
    frames_grad = (grad_mixed + jnp.where(is_valid, back_conv, 0.0)).astype(jnp.bfloat16)

    def summed(grad):
        part = lax.psum_scatter(
            grad.astype(jnp.bfloat16), "blk", scatter_dimension=0, tiled=True
        )
        return lax.psum(part, "dp").astype(jnp.float32)

    vectors = [
        conv_bias_grad,
        qv_bias_grad,
        out_bias_grad,
        norm1_gain_grad,
        norm1_bias_grad,
        ffn_in_bias_grad,
        ffn_out_bias_grad,
        norm2_gain_grad,
        norm2_bias_grad,
    ]
    stacked = jnp.concatenate([vector.reshape(count, -1) for vector in vectors], axis=1)
    stacked = lax.dynamic_index_in_dim(lax.psum(stacked, ("dp", "blk")), me, 0, keepdims=False)
    sums, start = [], 0
    for vector in vectors:
        size = vector.shape[0] // count
        sums.append(stacked[start : start + size])
        start += size
    return (
        layer_out.astype(jnp.bfloat16)[None],
        frames_grad[None],
        lax.psum(conv_weight_grad, "dp").astype(jnp.float32),
        sums[0],
        summed(qkv_weight_grad),
        sums[1],
        summed(out_weight_grad),
        sums[2],
        sums[3],
        sums[4],
        summed(ffn_in_grad),
        sums[5],
        summed(ffn_out_grad),
        sums[6],
        sums[7],
        sums[8],
    )


def solution(mesh):
    return jax.shard_map(
        functools.partial(shards, mesh.shape),
        mesh=mesh,
        in_specs=(
            P("dp", "blk", None),
            P("dp", "blk"),
            P(),
            P(),
            P(),
            P(),
            P(),
            P(),
            P(),
            P(),
            P(),
            P(),
            P(),
            P(),
            P(),
            P(),
            P("dp", "blk", None),
        ),
        out_specs=(
            P("dp", "blk", None),
            P("dp", "blk", None),
            P("blk", None, None),
            P("blk"),
            P("blk", None),
            P("blk"),
            P("blk", None),
            P("blk"),
            P("blk"),
            P("blk"),
            P("blk", None),
            P("blk"),
            P("blk", None),
            P("blk"),
            P("blk"),
            P("blk"),
        ),
        check_vma=False,
    )
```

```python
import functools
import math
import types

import jax
import jax.numpy as jnp
from jax import lax
from jax.experimental import pallas as pl
from jax.experimental.pallas import tpu as pltpu
from jax.sharding import PartitionSpec as P

HEADS = 12
GROUPS = 16


EPS = 1e-05
ROOT_HALF = 0.7071067811865476
DENSITY_CONST = 0.3989422804014327


def with_halo(x, sides, width):
    for axis, dim in sides:
        size, length = (lax.axis_size(axis), x.shape[dim])
        up = [(i, (i + 1) % size) for i in range(size - 1)]
        down = [(j, i) for i, j in up]
        last = lax.slice_in_dim(x, length - width, length, axis=dim)
        initial = lax.slice_in_dim(x, 0, width, axis=dim)
        before = lax.ppermute(last, axis, up)
        after = lax.ppermute(initial, axis, down)
        x = jnp.concatenate([before, x, after], axis=dim)
    return x


def from_behind(value, axis, steps):
    count = lax.axis_size(axis)
    pairs = [(source, (source + steps) % count) for source in range(count)]
    return lax.ppermute(value, axis, pairs)


def gelu_value(signal):
    return 0.5 * signal * (1.0 + lax.erf(signal * ROOT_HALF))


def gelu_slope(signal):
    return (
        0.5 * (1.0 + lax.erf(signal * ROOT_HALF))
        + signal * jnp.exp(-0.5 * signal * signal) * DENSITY_CONST
    )


def norm_forward(signal, gain_vec, shift_vec):
    average = jnp.mean(signal, axis=-1, keepdims=True)
    centred = signal - average
    inv_std = lax.rsqrt(jnp.mean(centred * centred, axis=-1, keepdims=True) + EPS)
    normed = centred * inv_std
    return (normed * gain_vec + shift_vec, normed, inv_std)


def norm_backward(grad_in, normed, inv_std, gain_vec):
    scaled = grad_in * gain_vec
    result = inv_std * (
        scaled
        - jnp.mean(scaled, axis=-1, keepdims=True)
        - normed * jnp.mean(scaled * normed, axis=-1, keepdims=True)
    )
    return (result, jnp.sum(grad_in * normed, axis=0), jnp.sum(grad_in, axis=0))


def block_grads(
    query_h, dout_h, query_seg, log_tot, row_delta, key_h, value_h, key_seg, score_scale
):
    scores = (
        jnp.einsum("rqhc,rkhc->rhqk", query_h, key_h, preferred_element_type=jnp.float32)
        * score_scale
    )
    same_seg = (query_seg[:, :, None] == key_seg[:, None, :])[:, None]
    weights_f = jnp.where(same_seg, jnp.exp(scores - log_tot[..., None]), 0.0)
    grad_prob = jnp.einsum("rqhc,rkhc->rhqk", dout_h, value_h, preferred_element_type=jnp.float32)
    grad_score = (weights_f * (grad_prob - row_delta[..., None])).astype(jnp.bfloat16)
    query_part = score_scale * jnp.einsum(
        "rhqk,rkhc->rqhc", grad_score, key_h, preferred_element_type=jnp.float32
    )
    key_part = score_scale * jnp.einsum(
        "rhqk,rqhc->rkhc", grad_score, query_h, preferred_element_type=jnp.float32
    )
    value_part = jnp.einsum(
        "rhqk,rqhc->rkhc",
        weights_f.astype(jnp.bfloat16),
        dout_h,
        preferred_element_type=jnp.float32,
    )
    return (query_part, key_part, value_part)


def ring_shards(
    frames,
    segment,
    conv_weight,
    conv_bias,
    qkv_weight,
    qv_bias,
    out_weight,
    out_bias,
    norm1_gain,
    norm1_bias,
    ffn_in,
    ffn_in_bias,
    ffn_out,
    ffn_out_bias,
    norm2_gain,
    norm2_bias,
    cotangent,
):
    row_count, block_len, model_width = frames.shape
    token_count = row_count * block_len
    group_width = conv_weight.shape[1]
    kernel = conv_weight.shape[2]
    half_kernel = kernel // 2
    head_dim = model_width // HEADS
    score_scale = head_dim ** (-0.5)
    cycle_len = lax.axis_size("blk")
    is_valid = segment >= 0
    masked = jnp.where(is_valid[..., None], frames, jnp.zeros_like(frames))
    padded = with_halo(masked, (("blk", 1),), half_kernel)
    conv_out = lax.conv_general_dilated(
        padded,
        conv_weight,
        (1,),
        "VALID",
        dimension_numbers=("NWC", "OIW", "NWC"),
        feature_group_count=GROUPS,
        preferred_element_type=jnp.float32,
    )
    pre_conv = conv_out[:, :block_len].reshape(token_count, model_width) + conv_bias.astype(
        jnp.float32
    )
    mixed_in = frames.reshape(token_count, model_width).astype(jnp.float32) + gelu_value(pre_conv)
    mixed_low = mixed_in.astype(jnp.bfloat16)
    pair_bias = qv_bias.astype(jnp.float32)
    zero_bias = jnp.zeros((model_width,), jnp.float32)
    full_bias = jnp.concatenate([pair_bias[:model_width], zero_bias, pair_bias[model_width:]])
    project = (
        jnp.dot(mixed_low, qkv_weight, preferred_element_type=jnp.float32) + full_bias
    ).astype(jnp.bfloat16)
    project = project.reshape(row_count, block_len, 3 * model_width)
    query_heads = project[..., :model_width].reshape(row_count, block_len, HEADS, head_dim)
    keys_local = project[..., model_width : 2 * model_width]
    values_local = project[..., 2 * model_width :]
    key_heads = keys_local.reshape(row_count, block_len, HEADS, head_dim)
    value_heads = values_local.reshape(row_count, block_len, HEADS, head_dim)
    query_seg = segment.astype(jnp.bfloat16)
    start_carry = (
        jnp.full((row_count, HEADS, block_len), -1e30, jnp.float32),
        jnp.zeros((row_count, HEADS, block_len), jnp.float32),
        jnp.zeros((row_count, HEADS, block_len, head_dim), jnp.float32),
    )
    key_piece = lax.all_gather(keys_local, "blk", axis=1, tiled=True)
    value_piece = lax.all_gather(values_local, "blk", axis=1, tiled=True)
    seg_piece = lax.all_gather(query_seg, "blk", axis=1, tiled=True)
    piece_len = key_piece.shape[1]
    block_size = math.gcd(piece_len, 512)

    def one_block(block_index, inner_carry):
        running_max, denominator, numerator = inner_carry
        offset = block_index * block_size
        key_block = lax.dynamic_slice_in_dim(key_piece, offset, block_size, 1).reshape(
            row_count, block_size, HEADS, head_dim
        )
        value_block = lax.dynamic_slice_in_dim(value_piece, offset, block_size, 1).reshape(
            row_count, block_size, HEADS, head_dim
        )
        seg_block = lax.dynamic_slice_in_dim(seg_piece, offset, block_size, 1)
        scores = (
            jnp.einsum(
                "rqhc,rkhc->rhqk", query_heads, key_block, preferred_element_type=jnp.float32
            )
            * score_scale
        )
        same_seg = (query_seg[:, :, None] == seg_block[:, None, :])[:, None]
        masked_scores = jnp.where(same_seg, scores, -1e30)
        new_max = jnp.maximum(running_max, jnp.max(masked_scores, axis=-1))
        weights_f = jnp.where(same_seg, jnp.exp(masked_scores - new_max[..., None]), 0.0)
        rescale = jnp.exp(running_max - new_max)
        denominator = denominator * rescale + jnp.sum(weights_f, axis=-1)
        numerator = numerator * rescale[..., None] + jnp.einsum(
            "rhqk,rkhc->rhqc",
            weights_f.astype(jnp.bfloat16),
            value_block,
            preferred_element_type=jnp.float32,
        )
        return (new_max, denominator, numerator)

    running_max, denominator, numerator = lax.fori_loop(
        0, piece_len // block_size, one_block, start_carry
    )
    log_total = running_max + jnp.log(denominator)
    attended_heads = (numerator / denominator[..., None]).transpose(0, 2, 1, 3)
    attended = attended_heads.reshape(token_count, model_width)
    attn_low = attended.astype(jnp.bfloat16)
    branch = jnp.dot(attn_low, out_weight, preferred_element_type=jnp.float32) + out_bias.astype(
        jnp.float32
    )
    gain_one = norm1_gain.astype(jnp.float32)
    hidden_norm, normed_one, inv_one = norm_forward(
        mixed_in + branch, gain_one, norm1_bias.astype(jnp.float32)
    )
    hidden_low = hidden_norm.astype(jnp.bfloat16)
    ffn_pre = jnp.dot(hidden_low, ffn_in, preferred_element_type=jnp.float32) + ffn_in_bias.astype(
        jnp.float32
    )
    ffn_act = gelu_value(ffn_pre).astype(jnp.bfloat16)
    ffn_branch = jnp.dot(
        ffn_act, ffn_out, preferred_element_type=jnp.float32
    ) + ffn_out_bias.astype(jnp.float32)
    gain_two = norm2_gain.astype(jnp.float32)
    layer_out, normed_two, inv_two = norm_forward(
        hidden_norm + ffn_branch, gain_two, norm2_bias.astype(jnp.float32)
    )
    grad_top = cotangent.reshape(token_count, model_width).astype(jnp.float32)
    grad_second, norm2_gain_grad, norm2_bias_grad = norm_backward(
        grad_top, normed_two, inv_two, gain_two
    )
    grad_branch_two = grad_second.astype(jnp.bfloat16)
    ffn_out_grad = jnp.einsum(
        "nf,nd->fd", ffn_act, grad_branch_two, preferred_element_type=jnp.float32
    )
    ffn_out_bias_grad = jnp.sum(grad_branch_two.astype(jnp.float32), axis=0)
    grad_act = jnp.einsum("nd,fd->nf", grad_branch_two, ffn_out, preferred_element_type=jnp.float32)
    grad_pre = (grad_act * gelu_slope(ffn_pre)).astype(jnp.bfloat16)
    ffn_in_grad = jnp.einsum("nd,nf->df", hidden_low, grad_pre, preferred_element_type=jnp.float32)
    ffn_in_bias_grad = jnp.sum(grad_pre.astype(jnp.float32), axis=0)
    grad_hidden = grad_second + jnp.einsum(
        "nf,df->nd", grad_pre, ffn_in, preferred_element_type=jnp.float32
    )
    grad_first, norm1_gain_grad, norm1_bias_grad = norm_backward(
        grad_hidden, normed_one, inv_one, gain_one
    )
    grad_branch = grad_first.astype(jnp.bfloat16)
    out_weight_grad = jnp.einsum(
        "ne,nd->ed", attn_low, grad_branch, preferred_element_type=jnp.float32
    )
    out_bias_grad = jnp.sum(grad_branch.astype(jnp.float32), axis=0)
    grad_att = jnp.einsum("nd,ed->ne", grad_branch, out_weight, preferred_element_type=jnp.float32)
    grad_heads = grad_att.astype(jnp.bfloat16).reshape(row_count, block_len, HEADS, head_dim)
    row_delta = jnp.einsum("rqhc,rqhc->rhq", grad_heads.astype(jnp.float32), attended_heads)
    zero_heads = jnp.zeros((row_count, block_len, HEADS, head_dim), jnp.float32)

    def key_step(carried):
        key_block, value_block, seg_block, key_grad, value_grad, query_grad = carried
        query_part, key_part, value_part = block_grads(
            query_heads,
            grad_heads,
            query_seg,
            log_total,
            row_delta,
            key_block,
            value_block,
            seg_block,
            score_scale,
        )
        query_grad = query_grad + query_part
        key_grad = key_grad + key_part
        value_grad = value_grad + value_part
        key_block, value_block, seg_block = from_behind(
            (key_block, value_block, seg_block), "blk", 1
        )
        key_grad, value_grad = (
            from_behind(key_grad.astype(jnp.bfloat16), "blk", 1).astype(key_grad.dtype),
            from_behind(value_grad.astype(jnp.bfloat16), "blk", 1).astype(value_grad.dtype),
        )
        return (key_block, value_block, seg_block, key_grad, value_grad, query_grad)

    def four_steps(turn_index, carried):
        for repeat in range(4):
            carried = key_step(carried)
        return carried

    final_state = lax.fori_loop(
        0,
        cycle_len // 4,
        four_steps,
        (key_heads, value_heads, query_seg, zero_heads, zero_heads, zero_heads),
    )
    key_grad, value_grad, query_grad = (final_state[3], final_state[4], final_state[5])
    grad_project = jnp.concatenate(
        [
            query_grad.reshape(token_count, model_width),
            key_grad.reshape(token_count, model_width),
            value_grad.reshape(token_count, model_width),
        ],
        axis=1,
    ).astype(jnp.bfloat16)
    qkv_weight_grad = jnp.einsum(
        "nd,ne->de", mixed_low, grad_project, preferred_element_type=jnp.float32
    )
    bias_sums = jnp.sum(grad_project.astype(jnp.float32), axis=0)
    qv_bias_grad = jnp.concatenate([bias_sums[:model_width], bias_sums[2 * model_width :]])
    grad_mixed = grad_first + jnp.einsum(
        "ne,de->nd", grad_project, qkv_weight, preferred_element_type=jnp.float32
    )
    grad_conv = (grad_mixed * gelu_slope(pre_conv)).astype(jnp.bfloat16)
    conv_bias_grad = jnp.sum(grad_conv.astype(jnp.float32), axis=0)
    grad_conv_rows = grad_conv.reshape(row_count, block_len, model_width)
    grad_padded = with_halo(grad_conv_rows, (("blk", 1),), half_kernel)
    flipped = conv_weight.reshape(GROUPS, group_width, group_width, kernel).transpose(0, 2, 1, 3)
    flipped = flipped.reshape(model_width, group_width, kernel)[:, :, ::-1]
    back_conv = lax.conv_general_dilated(
        grad_padded,
        flipped,
        (1,),
        "VALID",
        dimension_numbers=("NWC", "OIW", "NWC"),
        feature_group_count=GROUPS,
        preferred_element_type=jnp.float32,
    )[:, 1:]
    frames_grad = (
        grad_mixed.reshape(row_count, block_len, model_width)
        + jnp.where(is_valid[..., None], back_conv, 0.0)
    ).astype(jnp.bfloat16)
    conv_weight_grad = lax.conv_general_dilated(
        padded,
        grad_conv_rows,
        (1,),
        "VALID",
        dimension_numbers=("CWN", "IWO", "CNW"),
        batch_group_count=GROUPS,
        preferred_element_type=jnp.float32,
    )[:, :, :kernel]
    (
        conv_weight_part,
        conv_bias_part,
        qkv_weight_part,
        qv_bias_part,
        out_weight_part,
        out_bias_part,
        gain_one_part,
        shift_one_part,
        ffn_in_part,
        ffn_in_bias_part,
        ffn_out_part,
        ffn_out_bias_part,
        gain_two_part,
        shift_two_part,
    ) = (
        lax.psum_scatter(conv_weight_grad, "blk", scatter_dimension=0, tiled=True),
        lax.psum_scatter(conv_bias_grad, "blk", scatter_dimension=0, tiled=True),
        lax.psum_scatter(qkv_weight_grad, "blk", scatter_dimension=0, tiled=True),
        lax.psum_scatter(qv_bias_grad, "blk", scatter_dimension=0, tiled=True),
        lax.psum_scatter(out_weight_grad, "blk", scatter_dimension=0, tiled=True),
        lax.psum_scatter(out_bias_grad, "blk", scatter_dimension=0, tiled=True),
        lax.psum_scatter(norm1_gain_grad, "blk", scatter_dimension=0, tiled=True),
        lax.psum_scatter(norm1_bias_grad, "blk", scatter_dimension=0, tiled=True),
        lax.psum_scatter(ffn_in_grad, "blk", scatter_dimension=0, tiled=True),
        lax.psum_scatter(ffn_in_bias_grad, "blk", scatter_dimension=0, tiled=True),
        lax.psum_scatter(ffn_out_grad, "blk", scatter_dimension=0, tiled=True),
        lax.psum_scatter(ffn_out_bias_grad, "blk", scatter_dimension=0, tiled=True),
        lax.psum_scatter(norm2_gain_grad, "blk", scatter_dimension=0, tiled=True),
        lax.psum_scatter(norm2_bias_grad, "blk", scatter_dimension=0, tiled=True),
    )
    totals = (
        lax.psum(conv_weight_part.astype(jnp.bfloat16), "dp").astype(jnp.float32),
        lax.psum(conv_bias_part.astype(jnp.bfloat16), "dp").astype(jnp.float32),
        lax.psum(qkv_weight_part.astype(jnp.bfloat16), "dp").astype(jnp.float32),
        lax.psum(qv_bias_part.astype(jnp.bfloat16), "dp").astype(jnp.float32),
        lax.psum(out_weight_part.astype(jnp.bfloat16), "dp").astype(jnp.float32),
        lax.psum(out_bias_part.astype(jnp.bfloat16), "dp").astype(jnp.float32),
        lax.psum(gain_one_part.astype(jnp.bfloat16), "dp").astype(jnp.float32),
        lax.psum(shift_one_part.astype(jnp.bfloat16), "dp").astype(jnp.float32),
        lax.psum(ffn_in_part.astype(jnp.bfloat16), "dp").astype(jnp.float32),
        lax.psum(ffn_in_bias_part.astype(jnp.bfloat16), "dp").astype(jnp.float32),
        lax.psum(ffn_out_part.astype(jnp.bfloat16), "dp").astype(jnp.float32),
        lax.psum(ffn_out_bias_part.astype(jnp.bfloat16), "dp").astype(jnp.float32),
        lax.psum(gain_two_part.astype(jnp.bfloat16), "dp").astype(jnp.float32),
        lax.psum(shift_two_part.astype(jnp.bfloat16), "dp").astype(jnp.float32),
    )
    return (
        layer_out.reshape(row_count, block_len, model_width).astype(jnp.bfloat16),
        frames_grad,
        totals[0],
        totals[1],
        totals[2],
        totals[3],
        totals[4],
        totals[5],
        totals[6],
        totals[7],
        totals[8],
        totals[9],
        totals[10],
        totals[11],
        totals[12],
        totals[13],
    )


MESH = pl.DeviceIdType.MESH
LANES = 128
TAP_STEP = 16
VMEM = pl.BlockSpec(memory_space=pltpu.VMEM)


def peer(me, step, count):
    return lax.rem(me + step, count)


def greet(me, count, rows=1):
    barrier = pltpu.get_barrier_semaphore()
    for step in range(1, count):
        pl.semaphore_signal(
            barrier, inc=1, device_id={"blk": peer(me, step, count)}, device_id_type=MESH
        )
    for step in range(1, rows):
        row = peer(lax.axis_index("dp"), step, rows)
        pl.semaphore_signal(barrier, inc=1, device_id={"dp": row}, device_id_type=MESH)
    pl.semaphore_wait(barrier, count + rows - 2)


def remote(src, dst, send_sem, recv_sem, target, axis="blk"):
    copy = pltpu.make_async_remote_copy(
        src_ref=src,
        dst_ref=dst,
        send_sem=send_sem,
        recv_sem=recv_sem,
        device_id={axis: target},
        device_id_type=MESH,
    )
    copy.start()
    return copy


def turned(value):
    return value.astype(jnp.float32).T.astype(jnp.bfloat16)


def matmul_turned(left, right):
    return lax.dot_general(
        left, right, (((1,), (1,)), ((), ())), preferred_element_type=jnp.float32
    )


def sum_parts(parts_ref):
    total = parts_ref[0].astype(jnp.float32)
    for part in range(1, parts_ref.shape[0]):
        total = total + parts_ref[part].astype(jnp.float32)
    return total


def lane_block(index):
    return pl.ds(pl.multiple_of(index * LANES, LANES), LANES)


def row_block(index, size):
    return pl.ds(pl.multiple_of(index * size, size), size)


def swap_blocks(tiles, width):
    count = len(tiles)
    lane = lax.broadcasted_iota(jnp.int32, tiles[0].shape, 1) // width
    tiles = list(tiles)
    step = count // 2
    while step:
        low = (lane & step) == 0
        for u in range(count):
            if u & step == 0:
                one, two = tiles[u], tiles[u + step]
                tiles[u] = jnp.where(low, one, pltpu.roll(two, step * width, 1))
                tiles[u + step] = jnp.where(low, pltpu.roll(one, LANES - step * width, 1), two)
        step //= 2
    return tiles


def spread_taps(source, offset, direction, stage_ref, out_ref):
    rows, length = source.shape
    blocks = out_ref.shape[1] // LANES
    for tap in range(TAP_STEP):
        shift = (length - offset - direction * tap) % length
        moved = pltpu.roll(source, shift, 1)
        for block in range(blocks):
            stage_ref[block, pl.ds(tap, rows, stride=TAP_STEP), :] = moved[
                :, block * LANES : (block + 1) * LANES
            ]
    for block in range(blocks):
        out_ref[:, block * LANES : (block + 1) * LANES] = stage_ref[block].astype(jnp.bfloat16)


def query_span(index, size):
    return pl.ds(pl.multiple_of(index * size, size), size)


def same_clip(column_ref, seg_row):
    column = column_ref[...]
    parts = [
        column == seg_row[:, start : start + LANES]
        for start in range(0, seg_row.shape[1], LANES)
    ]
    return jnp.concatenate(parts, axis=1)


def clip_column(count, segs_ref, column_ref):
    for block in range(count):
        row = segs_ref[block].astype(jnp.float32)
        column_ref[block * LANES : (block + 1) * LANES, :] = jnp.broadcast_to(
            row, (LANES, LANES)
        ).T


def clip_row(segs_ref, first, size):
    parts = [segs_ref[first + i].astype(jnp.float32) for i in range(size // LANES)]
    return jnp.concatenate(parts, axis=1)


def layer_kernel(names, count, rows_count, head_dim, *refs):
    R = types.SimpleNamespace(**dict(zip(names, refs)))
    low, f32 = jnp.bfloat16, jnp.float32
    me, row = lax.axis_index("blk"), lax.axis_index("dp")
    level, side = me // 2, lax.rem(me, 2)
    levels = count // 2
    half = count // 2
    near = me + 1 - 2 * side
    core = lax.rem(row, 2)
    twin = row + 1 - 2 * core
    across = peer(row, 2, rows_count)
    tokens, width = R.frames.shape
    channels = width // count
    length = count * LANES
    groups, group_width = R.turned_weight.shape[:2]
    steps = LANES // TAP_STEP
    scale = head_dim ** (-0.5)
    chunks = R.in_hbm.shape[1] // width

    def send(kind, step, source, target_ref, target, axis="blk"):
        return remote(
            source, target_ref, R.out_sem.at[kind, step], R.in_sem.at[kind, step], target, axis
        )

    def wait(copies):
        for copy in copies:
            copy.wait()

    def to_blocks(kind, source, target_ref):
        copies = []
        for step in range(1, count):
            target = peer(me, step, count)
            copies.append(send(kind, step, source(target), target_ref, target))
        return copies

    def chunk_of(index):
        return slice(index * width, (index + 1) * width)

    def table(index):
        return R.table[index : index + 1, :]

    def dot(left, right):
        return jnp.dot(left, right, preferred_element_type=f32)

    loads = [pltpu.make_async_copy(R.qkv_hbm, R.qkv_w, R.load_sem.at[0])]
    loads.append(pltpu.make_async_copy(R.out_hbm, R.out_w, R.load_sem.at[1]))
    for chunk in range(chunks):
        span = chunk_of(chunk)
        loads.append(
            pltpu.make_async_copy(
                R.in_hbm.at[:, span], R.in_w.at[:, span], R.load_sem.at[2 + 2 * chunk]
            )
        )
        loads.append(
            pltpu.make_async_copy(
                R.back_hbm.at[span], R.back_w.at[span], R.load_sem.at[3 + 2 * chunk]
            )
        )
    for load in loads:
        load.start()
    valid = (R.segment[...] >= 0).astype(f32)
    R.turned[...] = (R.frames[...].astype(f32).T * valid).astype(low)
    greet(me, count, rows_count)

    copies = to_blocks(
        0, lambda p: R.turned.at[row_block(p, channels), :], R.column.at[:, lane_block(me + 1)]
    )
    copies += to_blocks(1, lambda p: R.segment, R.segs.at[me])
    R.column[:, lane_block(me + 1)] = R.turned[row_block(me, channels), :]
    for ref in (R.column, R.gcol):
        ref[:, :LANES] = jnp.zeros((channels, LANES), low)
        ref[:, length + LANES :] = jnp.zeros((channels, LANES), low)
    R.segs[me] = R.segment[...]
    R.table[...] = jnp.zeros_like(R.table)
    R.small[...] = jnp.zeros_like(R.small)
    place = 0
    for vector in VECTORS:
        ref = getattr(R, vector)
        for part in range(ref.shape[0] // width):
            R.table[place, :] = ref[chunk_of(part)].astype(f32)
            place += 1
    for group in range(groups):
        for block in range(group_width // steps):
            span = slice(block * LANES, (block + 1) * LANES)
            for mix, tile_at in (
                (R.mix, lambda u: R.turned_weight[group, block * steps + u]),
                (R.mix_back, lambda u: R.own_weight[group * group_width + block * steps + u]),
            ):
                tiles = [tile_at(u).astype(f32) for u in range(steps)]
                for a, tile in enumerate(swap_blocks(tiles, TAP_STEP)):
                    rows = slice(a * group_width, (a + 1) * group_width)
                    mix[group, rows, span] = tile.astype(low)
    wait(copies)

    for group in range(groups):
        rows = slice(group * group_width, (group + 1) * group_width)
        spread_taps(R.column[rows, :].astype(f32), LANES // 2, 1, R.stage, R.taps.at[group])
        product = dot(R.mix[group], R.taps[group])
        total = product[:group_width, :length]
        for a in range(1, steps):
            part = product[a * group_width : (a + 1) * group_width, :]
            part = pltpu.roll(part, product.shape[1] - a * TAP_STEP, 1)
            total = total + part[:, :length]
        R.result[rows, :] = total.astype(low)
    copies = to_blocks(
        2, lambda p: R.result.at[:, lane_block(p)], R.conv_home.at[row_block(me, channels), :]
    )
    R.conv_home[row_block(me, channels), :] = R.result[:, lane_block(me)]
    for group in range(groups):
        rows = slice(group * group_width, (group + 1) * group_width)
        source = R.column[rows, :].astype(f32)
        span = R.shifted.shape[2]
        for a in range(steps):
            moved = pltpu.roll(source, (span + LANES - a * TAP_STEP) % (span + LANES), 1)
            R.shifted[group, a * group_width : (a + 1) * group_width, :] = moved[:, :span].astype(
                low
            )
    clip_column(count, R.segs, R.clip)
    wait(copies)

    pre = R.conv_home[...].astype(f32).T + table(0)
    share = 0.5 * (1.0 + lax.erf(pre * ROOT_HALF))
    R.slope[...] = share + pre * jnp.exp(-0.5 * pre * pre) * DENSITY_CONST
    mixed = R.frames[...].astype(f32) + pre * share
    R.mixed[...] = mixed
    mixed_low = mixed.astype(low)
    loads[0].wait()
    for part in range(3):
        block = dot(mixed_low, R.qkv_w[:, chunk_of(part)])
        if part != 1:
            block = block + table(1 + part // 2)
        block = block.astype(low).astype(f32)
        if part == 0:
            block = block * scale
        R.project[part] = block.T.astype(low)
    copies = to_blocks(
        3,
        lambda p: R.project.at[:, row_block(p, head_dim), :],
        R.main.at[:, :, lane_block(me)],
    )
    copies += to_blocks(
        4,
        lambda p: R.project.at[:, row_block(count + p // 2, head_dim), :],
        R.extra.at[:, :, lane_block(me)],
    )
    R.main[:, :, lane_block(me)] = R.project[:, row_block(me, head_dim), :]
    R.extra[:, :, lane_block(me)] = R.project[:, row_block(count + me // 2, head_dim), :]
    R.left[0] = turned(mixed_low)
    wait(copies)

    size = 2 * LANES
    halves = half * LANES // size

    def scores_of(held, start, seg_row):
        scores = lax.dot_general(
            held[1], held[0, :, start], (((0,), (0,)), ((), ())), preferred_element_type=f32
        )
        return jnp.where(same_clip(R.clip, seg_row), scores, -1e30)

    def attend(held, start, index, att_ref, low_ref, lse_ref, place):
        scores = scores_of(held, start, clip_row(R.segs, index * 2, size))
        top = jnp.max(scores, axis=0, keepdims=True)
        weights = jnp.exp(scores - top)
        total = jnp.sum(weights, axis=0, keepdims=True)
        mean = dot(held[2], weights.astype(low)) / total
        att_ref[:, place] = mean
        low_ref[:, start] = mean.astype(low)
        lse_ref[:, place] = top + jnp.log(total)

    own_rows = row_block(me, head_dim)
    extra_rows = row_block(count + me // 2, head_dim)

    def to_half(kind, source, target_ref):
        pending = []
        for step in range(1, count):
            target, origin = peer(me, step, count), peer(me, count - step, count)
            copy = pltpu.make_async_remote_copy(
                src_ref=source(target),
                dst_ref=target_ref,
                send_sem=R.out_sem.at[kind, step],
                recv_sem=R.in_sem.at[kind, step],
                device_id={"blk": target},
                device_id_type=MESH,
            )
            sends, comes = target // half == side, me // half == lax.rem(origin, 2)
            pl.when(sends)(copy.start)
            pending.append((sends, comes, copy))
        return pending

    def wait_half(pending):
        for sends, comes, copy in pending:
            pl.when(sends)(copy.wait_send)
            pl.when(comes)(copy.wait_recv)

    for block in range(halves):
        index = side * halves + block
        place = slice(block * size, (block + 1) * size)
        attend(
            R.extra,
            query_span(index, size),
            index,
            R.att_extra,
            R.low_extra,
            R.lse_extra,
            place,
        )
    pending = to_half(5, lambda p: R.low_extra.at[:, lane_block(p)], R.att_home.at[extra_rows, :])

    @pl.when(me // half == side)
    def _():
        R.att_home[extra_rows, :] = R.low_extra[:, lane_block(me)]

    for block in range(length // size):
        span = slice(block * size, (block + 1) * size)
        attend(R.main, span, block, R.att_main, R.low_main, R.lse_main, span)
    copies = to_blocks(6, lambda p: R.low_main.at[:, lane_block(p)], R.att_home.at[own_rows, :])
    R.att_home[own_rows, :] = R.low_main[:, lane_block(me)]
    wait(copies)
    wait_half(pending)

    background = []

    def to_rows(kind, source, target_ref):
        for step in range(1, rows_count):
            target = peer(row, step, rows_count)
            background.append(send(kind, step, source(target), target_ref, target, "dp"))

    def spread_rows(kind, ref):
        own = ref.at[:, lane_block(row)]
        background.append(send(kind, 1, own, own, twin, "dp"))
        return send(kind, 2, own, own, across, "dp")

    def forward_rows(kind, ref, copy):
        copy.wait()
        got = ref.at[:, lane_block(across)]
        background.append(send(kind, 3, got, got, twin, "dp"))

    R.left[1] = R.att_home[...]
    att = R.att_home[...].astype(f32).T.astype(low)
    loads[1].wait()
    branch = dot(att, R.out_w[...]) + table(3)
    hidden, normed_one, inv_one = norm_forward(R.mixed[...] + branch, table(4), table(5))
    hidden_low = hidden.astype(low)
    R.hidden_all[:, lane_block(row)] = turned(hidden_low)
    hidden_across = spread_rows(7, R.hidden_all)
    to_rows(
        8, lambda p: R.left.at[p // (rows_count - 1)], R.late_left.at[:, lane_block(row)]
    )
    R.late_left[:, lane_block(row)] = R.left[row // (rows_count - 1)]
    total = hidden + table(10)
    pieces = count // chunks
    for chunk in range(chunks):
        span = chunk_of(chunk)
        loads[2 + 2 * chunk].wait()
        pre = dot(hidden_low, R.in_w[:, span]) + table(6 + chunk)
        share = 0.5 * (1.0 + lax.erf(pre * ROOT_HALF))
        act = (pre * share).astype(low)
        R.keep[:, span] = share + pre * jnp.exp(-0.5 * pre * pre) * DENSITY_CONST
        R.act_turned[chunk * pieces : (chunk + 1) * pieces] = turned(act).reshape(
            pieces, rows_count, -1, LANES
        )
        loads[3 + 2 * chunk].wait()
        total = total + dot(act, R.back_w[span, :])
    to_rows(9, lambda p: R.act_turned.at[:, p], R.act_all.at[:, :, lane_block(row)])
    R.act_all[:, :, lane_block(row)] = R.act_turned[:, row]
    layer, normed_two, inv_two = norm_forward(total, table(11), table(12))
    R.layer_out[...] = layer.astype(low)
    grad_second, gain_sum, shift_sum = norm_backward(
        R.cotangent[...].astype(f32), normed_two, inv_two, table(11)
    )
    R.small[11, :] = gain_sum
    R.small[12, :] = shift_sum
    grad_two = grad_second.astype(low)
    R.two_all[:, lane_block(row)] = turned(grad_two)
    two_across = spread_rows(10, R.two_all)
    R.small[10, :] = jnp.sum(grad_two.astype(f32), axis=0)
    grad_hidden = grad_second
    for chunk in range(chunks):
        span = chunk_of(chunk)
        grad_pre = matmul_turned(grad_two, R.back_w[span, :]) * R.keep[:, span]
        grad_pre = grad_pre.astype(low)
        R.pre_turned[chunk] = turned(grad_pre)
        R.small[6 + chunk, :] = jnp.sum(grad_pre.astype(f32), axis=0)
        grad_hidden = grad_hidden + matmul_turned(grad_pre, R.in_w[:, span])
    grad_first, gain_sum, shift_sum = norm_backward(grad_hidden, normed_one, inv_one, table(4))
    R.small[4, :] = gain_sum
    R.small[5, :] = shift_sum
    R.mixed[...] = grad_first
    grad_branch = grad_first.astype(low)
    R.small[3, :] = jnp.sum(grad_branch.astype(f32), axis=0)
    R.turned[...] = turned(matmul_turned(grad_branch, R.out_w[...]).astype(low))

    copies = to_blocks(
        11, lambda p: R.turned.at[row_block(p, head_dim), :], R.gmain.at[:, lane_block(me)]
    )
    copies += to_blocks(
        12,
        lambda p: R.turned.at[row_block(count + p // 2, head_dim), :],
        R.gextra.at[:, lane_block(me)],
    )
    R.gmain[:, lane_block(me)] = R.turned[row_block(me, head_dim), :]
    R.gextra[:, lane_block(me)] = R.turned[row_block(count + me // 2, head_dim), :]
    to_rows(13, lambda p: R.pre_turned.at[p], R.pre_all.at[:, lane_block(row)])
    R.pre_all[:, lane_block(row)] = R.pre_turned[row]
    R.dproject[3] = turned(grad_branch)
    wait(copies)

    def attend_back(held, grads, start, index, att, lse):
        queries = held[0, :, start]
        weights = jnp.exp(scores_of(held, start, clip_row(R.segs, index * 2, size)) - lse)
        grad_prob = lax.dot_general(
            held[2], grads, (((0,), (0,)), ((), ())), preferred_element_type=f32
        )
        delta = jnp.sum(grads.astype(f32) * att, axis=0, keepdims=True)
        grad_score = (weights * (grad_prob - delta)).astype(low)
        return (
            dot(held[1], grad_score) * scale,
            matmul_turned(queries, grad_score),
            matmul_turned(grads, weights.astype(low)),
        )

    sums = None
    for block in range(halves):
        index = side * halves + block
        span = query_span(index, size)
        place = slice(block * size, (block + 1) * size)
        parts = attend_back(
            R.extra, R.gextra[:, span], span, index, R.att_extra[:, place], R.lse_extra[:, place]
        )
        R.dextra[0, :, span] = parts[0].astype(low)
        sums = parts[1:] if sums is None else [a + b for a, b in zip(sums, parts[1:])]
    R.dextra[1] = sums[0].astype(low)
    R.dextra[2] = sums[1].astype(low)
    part_rows = row_block(me // 2, head_dim)
    copies = to_blocks(
        14, lambda p: R.dextra.at[1:3, :, lane_block(p)], R.halves.at[side, :, part_rows, :]
    )
    pending = to_half(
        15, lambda p: R.dextra.at[0, :, lane_block(p)], R.dproject.at[0, extra_rows, :]
    )
    R.halves[side, :, part_rows, :] = R.dextra[1:3, :, lane_block(me)]

    @pl.when(me // half == side)
    def _():
        R.dproject[0, extra_rows, :] = R.dextra[0, :, lane_block(me)]

    forward_rows(7, R.hidden_all, hidden_across)
    forward_rows(10, R.two_all, two_across)
    sums = None
    for block in range(length // size):
        span = slice(block * size, (block + 1) * size)
        parts = attend_back(
            R.main, R.gmain[:, span], span, block, R.att_main[:, span], R.lse_main[:, span]
        )
        R.dmain[0, :, span] = parts[0].astype(low)
        sums = parts[1:] if sums is None else [a + b for a, b in zip(sums, parts[1:])]
    R.dmain[1] = sums[0].astype(low)
    R.dmain[2] = sums[1].astype(low)
    copies += to_blocks(
        16, lambda p: R.dmain.at[:, :, lane_block(p)], R.dproject.at[0:3, own_rows, :]
    )
    R.dproject[0:3, own_rows, :] = R.dmain[:, :, lane_block(me)]

    wait(background)
    background = []

    def part_span(which):
        return slice(which * width, (which + 1) * width)

    def sum_near_start(kind, which, left, right):
        R.in_w[:, part_span(which)] = matmul_turned(left, right).astype(low)
        return [
            send(
                kind,
                lev,
                R.in_w.at[row_block(2 * lev + 1 - side, channels), part_span(which)],
                R.near_got.at[which, lev],
                near,
            )
            for lev in range(levels)
        ]

    def sum_far_start(kind, which, copies):
        wait(copies)
        for lev in range(levels):
            own = R.in_w[row_block(2 * lev + side, channels), part_span(which)]
            R.near_sum[which, lev] = (
                own.astype(f32) + R.near_got[which, lev].astype(f32)
            ).astype(low)
        R.far_got[which, level] = R.near_sum[which, level]
        far = []
        for step in range(1, levels):
            target = peer(level, step, levels)
            far.append(
                send(
                    kind,
                    step,
                    R.near_sum.at[which, target],
                    R.far_got.at[which, level],
                    2 * target + side,
                )
            )
        return far

    def share_start(kind, ref):
        own = ref.at[row]
        background.append(send(kind, 1, own, own, twin, "dp"))
        return send(kind, 2, own, own, across, "dp")

    def share_forward(kind, ref, copy):
        copy.wait()
        got = ref.at[across]
        background.append(send(kind, 3, got, got, twin, "dp"))

    near_in = sum_near_start(17, 0, R.hidden_all[...], R.pre_all[...])
    near_out = sum_near_start(18, 1, R.act_all[...].reshape(width, -1), R.two_all[...])
    wait(copies)
    wait_half(pending)
    first = half * head_dim
    for which in range(2):
        total = R.halves[0, which].astype(f32) + R.halves[1, which].astype(f32)
        R.dproject[1 + which, width - first :, :] = total.astype(low)

    late = []
    for step in range(1, rows_count):
        target = peer(row, step, rows_count)
        late.append(
            send(
                19, step, R.dproject.at[target], R.late_right.at[:, lane_block(row)], target, "dp"
            )
        )
    R.late_right[:, lane_block(row)] = R.dproject[row]
    grad_mixed = R.mixed[...]
    for part in range(3):
        block = R.dproject[part].astype(f32).T
        if part != 1:
            R.small[1 + part // 2, :] = jnp.sum(block, axis=0)
        grad_mixed = grad_mixed + matmul_turned(block.astype(low), R.qkv_w[:, chunk_of(part)])
    R.mixed[...] = grad_mixed
    grad_conv = (grad_mixed * R.slope[...]).astype(low)
    R.small[0, :] = jnp.sum(grad_conv.astype(f32), axis=0)
    R.conv_turned[...] = turned(grad_conv)
    copies = to_blocks(
        20, lambda p: R.conv_turned.at[row_block(p, channels), :], R.gcol.at[:, lane_block(me + 1)]
    )
    R.gcol[:, lane_block(me + 1)] = R.conv_turned[row_block(me, channels), :]
    small_copy = send(21, 0, R.small, R.small_got.at[0], twin, "dp")
    far_in = sum_far_start(22, 0, near_in)
    far_out = sum_far_start(23, 1, near_out)
    wait(copies)
    for group in range(groups):
        rows = slice(group * group_width, (group + 1) * group_width)
        spread_taps(R.gcol[rows, :].astype(f32), LANES // 2, -1, R.stage, R.taps.at[group])
        product = dot(R.mix_back[group], R.taps[group])
        total = product[:group_width, LANES:]
        for a in range(1, steps):
            part = product[a * group_width : (a + 1) * group_width, :]
            total = total + pltpu.roll(part, a * TAP_STEP, 1)[:, LANES:]
        R.result[rows, :] = total.astype(low)
    back = to_blocks(
        24, lambda p: R.result.at[:, lane_block(p)], R.back_home.at[row_block(me, channels), :]
    )
    R.back_home[row_block(me, channels), :] = R.result[:, lane_block(me)]
    quarter = channels // rows_count
    for group in range(groups):
        grad = matmul_turned(R.shifted[group], R.taps[group])
        for block in range(group_width // steps):
            span = slice(block * LANES, (block + 1) * LANES)
            tiles = [
                grad[a * group_width : (a + 1) * group_width, span] for a in range(steps)
            ]
            for u, tile in enumerate(swap_blocks(tiles, TAP_STEP)):
                channel = group * group_width + block * steps + u
                part = channel // quarter
                R.conv_part[part // 2, part % 2, channel % quarter] = tile.astype(low)
    conv_copy = send(25, 0, R.conv_part.at[:, 1 - core], R.conv_got, twin, "dp")
    small_copy.wait()
    R.small_sum[0] = R.small[...] + R.small_got[0]
    small_copy = send(21, 1, R.small_sum.at[0], R.small_got.at[1], across, "dp")

    wait(late)
    wait(background)
    background = []
    near_att = sum_near_start(26, 2, R.late_left[...], R.late_right[...])
    conv_copy.wait()
    for part in range(2):
        R.conv_sum[part] = (
            R.conv_part[part, core].astype(f32) + R.conv_got[part].astype(f32)
        ).astype(low)
    conv_copy = send(25, 1, R.conv_sum.at[1 - row // 2], R.conv_far, across, "dp")
    small_copy.wait()
    R.small_sum[1] = R.small_sum[0] + R.small_got[1]
    small_copy = send(21, 2, R.small_sum.at[1], R.small_got.at[2], near)
    wait(far_in)
    wait(far_out)
    for which in range(2):
        R.ffn_all[row, which] = sum_parts(R.far_got.at[which]).astype(low)
    ffn_copy = share_start(27, R.ffn_all)
    far_att = sum_far_start(28, 2, near_att)
    wait(back)
    R.frames_out[...] = (
        R.mixed[...] + (R.back_home[...].astype(f32) * valid).T
    ).astype(low)
    conv_copy.wait()
    R.conv_all[row] = (
        R.conv_sum[row // 2].astype(f32) + R.conv_far[...].astype(f32)
    ).astype(low)
    conv_copy = share_start(29, R.conv_all)
    small_copy.wait()
    R.small_far[level] = R.small_sum[1] + R.small_got[2]
    smalls = []
    for step in range(1, levels):
        target = 2 * peer(level, step, levels) + side
        smalls.append(
            send(30, step, R.small_far.at[level], R.small_far.at[level], target)
        )
    wait(far_att)
    R.attn_all[row] = sum_parts(R.far_got.at[2]).astype(low)
    attn_copy = share_start(31, R.attn_all)
    share_forward(27, R.ffn_all, ffn_copy)
    share_forward(29, R.conv_all, conv_copy)
    wait(smalls)
    R.small_out[...] = sum_parts(R.small_far)
    share_forward(31, R.attn_all, attn_copy)
    wait(background)


VECTORS = (
    "conv_bias",
    "qv_bias",
    "out_bias",
    "gain_one",
    "shift_one",
    "in_bias",
    "back_bias",
    "gain_two",
    "shift_two",
)


def layer(count, rows_count, head_dim, named):
    low, f32 = jnp.bfloat16, jnp.float32
    tokens, width = named["frames"].shape
    wide = named["in_hbm"].shape[1]
    channels, group_width, kernel = named["own_weight"].shape
    groups = channels // group_width
    length = count * LANES
    span = length + LANES
    steps = kernel // TAP_STEP
    taps = group_width * TAP_STEP
    every = rows_count * tokens
    piece = channels // rows_count
    extras = count // 2 * head_dim
    levels = count // 2
    outs = {
        "layer_out": ((tokens, width), low),
        "frames_out": ((tokens, width), low),
        "conv_all": ((rows_count, piece, group_width, kernel), low),
        "ffn_all": ((rows_count, 2, channels, width), low),
        "attn_all": ((rows_count, channels, width), low),
        "small_out": ((16, width), f32),
    }
    scratch = {
        "qkv_w": (named["qkv_hbm"].shape, low),
        "out_w": (named["out_hbm"].shape, low),
        "in_w": (named["in_hbm"].shape, low),
        "back_w": (named["back_hbm"].shape, low),
        "table": ((16, width), f32),
        "small": ((16, width), f32),
        "small_got": ((3, 16, width), f32),
        "small_sum": ((2, 16, width), f32),
        "small_far": ((levels, 16, width), f32),
        "turned": ((width, tokens), low),
        "conv_turned": ((width, tokens), low),
        "column": ((channels, span + LANES), low),
        "gcol": ((channels, span + LANES), low),
        "segs": ((count, 1, LANES), jnp.int32),
        "clip": ((length, LANES), f32),
        "stage": ((span // LANES, taps, LANES), f32),
        "taps": ((groups, taps, span), low),
        "mix": ((groups, steps * group_width, taps), low),
        "mix_back": ((groups, steps * group_width, taps), low),
        "shifted": ((groups, steps * group_width, span), low),
        "result": ((channels, length), low),
        "conv_home": ((width, tokens), low),
        "back_home": ((width, tokens), low),
        "slope": ((tokens, width), f32),
        "mixed": ((tokens, width), f32),
        "project": ((3, width, tokens), low),
        "main": ((3, head_dim, length), low),
        "extra": ((3, head_dim, length), low),
        "att_main": ((head_dim, length), f32),
        "att_extra": ((head_dim, length // 2), f32),
        "low_main": ((head_dim, length), low),
        "low_extra": ((head_dim, length), low),
        "lse_main": ((1, length), f32),
        "lse_extra": ((1, length // 2), f32),
        "att_home": ((width, tokens), low),
        "keep": ((tokens, wide), f32),
        "left": ((2, width, tokens), low),
        "act_turned": ((count, rows_count, wide // (count * rows_count), tokens), low),
        "pre_turned": ((rows_count, width, tokens), low),
        "hidden_all": ((width, every), low),
        "two_all": ((width, every), low),
        "pre_all": ((width, every), low),
        "act_all": ((count, wide // (count * rows_count), every), low),
        "late_left": ((width, every), low),
        "late_right": ((width, every), low),
        "gmain": ((head_dim, length), low),
        "gextra": ((head_dim, length), low),
        "dmain": ((3, head_dim, length), low),
        "dextra": ((3, head_dim, length), low),
        "dproject": ((4, width, tokens), low),
        "halves": ((2, 2, extras, tokens), low),
        "near_got": ((3, levels, channels, width), low),
        "near_sum": ((3, levels, channels, width), low),
        "far_got": ((3, levels, channels, width), low),
        "conv_part": ((2, 2, piece, group_width, kernel), low),
        "conv_got": ((2, piece, group_width, kernel), low),
        "conv_sum": ((2, piece, group_width, kernel), low),
        "conv_far": ((piece, group_width, kernel), low),
    }
    hbm = pl.BlockSpec(memory_space=pl.ANY)
    names = (*named, *outs, *scratch, "out_sem", "in_sem", "load_sem")
    return pl.pallas_call(
        functools.partial(layer_kernel, names, count, rows_count, head_dim),
        out_shape=tuple(jax.ShapeDtypeStruct(*out) for out in outs.values()),
        in_specs=[hbm if name.endswith("_hbm") else VMEM for name in named],
        out_specs=(VMEM,) * len(outs),
        scratch_shapes=[pltpu.VMEM(*item) for item in scratch.values()]
        + [
            pltpu.SemaphoreType.DMA((32, count)),
            pltpu.SemaphoreType.DMA((32, count)),
            pltpu.SemaphoreType.DMA((2 + 2 * (wide // width),)),
        ],
        compiler_params=pltpu.CompilerParams(
            collective_id=0, has_side_effects=True, vmem_limit_bytes=62 * 2**20
        ),
        name="layer",
    )(*named.values())


def shards(sizes, *arrays):
    frames, segment, conv_weight = arrays[:3]
    row_count, block_len, model_width = frames.shape
    group_width, kernel = conv_weight.shape[1:]
    count = sizes["blk"]
    head_dim = model_width // HEADS
    channels = model_width // count
    fits = (
        row_count == 1
        and block_len == LANES
        and kernel == LANES
        and channels % group_width == 0
        and group_width % TAP_STEP == 0
        and count % 4 == 0
        and 2 * HEADS == 3 * count
        and head_dim % TAP_STEP == 0
        and sizes["dp"] == 4
        and count % sizes["dp"] == 0
        and arrays[10].shape[1] == 4 * model_width
    )
    if fits:
        return swap_shards(count, sizes["dp"], *arrays)
    return ring_shards(*arrays)


def swap_shards(
    count,
    rows_count,
    frames,
    segment,
    conv_weight,
    conv_bias,
    qkv_weight,
    qv_bias,
    out_weight,
    out_bias,
    norm1_gain,
    norm1_bias,
    ffn_in,
    ffn_in_bias,
    ffn_out,
    ffn_out_bias,
    norm2_gain,
    norm2_bias,
    cotangent,
):
    width = frames.shape[2]
    group_width = conv_weight.shape[1]
    channels = width // count
    me = lax.axis_index("blk")
    own_weight = lax.dynamic_slice_in_dim(conv_weight, me * channels, channels, 0)
    turned_weight = own_weight.reshape(-1, group_width, *conv_weight.shape[1:])
    named = {
        "frames": frames[0],
        "segment": segment,
        "cotangent": cotangent[0],
        "own_weight": own_weight,
        "turned_weight": turned_weight.transpose(0, 2, 1, 3),
        "conv_bias": conv_bias,
        "qv_bias": qv_bias,
        "out_bias": out_bias,
        "gain_one": norm1_gain,
        "shift_one": norm1_bias,
        "in_bias": ffn_in_bias,
        "back_bias": ffn_out_bias,
        "gain_two": norm2_gain,
        "shift_two": norm2_bias,
        "qkv_hbm": qkv_weight,
        "out_hbm": out_weight,
        "in_hbm": ffn_in,
        "back_hbm": ffn_out,
    }
    layer_out, frames_grad, conv_all, ffn_all, attn_all, small_all = layer(
        count, rows_count, width // HEADS, named
    )
    conv_grad = conv_all.reshape(own_weight.shape).astype(jnp.float32)
    ffn_in_grad = ffn_all[:, 0].transpose(1, 0, 2).reshape(channels, -1).astype(jnp.float32)
    ffn_out_grad = ffn_all[:, 1].reshape(-1, width).astype(jnp.float32)
    qkv_grad = attn_all[:-1].transpose(1, 0, 2).reshape(channels, -1).astype(jnp.float32)
    out_grad = attn_all[-1].astype(jnp.float32)
    small_all = small_all.reshape(-1)
    sums, start = [], 0
    for vector in VECTORS:
        size = named[vector].shape[0]
        sums.append(
            lax.dynamic_slice_in_dim(small_all, start + me * (size // count), size // count)
        )
        start += size
    return (
        layer_out[None],
        frames_grad[None],
        conv_grad,
        sums[0],
        qkv_grad,
        sums[1],
        out_grad,
        sums[2],
        sums[3],
        sums[4],
        ffn_in_grad,
        sums[5],
        ffn_out_grad,
        sums[6],
        sums[7],
        sums[8],
    )


def solution(mesh):
    return jax.shard_map(
        functools.partial(shards, mesh.shape),
        mesh=mesh,
        in_specs=(
            P("dp", "blk", None),
            P("dp", "blk"),
            P(),
            P(),
            P(),
            P(),
            P(),
            P(),
            P(),
            P(),
            P(),
            P(),
            P(),
            P(),
            P(),
            P(),
            P("dp", "blk", None),
        ),
        out_specs=(
            P("dp", "blk", None),
            P("dp", "blk", None),
            P("blk", None, None),
            P("blk"),
            P("blk", None),
            P("blk"),
            P("blk", None),
            P("blk"),
            P("blk"),
            P("blk"),
            P("blk", None),
            P("blk"),
            P("blk", None),
            P("blk"),
            P("blk"),
            P("blk"),
        ),
        check_vma=False,
    )
```

```python
import functools
import math
import types

import jax
import jax.numpy as jnp
from jax import lax
from jax.experimental import pallas as pl
from jax.experimental.pallas import tpu as pltpu
from jax.sharding import PartitionSpec as P

HEADS = 12
GROUPS = 16


EPS = 1e-05
ROOT_HALF = 0.7071067811865476
DENSITY_CONST = 0.3989422804014327


def with_halo(x, sides, width):
    for axis, dim in sides:
        size, length = (lax.axis_size(axis), x.shape[dim])
        up = [(i, (i + 1) % size) for i in range(size - 1)]
        down = [(j, i) for i, j in up]
        last = lax.slice_in_dim(x, length - width, length, axis=dim)
        initial = lax.slice_in_dim(x, 0, width, axis=dim)
        before = lax.ppermute(last, axis, up)
        after = lax.ppermute(initial, axis, down)
        x = jnp.concatenate([before, x, after], axis=dim)
    return x


def from_behind(value, axis, steps):
    count = lax.axis_size(axis)
    pairs = [(source, (source + steps) % count) for source in range(count)]
    return lax.ppermute(value, axis, pairs)


def gelu_value(signal):
    return 0.5 * signal * (1.0 + lax.erf(signal * ROOT_HALF))


def gelu_slope(signal):
    return (
        0.5 * (1.0 + lax.erf(signal * ROOT_HALF))
        + signal * jnp.exp(-0.5 * signal * signal) * DENSITY_CONST
    )


def norm_forward(signal, gain_vec, shift_vec):
    average = jnp.mean(signal, axis=-1, keepdims=True)
    centred = signal - average
    inv_std = lax.rsqrt(jnp.mean(centred * centred, axis=-1, keepdims=True) + EPS)
    normed = centred * inv_std
    return (normed * gain_vec + shift_vec, normed, inv_std)


def norm_backward(grad_in, normed, inv_std, gain_vec):
    scaled = grad_in * gain_vec
    result = inv_std * (
        scaled
        - jnp.mean(scaled, axis=-1, keepdims=True)
        - normed * jnp.mean(scaled * normed, axis=-1, keepdims=True)
    )
    return (result, jnp.sum(grad_in * normed, axis=0), jnp.sum(grad_in, axis=0))


def block_grads(
    query_h, dout_h, query_seg, log_tot, row_delta, key_h, value_h, key_seg, score_scale
):
    scores = (
        jnp.einsum("rqhc,rkhc->rhqk", query_h, key_h, preferred_element_type=jnp.float32)
        * score_scale
    )
    same_seg = (query_seg[:, :, None] == key_seg[:, None, :])[:, None]
    weights_f = jnp.where(same_seg, jnp.exp(scores - log_tot[..., None]), 0.0)
    grad_prob = jnp.einsum("rqhc,rkhc->rhqk", dout_h, value_h, preferred_element_type=jnp.float32)
    grad_score = (weights_f * (grad_prob - row_delta[..., None])).astype(jnp.bfloat16)
    query_part = score_scale * jnp.einsum(
        "rhqk,rkhc->rqhc", grad_score, key_h, preferred_element_type=jnp.float32
    )
    key_part = score_scale * jnp.einsum(
        "rhqk,rqhc->rkhc", grad_score, query_h, preferred_element_type=jnp.float32
    )
    value_part = jnp.einsum(
        "rhqk,rqhc->rkhc",
        weights_f.astype(jnp.bfloat16),
        dout_h,
        preferred_element_type=jnp.float32,
    )
    return (query_part, key_part, value_part)


def ring_shards(
    frames,
    segment,
    conv_weight,
    conv_bias,
    qkv_weight,
    qv_bias,
    out_weight,
    out_bias,
    norm1_gain,
    norm1_bias,
    ffn_in,
    ffn_in_bias,
    ffn_out,
    ffn_out_bias,
    norm2_gain,
    norm2_bias,
    cotangent,
):
    row_count, block_len, model_width = frames.shape
    token_count = row_count * block_len
    group_width = conv_weight.shape[1]
    kernel = conv_weight.shape[2]
    half_kernel = kernel // 2
    head_dim = model_width // HEADS
    score_scale = head_dim ** (-0.5)
    cycle_len = lax.axis_size("blk")
    is_valid = segment >= 0
    masked = jnp.where(is_valid[..., None], frames, jnp.zeros_like(frames))
    padded = with_halo(masked, (("blk", 1),), half_kernel)
    conv_out = lax.conv_general_dilated(
        padded,
        conv_weight,
        (1,),
        "VALID",
        dimension_numbers=("NWC", "OIW", "NWC"),
        feature_group_count=GROUPS,
        preferred_element_type=jnp.float32,
    )
    pre_conv = conv_out[:, :block_len].reshape(token_count, model_width) + conv_bias.astype(
        jnp.float32
    )
    mixed_in = frames.reshape(token_count, model_width).astype(jnp.float32) + gelu_value(pre_conv)
    mixed_low = mixed_in.astype(jnp.bfloat16)
    pair_bias = qv_bias.astype(jnp.float32)
    zero_bias = jnp.zeros((model_width,), jnp.float32)
    full_bias = jnp.concatenate([pair_bias[:model_width], zero_bias, pair_bias[model_width:]])
    project = (
        jnp.dot(mixed_low, qkv_weight, preferred_element_type=jnp.float32) + full_bias
    ).astype(jnp.bfloat16)
    project = project.reshape(row_count, block_len, 3 * model_width)
    query_heads = project[..., :model_width].reshape(row_count, block_len, HEADS, head_dim)
    keys_local = project[..., model_width : 2 * model_width]
    values_local = project[..., 2 * model_width :]
    key_heads = keys_local.reshape(row_count, block_len, HEADS, head_dim)
    value_heads = values_local.reshape(row_count, block_len, HEADS, head_dim)
    query_seg = segment.astype(jnp.bfloat16)
    start_carry = (
        jnp.full((row_count, HEADS, block_len), -1e30, jnp.float32),
        jnp.zeros((row_count, HEADS, block_len), jnp.float32),
        jnp.zeros((row_count, HEADS, block_len, head_dim), jnp.float32),
    )
    key_piece = lax.all_gather(keys_local, "blk", axis=1, tiled=True)
    value_piece = lax.all_gather(values_local, "blk", axis=1, tiled=True)
    seg_piece = lax.all_gather(query_seg, "blk", axis=1, tiled=True)
    piece_len = key_piece.shape[1]
    block_size = math.gcd(piece_len, 512)

    def one_block(block_index, inner_carry):
        running_max, denominator, numerator = inner_carry
        offset = block_index * block_size
        key_block = lax.dynamic_slice_in_dim(key_piece, offset, block_size, 1).reshape(
            row_count, block_size, HEADS, head_dim
        )
        value_block = lax.dynamic_slice_in_dim(value_piece, offset, block_size, 1).reshape(
            row_count, block_size, HEADS, head_dim
        )
        seg_block = lax.dynamic_slice_in_dim(seg_piece, offset, block_size, 1)
        scores = (
            jnp.einsum(
                "rqhc,rkhc->rhqk", query_heads, key_block, preferred_element_type=jnp.float32
            )
            * score_scale
        )
        same_seg = (query_seg[:, :, None] == seg_block[:, None, :])[:, None]
        masked_scores = jnp.where(same_seg, scores, -1e30)
        new_max = jnp.maximum(running_max, jnp.max(masked_scores, axis=-1))
        weights_f = jnp.where(same_seg, jnp.exp(masked_scores - new_max[..., None]), 0.0)
        rescale = jnp.exp(running_max - new_max)
        denominator = denominator * rescale + jnp.sum(weights_f, axis=-1)
        numerator = numerator * rescale[..., None] + jnp.einsum(
            "rhqk,rkhc->rhqc",
            weights_f.astype(jnp.bfloat16),
            value_block,
            preferred_element_type=jnp.float32,
        )
        return (new_max, denominator, numerator)

    running_max, denominator, numerator = lax.fori_loop(
        0, piece_len // block_size, one_block, start_carry
    )
    log_total = running_max + jnp.log(denominator)
    attended_heads = (numerator / denominator[..., None]).transpose(0, 2, 1, 3)
    attended = attended_heads.reshape(token_count, model_width)
    attn_low = attended.astype(jnp.bfloat16)
    branch = jnp.dot(attn_low, out_weight, preferred_element_type=jnp.float32) + out_bias.astype(
        jnp.float32
    )
    gain_one = norm1_gain.astype(jnp.float32)
    hidden_norm, normed_one, inv_one = norm_forward(
        mixed_in + branch, gain_one, norm1_bias.astype(jnp.float32)
    )
    hidden_low = hidden_norm.astype(jnp.bfloat16)
    ffn_pre = jnp.dot(hidden_low, ffn_in, preferred_element_type=jnp.float32) + ffn_in_bias.astype(
        jnp.float32
    )
    ffn_act = gelu_value(ffn_pre).astype(jnp.bfloat16)
    ffn_branch = jnp.dot(
        ffn_act, ffn_out, preferred_element_type=jnp.float32
    ) + ffn_out_bias.astype(jnp.float32)
    gain_two = norm2_gain.astype(jnp.float32)
    layer_out, normed_two, inv_two = norm_forward(
        hidden_norm + ffn_branch, gain_two, norm2_bias.astype(jnp.float32)
    )
    grad_top = cotangent.reshape(token_count, model_width).astype(jnp.float32)
    grad_second, norm2_gain_grad, norm2_bias_grad = norm_backward(
        grad_top, normed_two, inv_two, gain_two
    )
    grad_branch_two = grad_second.astype(jnp.bfloat16)
    ffn_out_grad = jnp.einsum(
        "nf,nd->fd", ffn_act, grad_branch_two, preferred_element_type=jnp.float32
    )
    ffn_out_bias_grad = jnp.sum(grad_branch_two.astype(jnp.float32), axis=0)
    grad_act = jnp.einsum("nd,fd->nf", grad_branch_two, ffn_out, preferred_element_type=jnp.float32)
    grad_pre = (grad_act * gelu_slope(ffn_pre)).astype(jnp.bfloat16)
    ffn_in_grad = jnp.einsum("nd,nf->df", hidden_low, grad_pre, preferred_element_type=jnp.float32)
    ffn_in_bias_grad = jnp.sum(grad_pre.astype(jnp.float32), axis=0)
    grad_hidden = grad_second + jnp.einsum(
        "nf,df->nd", grad_pre, ffn_in, preferred_element_type=jnp.float32
    )
    grad_first, norm1_gain_grad, norm1_bias_grad = norm_backward(
        grad_hidden, normed_one, inv_one, gain_one
    )
    grad_branch = grad_first.astype(jnp.bfloat16)
    out_weight_grad = jnp.einsum(
        "ne,nd->ed", attn_low, grad_branch, preferred_element_type=jnp.float32
    )
    out_bias_grad = jnp.sum(grad_branch.astype(jnp.float32), axis=0)
    grad_att = jnp.einsum("nd,ed->ne", grad_branch, out_weight, preferred_element_type=jnp.float32)
    grad_heads = grad_att.astype(jnp.bfloat16).reshape(row_count, block_len, HEADS, head_dim)
    row_delta = jnp.einsum("rqhc,rqhc->rhq", grad_heads.astype(jnp.float32), attended_heads)
    zero_heads = jnp.zeros((row_count, block_len, HEADS, head_dim), jnp.float32)

    def key_step(carried):
        key_block, value_block, seg_block, key_grad, value_grad, query_grad = carried
        query_part, key_part, value_part = block_grads(
            query_heads,
            grad_heads,
            query_seg,
            log_total,
            row_delta,
            key_block,
            value_block,
            seg_block,
            score_scale,
        )
        query_grad = query_grad + query_part
        key_grad = key_grad + key_part
        value_grad = value_grad + value_part
        key_block, value_block, seg_block = from_behind(
            (key_block, value_block, seg_block), "blk", 1
        )
        key_grad, value_grad = (
            from_behind(key_grad.astype(jnp.bfloat16), "blk", 1).astype(key_grad.dtype),
            from_behind(value_grad.astype(jnp.bfloat16), "blk", 1).astype(value_grad.dtype),
        )
        return (key_block, value_block, seg_block, key_grad, value_grad, query_grad)

    def four_steps(turn_index, carried):
        for repeat in range(4):
            carried = key_step(carried)
        return carried

    final_state = lax.fori_loop(
        0,
        cycle_len // 4,
        four_steps,
        (key_heads, value_heads, query_seg, zero_heads, zero_heads, zero_heads),
    )
    key_grad, value_grad, query_grad = (final_state[3], final_state[4], final_state[5])
    grad_project = jnp.concatenate(
        [
            query_grad.reshape(token_count, model_width),
            key_grad.reshape(token_count, model_width),
            value_grad.reshape(token_count, model_width),
        ],
        axis=1,
    ).astype(jnp.bfloat16)
    qkv_weight_grad = jnp.einsum(
        "nd,ne->de", mixed_low, grad_project, preferred_element_type=jnp.float32
    )
    bias_sums = jnp.sum(grad_project.astype(jnp.float32), axis=0)
    qv_bias_grad = jnp.concatenate([bias_sums[:model_width], bias_sums[2 * model_width :]])
    grad_mixed = grad_first + jnp.einsum(
        "ne,de->nd", grad_project, qkv_weight, preferred_element_type=jnp.float32
    )
    grad_conv = (grad_mixed * gelu_slope(pre_conv)).astype(jnp.bfloat16)
    conv_bias_grad = jnp.sum(grad_conv.astype(jnp.float32), axis=0)
    grad_conv_rows = grad_conv.reshape(row_count, block_len, model_width)
    grad_padded = with_halo(grad_conv_rows, (("blk", 1),), half_kernel)
    flipped = conv_weight.reshape(GROUPS, group_width, group_width, kernel).transpose(0, 2, 1, 3)
    flipped = flipped.reshape(model_width, group_width, kernel)[:, :, ::-1]
    back_conv = lax.conv_general_dilated(
        grad_padded,
        flipped,
        (1,),
        "VALID",
        dimension_numbers=("NWC", "OIW", "NWC"),
        feature_group_count=GROUPS,
        preferred_element_type=jnp.float32,
    )[:, 1:]
    frames_grad = (
        grad_mixed.reshape(row_count, block_len, model_width)
        + jnp.where(is_valid[..., None], back_conv, 0.0)
    ).astype(jnp.bfloat16)
    conv_weight_grad = lax.conv_general_dilated(
        padded,
        grad_conv_rows,
        (1,),
        "VALID",
        dimension_numbers=("CWN", "IWO", "CNW"),
        batch_group_count=GROUPS,
        preferred_element_type=jnp.float32,
    )[:, :, :kernel]
    (
        conv_weight_part,
        conv_bias_part,
        qkv_weight_part,
        qv_bias_part,
        out_weight_part,
        out_bias_part,
        gain_one_part,
        shift_one_part,
        ffn_in_part,
        ffn_in_bias_part,
        ffn_out_part,
        ffn_out_bias_part,
        gain_two_part,
        shift_two_part,
    ) = (
        lax.psum_scatter(conv_weight_grad, "blk", scatter_dimension=0, tiled=True),
        lax.psum_scatter(conv_bias_grad, "blk", scatter_dimension=0, tiled=True),
        lax.psum_scatter(qkv_weight_grad, "blk", scatter_dimension=0, tiled=True),
        lax.psum_scatter(qv_bias_grad, "blk", scatter_dimension=0, tiled=True),
        lax.psum_scatter(out_weight_grad, "blk", scatter_dimension=0, tiled=True),
        lax.psum_scatter(out_bias_grad, "blk", scatter_dimension=0, tiled=True),
        lax.psum_scatter(norm1_gain_grad, "blk", scatter_dimension=0, tiled=True),
        lax.psum_scatter(norm1_bias_grad, "blk", scatter_dimension=0, tiled=True),
        lax.psum_scatter(ffn_in_grad, "blk", scatter_dimension=0, tiled=True),
        lax.psum_scatter(ffn_in_bias_grad, "blk", scatter_dimension=0, tiled=True),
        lax.psum_scatter(ffn_out_grad, "blk", scatter_dimension=0, tiled=True),
        lax.psum_scatter(ffn_out_bias_grad, "blk", scatter_dimension=0, tiled=True),
        lax.psum_scatter(norm2_gain_grad, "blk", scatter_dimension=0, tiled=True),
        lax.psum_scatter(norm2_bias_grad, "blk", scatter_dimension=0, tiled=True),
    )
    totals = (
        lax.psum(conv_weight_part.astype(jnp.bfloat16), "dp").astype(jnp.float32),
        lax.psum(conv_bias_part.astype(jnp.bfloat16), "dp").astype(jnp.float32),
        lax.psum(qkv_weight_part.astype(jnp.bfloat16), "dp").astype(jnp.float32),
        lax.psum(qv_bias_part.astype(jnp.bfloat16), "dp").astype(jnp.float32),
        lax.psum(out_weight_part.astype(jnp.bfloat16), "dp").astype(jnp.float32),
        lax.psum(out_bias_part.astype(jnp.bfloat16), "dp").astype(jnp.float32),
        lax.psum(gain_one_part.astype(jnp.bfloat16), "dp").astype(jnp.float32),
        lax.psum(shift_one_part.astype(jnp.bfloat16), "dp").astype(jnp.float32),
        lax.psum(ffn_in_part.astype(jnp.bfloat16), "dp").astype(jnp.float32),
        lax.psum(ffn_in_bias_part.astype(jnp.bfloat16), "dp").astype(jnp.float32),
        lax.psum(ffn_out_part.astype(jnp.bfloat16), "dp").astype(jnp.float32),
        lax.psum(ffn_out_bias_part.astype(jnp.bfloat16), "dp").astype(jnp.float32),
        lax.psum(gain_two_part.astype(jnp.bfloat16), "dp").astype(jnp.float32),
        lax.psum(shift_two_part.astype(jnp.bfloat16), "dp").astype(jnp.float32),
    )
    return (
        layer_out.reshape(row_count, block_len, model_width).astype(jnp.bfloat16),
        frames_grad,
        totals[0],
        totals[1],
        totals[2],
        totals[3],
        totals[4],
        totals[5],
        totals[6],
        totals[7],
        totals[8],
        totals[9],
        totals[10],
        totals[11],
        totals[12],
        totals[13],
    )


MESH = pl.DeviceIdType.MESH
LANES = 128
TAP_STEP = 16
VMEM = pl.BlockSpec(memory_space=pltpu.VMEM)


def peer(me, step, count):
    return lax.rem(me + step, count)


def greet(index, count, rows):
    barrier = pltpu.get_barrier_semaphore()
    for step in range(1, count * rows):
        other = lax.rem(index + step, count * rows)
        pl.semaphore_signal(
            barrier,
            inc=1,
            device_id={"dp": other // count, "blk": lax.rem(other, count)},
            device_id_type=MESH,
        )


def greet_wait(count, rows):
    pl.semaphore_wait(pltpu.get_barrier_semaphore(), count * rows - 1)


def remote(src, dst, send_sem, recv_sem, target, axis="blk"):
    copy = pltpu.make_async_remote_copy(
        src_ref=src,
        dst_ref=dst,
        send_sem=send_sem,
        recv_sem=recv_sem,
        device_id=target if isinstance(target, dict) else {axis: target},
        device_id_type=MESH,
    )
    copy.start()
    return copy


def turned(value):
    return value.astype(jnp.float32).T.astype(jnp.bfloat16)


def matmul_turned(left, right):
    return lax.dot_general(
        left, right, (((1,), (1,)), ((), ())), preferred_element_type=jnp.float32
    )


def sum_parts(parts_ref):
    total = parts_ref[0].astype(jnp.float32)
    for part in range(1, parts_ref.shape[0]):
        total = total + parts_ref[part].astype(jnp.float32)
    return total


def lane_block(index):
    return pl.ds(pl.multiple_of(index * LANES, LANES), LANES)


def row_block(index, size):
    return pl.ds(pl.multiple_of(index * size, size), size)


def swap_blocks(tiles, width):
    count = len(tiles)
    lane = lax.broadcasted_iota(jnp.int32, tiles[0].shape, 1) // width
    tiles = list(tiles)
    step = count // 2
    while step:
        low = (lane & step) == 0
        for u in range(count):
            if u & step == 0:
                one, two = tiles[u], tiles[u + step]
                tiles[u] = jnp.where(low, one, pltpu.roll(two, step * width, 1))
                tiles[u + step] = jnp.where(low, pltpu.roll(one, LANES - step * width, 1), two)
        step //= 2
    return tiles


def spread_taps(source, offset, direction, stage_ref, out_ref):
    rows, length = source.shape
    blocks = out_ref.shape[1] // LANES
    for tap in range(TAP_STEP):
        shift = (length - offset - direction * tap) % length
        moved = pltpu.roll(source, shift, 1)
        for block in range(blocks):
            first = block * rows * TAP_STEP + tap
            stage_ref[pl.ds(first, rows, stride=TAP_STEP), :] = moved[
                :, block * LANES : (block + 1) * LANES
            ]
    size = rows * TAP_STEP
    for block in range(blocks):
        out_ref[:, block * LANES : (block + 1) * LANES] = stage_ref[
            block * size : (block + 1) * size, :
        ].astype(jnp.bfloat16)


def query_span(index, size):
    return pl.ds(pl.multiple_of(index * size, size), size)


def same_clip(column_ref, seg_row):
    column = column_ref[...]
    parts = [
        column == seg_row[:, start : start + LANES]
        for start in range(0, seg_row.shape[1], LANES)
    ]
    return jnp.concatenate(parts, axis=1)


def clip_column(count, segs_ref, column_ref):
    for block in range(count):
        row = segs_ref[block].astype(jnp.float32)
        column_ref[block * LANES : (block + 1) * LANES, :] = jnp.broadcast_to(
            row, (LANES, LANES)
        ).T


def clip_row(segs_ref, first, size):
    parts = [segs_ref[first + i].astype(jnp.float32) for i in range(size // LANES)]
    return jnp.concatenate(parts, axis=1)


def layer_kernel(names, count, rows_count, head_dim, *refs):
    R = types.SimpleNamespace(**dict(zip(names, refs)))
    low, f32 = jnp.bfloat16, jnp.float32
    me, row = lax.axis_index("blk"), lax.axis_index("dp")
    level, side = me // 2, lax.rem(me, 2)
    levels = count // 2
    half = count // 2
    near = me + 1 - 2 * side
    core = lax.rem(row, 2)
    twin = row + 1 - 2 * core
    upper = level // 2
    pos = 4 * core + 2 * lax.rem(level, 2) + side
    home_row = 2 * (row // 2) + upper
    at_home = core == upper
    across = peer(row, 2, rows_count)
    tokens, width = R.frames.shape
    channels = width // count
    length = count * LANES
    group_width = R.own_weight.shape[1]
    groups = channels // group_width
    steps = LANES // TAP_STEP
    scale = head_dim ** (-0.5)
    chunks = R.in_hbm.shape[1] // width

    def send(kind, step, source, target_ref, target, axis="blk"):
        return remote(
            source, target_ref, R.out_sem.at[kind, step], R.in_sem.at[kind, step], target, axis
        )

    def wait(copies):
        for copy in copies:
            copy.wait()

    def to_blocks(kind, source, target_ref):
        copies = []
        for step in range(1, count):
            target = peer(me, step, count)
            copies.append(send(kind, step, source(target), target_ref, target))
        return copies

    def device_at(place, part):
        return {"dp": 2 * (row // 2) + place // 4, "blk": 4 * part + lax.rem(place, 4)}

    def to_places(kind, source, target_ref):
        copies = []
        for step in range(1, count):
            target = peer(pos, step, count)
            copies.append(send(kind, step, source(target), target_ref, device_at(target, upper)))
        return copies

    def move(kind, source, target_ref, device):
        copy = pltpu.make_async_remote_copy(
            src_ref=source,
            dst_ref=target_ref,
            send_sem=R.out_sem.at[kind, 0],
            recv_sem=R.in_sem.at[kind, 0],
            device_id=device,
            device_id_type=MESH,
        )
        away = jnp.logical_not(at_home)
        pl.when(away)(copy.start)

        @pl.when(at_home)
        def _():
            target_ref[...] = source[...]

        return [(away, away, copy)]

    def shift_all(kind, first, own, device_of, source, target_ref):
        pending = []
        for step in range(count):
            target = peer(first, step, count)
            away = jnp.logical_not(jnp.logical_and(at_home, target == own))
            copy = pltpu.make_async_remote_copy(
                src_ref=source(target),
                dst_ref=target_ref,
                send_sem=R.out_sem.at[kind, step],
                recv_sem=R.in_sem.at[kind, step],
                device_id=device_of(target),
                device_id_type=MESH,
            )
            pl.when(away)(copy.start)
            pending.append((away, away, copy))

        @pl.when(at_home)
        def _():
            target_ref[...] = source(own)[...]

        return pending

    def to_level(kind, source, target_ref):
        return shift_all(
            kind, me, pos, lambda place: device_at(place, core), source, target_ref
        )

    def from_level(kind, source, target_ref):
        return shift_all(
            kind, pos, me, lambda block: {"dp": home_row, "blk": block}, source, target_ref
        )

    def wait_some(pending):
        for sends, comes, copy in pending:
            pl.when(sends)(copy.wait_send)
            pl.when(comes)(copy.wait_recv)

    def chunk_of(index):
        return slice(index * width, (index + 1) * width)

    def table(index):
        return R.table[index : index + 1, :]

    def dot(left, right):
        return jnp.dot(left, right, preferred_element_type=f32)

    greet(row * count + me, count, rows_count)

    loads = [pltpu.make_async_copy(R.qkv_hbm, R.qkv_w, R.load_sem.at[0])]
    loads.append(pltpu.make_async_copy(R.out_hbm, R.out_w, R.load_sem.at[1]))
    for chunk in range(chunks):
        span = chunk_of(chunk)
        loads.append(
            pltpu.make_async_copy(
                R.in_hbm.at[:, span], R.in_w.at[:, span], R.load_sem.at[2 + 2 * chunk]
            )
        )
        loads.append(
            pltpu.make_async_copy(
                R.back_hbm.at[span], R.back_w.at[span], R.load_sem.at[3 + 2 * chunk]
            )
        )
    for load in loads:
        load.start()
    own_load = pltpu.make_async_copy(
        R.conv_hbm.at[row_block(me, channels)], R.own_weight, R.load_sem.at[2 + 2 * chunks]
    )
    own_load.start()
    valid = (R.segment[...] >= 0).astype(f32)
    R.turned[...] = (R.frames[...].astype(f32).T * valid).astype(low)
    to_level_device = device_at(me, core)
    from_level_device = {"dp": home_row, "blk": pos}

    R.table[...] = jnp.zeros_like(R.table)
    R.small[...] = jnp.zeros_like(R.small)
    place = 0
    for vector in VECTORS:
        ref = getattr(R, vector)
        for part in range(ref.shape[0] // width):
            R.table[place, :] = ref[chunk_of(part)].astype(f32)
            place += 1

    def mix_taps(mix, tile_rows):
        @pl.loop(0, group_width // steps)
        def _(block):
            for group in range(groups):
                tiles = [
                    R.stage[tile_rows(group, block * steps + u), :] for u in range(steps)
                ]
                for a, tile in enumerate(swap_blocks(tiles, TAP_STEP)):
                    rows = slice(a * group_width, (a + 1) * group_width)
                    mix[group, rows, lane_block(block)] = tile.astype(low)

    square = group_width * group_width
    own_load.wait()
    total_rows = channels * group_width
    R.stage[:total_rows, :] = R.own_weight[...].astype(f32).reshape(total_rows, LANES)
    mix_taps(R.mix, lambda g, i: pl.ds(g * square + i, group_width, stride=group_width))
    greet_wait(count, rows_count)

    copies = to_blocks(
        0, lambda p: R.turned.at[row_block(p, channels), :], R.column.at[:, lane_block(me + 1)]
    )
    brought = move(33, R.frames, R.frames_home, to_level_device)
    seg_pending = to_level(1, lambda p: R.segment, R.segs.at[me])
    R.column[:, lane_block(me + 1)] = R.turned[row_block(me, channels), :]
    for ref in (R.column, R.gcol):
        ref[:, :LANES] = jnp.zeros((channels, LANES), low)
        ref[:, length + LANES :] = jnp.zeros((channels, LANES), low)
    mix_taps(R.mix_back, lambda g, c: pl.ds(g * square + c * group_width, group_width))
    wait(copies)

    @pl.loop(0, groups)
    def _(group):
        rows = row_block(group, group_width)
        spread_taps(R.column[rows, :].astype(f32), LANES // 2, 1, R.stage, R.taps.at[group])
        product = dot(R.mix[group], R.taps[group])
        total = product[:group_width, :length]
        for a in range(1, steps):
            part = product[a * group_width : (a + 1) * group_width, :]
            part = pltpu.roll(part, product.shape[1] - a * TAP_STEP, 1)
            total = total + part[:, :length]
        R.result[rows, :] = total.astype(low)
    pending = to_level(
        2, lambda p: R.result.at[:, lane_block(p)], R.conv_home.at[row_block(me, channels), :]
    )
    @pl.loop(0, groups)
    def _(group):
        source = R.column[row_block(group, group_width), :].astype(f32)
        span = R.shifted.shape[2]
        for a in range(steps):
            moved = pltpu.roll(source, (span + LANES - a * TAP_STEP) % (span + LANES), 1)
            R.shifted[group, a * group_width : (a + 1) * group_width, :] = moved[:, :span].astype(
                low
            )
    wait_some(seg_pending)
    clip_column(count, R.segs, R.clip)
    wait_some(brought)
    wait_some(pending)
    brought = move(34, R.cotangent, R.cotangent_home, to_level_device)

    pre = R.conv_home[...].astype(f32).T + table(0)
    share = 0.5 * (1.0 + lax.erf(pre * ROOT_HALF))
    R.slope[...] = share + pre * jnp.exp(-0.5 * pre * pre) * DENSITY_CONST
    mixed = R.frames_home[...].astype(f32) + pre * share
    R.mixed[...] = mixed
    mixed_low = mixed.astype(low)
    loads[0].wait()
    for part in range(3):
        block = dot(mixed_low, R.qkv_w[:, chunk_of(part)])
        if part != 1:
            block = block + table(1 + part // 2)
        block = block.astype(low).astype(f32)
        if part == 0:
            block = block * scale
        R.project[part] = block.T.astype(low)
    copies = to_places(
        3,
        lambda p: R.project.at[:, row_block(p, head_dim), :],
        R.main.at[:, :, lane_block(pos)],
    )
    copies += to_places(
        4,
        lambda p: R.project.at[:, row_block(count + p // 2, head_dim), :],
        R.extra.at[:, :, lane_block(pos)],
    )
    R.main[:, :, lane_block(pos)] = R.project[:, row_block(pos, head_dim), :]
    R.extra[:, :, lane_block(pos)] = R.project[:, row_block(count + pos // 2, head_dim), :]
    R.left[0] = turned(mixed_low)
    last_row = rows_count - 1

    def to_some_rows(kind, source, sends_to, comes_to):
        pending = []
        for step in range(1, rows_count):
            target = peer(row, step, rows_count)
            copy = pltpu.make_async_remote_copy(
                src_ref=source,
                dst_ref=R.late_left.at[:, lane_block(row)],
                send_sem=R.out_sem.at[kind, step],
                recv_sem=R.in_sem.at[kind, step],
                device_id={"dp": target},
                device_id_type=MESH,
            )
            sends = sends_to(target)
            pl.when(sends)(copy.start)
            pending.append((sends, comes_to, copy))
        return pending

    left_pending = to_some_rows(8, R.left.at[0], lambda p: p != last_row, row != last_row)
    wait(copies)

    size = 2 * LANES
    halves = half * LANES // size

    def scores_of(held, start, seg_row):
        scores = lax.dot_general(
            held[1], held[0, :, start], (((0,), (0,)), ((), ())), preferred_element_type=f32
        )
        return jnp.where(same_clip(R.clip, seg_row), scores, -1e30)

    def attend(held, start, index, att_ref, low_ref, lse_ref, place):
        scores = scores_of(held, start, clip_row(R.segs, index * 2, size))
        top = jnp.max(scores, axis=0, keepdims=True)
        weights = jnp.exp(scores - top)
        total = jnp.sum(weights, axis=0, keepdims=True)
        mean = dot(held[2], weights.astype(low)) / total
        att_ref[:, place] = mean
        low_ref[:, start] = mean.astype(low)
        lse_ref[:, place] = top + jnp.log(total)

    own_rows = row_block(pos, head_dim)
    extra_rows = row_block(count + pos // 2, head_dim)

    def to_half(kind, source, target_ref):
        pending = []
        for step in range(1, count):
            target, origin = peer(pos, step, count), peer(pos, count - step, count)
            copy = pltpu.make_async_remote_copy(
                src_ref=source(target),
                dst_ref=target_ref,
                send_sem=R.out_sem.at[kind, step],
                recv_sem=R.in_sem.at[kind, step],
                device_id=device_at(target, upper),
                device_id_type=MESH,
            )
            sends, comes = target // half == side, pos // half == lax.rem(origin, 2)
            pl.when(sends)(copy.start)
            pending.append((sends, comes, copy))
        return pending

    @pl.loop(0, halves)
    def _(block):
        index = side * halves + block
        place = query_span(block, size)
        attend(
            R.extra,
            query_span(index, size),
            index,
            R.att_extra,
            R.low_extra,
            R.lse_extra,
            place,
        )
    pending = to_half(5, lambda p: R.low_extra.at[:, lane_block(p)], R.att_home.at[extra_rows, :])

    @pl.when(pos // half == side)
    def _():
        R.att_home[extra_rows, :] = R.low_extra[:, lane_block(pos)]

    @pl.loop(0, length // size)
    def _(block):
        span = query_span(block, size)
        attend(R.main, span, block, R.att_main, R.low_main, R.lse_main, span)

    copies = to_places(6, lambda p: R.low_main.at[:, lane_block(p)], R.att_home.at[own_rows, :])
    R.att_home[own_rows, :] = R.low_main[:, lane_block(pos)]
    wait(copies)
    wait_some(pending)

    def to_rows(kind, source, target_ref):
        return [
            send(kind, step, source(peer(row, step, rows_count)), target_ref, target, "dp")
            for step, target in ((n, peer(row, n, rows_count)) for n in range(1, rows_count))
        ]

    def share_start(kind, part):
        own = part(row)
        return [send(kind, 2, own, own, across, "dp"), send(kind, 1, own, own, twin, "dp")]

    def share_forward(kind, part, copies):
        copies[0].wait()
        got = part(across)
        copies[0] = send(kind, 3, got, got, twin, "dp")

    def lanes_of(ref):
        return lambda index: ref.at[:, lane_block(index)]

    R.left[1] = R.att_home[...]
    att = R.att_home[...].astype(f32).T.astype(low)
    loads[1].wait()
    branch = dot(att, R.out_w[...]) + table(3)
    hidden, normed_one, inv_one = norm_forward(R.mixed[...] + branch, table(4), table(5))
    hidden_low = hidden.astype(low)
    R.hidden_all[:, lane_block(row)] = turned(hidden_low)
    hidden_copies = share_start(7, lanes_of(R.hidden_all))
    left_pending += to_some_rows(32, R.left.at[1], lambda p: p == last_row, row == last_row)
    R.late_left[:, lane_block(row)] = R.left[row // last_row]
    pieces = count // chunks
    for load in loads[2:]:
        load.wait()
    R.total[...] = hidden + table(10)

    @pl.loop(0, chunks)
    def _(chunk):
        span = query_span(chunk, width)
        pre = dot(hidden_low, R.in_w[:, span]) + R.table[pl.ds(6 + chunk, 1), :]
        share = 0.5 * (1.0 + lax.erf(pre * ROOT_HALF))
        act = (pre * share).astype(low)
        R.keep[:, span] = share + pre * jnp.exp(-0.5 * pre * pre) * DENSITY_CONST
        R.act_turned[pl.ds(chunk * pieces, pieces)] = turned(act).reshape(
            pieces, rows_count, -1, LANES
        )
        R.total[...] += dot(act, R.back_w[row_block(chunk, width), :])

    act_copies = to_rows(9, lambda p: R.act_turned.at[:, p], R.act_all.at[:, :, lane_block(row)])
    R.act_all[:, :, lane_block(row)] = R.act_turned[:, row]
    layer, normed_two, inv_two = norm_forward(R.total[...], table(11), table(12))
    R.layer_here[...] = layer.astype(low)
    layer_pending = move(35, R.layer_here, R.layer_got, from_level_device)
    wait_some(brought)
    grad_second, gain_sum, shift_sum = norm_backward(
        R.cotangent_home[...].astype(f32), normed_two, inv_two, table(11)
    )
    R.small[11, :] = gain_sum
    R.small[12, :] = shift_sum
    grad_two = grad_second.astype(low)
    R.two_all[:, lane_block(row)] = turned(grad_two)
    two_copies = share_start(10, lanes_of(R.two_all))
    R.small[10, :] = jnp.sum(grad_two.astype(f32), axis=0)
    R.total[...] = grad_second

    @pl.loop(0, chunks)
    def _(chunk):
        span = query_span(chunk, width)
        grad_pre = matmul_turned(grad_two, R.back_w[row_block(chunk, width), :]) * R.keep[:, span]
        grad_pre = grad_pre.astype(low)
        R.pre_turned[chunk] = turned(grad_pre)
        R.small[pl.ds(6 + chunk, 1), :] = jnp.sum(grad_pre.astype(f32), axis=0, keepdims=True)
        R.total[...] += matmul_turned(grad_pre, R.in_w[:, span])

    grad_first, gain_sum, shift_sum = norm_backward(R.total[...], normed_one, inv_one, table(4))
    R.small[4, :] = gain_sum
    R.small[5, :] = shift_sum
    R.mixed[...] = grad_first
    grad_branch = grad_first.astype(low)
    R.small[3, :] = jnp.sum(grad_branch.astype(f32), axis=0)
    R.turned[...] = turned(matmul_turned(grad_branch, R.out_w[...]).astype(low))

    copies = to_places(
        11, lambda p: R.turned.at[row_block(p, head_dim), :], R.gmain.at[:, lane_block(pos)]
    )
    copies += to_places(
        12,
        lambda p: R.turned.at[row_block(count + p // 2, head_dim), :],
        R.gextra.at[:, lane_block(pos)],
    )
    R.gmain[:, lane_block(pos)] = R.turned[row_block(pos, head_dim), :]
    R.gextra[:, lane_block(pos)] = R.turned[row_block(count + pos // 2, head_dim), :]
    pre_copies = to_rows(13, lambda p: R.pre_turned.at[p], R.pre_all.at[:, lane_block(row)])
    R.pre_all[:, lane_block(row)] = R.pre_turned[row]
    R.dproject[3] = turned(grad_branch)
    wait(copies)

    def attend_back(held, grads, start, index, att, lse):
        queries = held[0, :, start]
        weights = jnp.exp(scores_of(held, start, clip_row(R.segs, index * 2, size)) - lse)
        grad_prob = lax.dot_general(
            held[2], grads, (((0,), (0,)), ((), ())), preferred_element_type=f32
        )
        delta = jnp.sum(grads.astype(f32) * att, axis=0, keepdims=True)
        grad_score = (weights * (grad_prob - delta)).astype(low)
        return (
            dot(held[1], grad_score) * scale,
            matmul_turned(queries, grad_score),
            matmul_turned(grads, weights.astype(low)),
        )

    R.dkey[...] = jnp.zeros_like(R.dkey)
    R.dvalue[...] = jnp.zeros_like(R.dvalue)

    @pl.loop(0, halves)
    def _(block):
        index = side * halves + block
        span = query_span(index, size)
        place = query_span(block, size)
        parts = attend_back(
            R.extra, R.gextra[:, span], span, index, R.att_extra[:, place], R.lse_extra[:, place]
        )
        R.dextra[0, :, span] = parts[0].astype(low)
        R.dkey[...] += parts[1]
        R.dvalue[...] += parts[2]

    R.dextra[1] = R.dkey[...].astype(low)
    R.dextra[2] = R.dvalue[...].astype(low)
    part_rows = row_block(pos // 2, head_dim)
    copies = to_places(
        14, lambda p: R.dextra.at[1:3, :, lane_block(p)], R.halves.at[side, :, part_rows, :]
    )
    pending = to_half(
        15, lambda p: R.dextra.at[0, :, lane_block(p)], R.dproject.at[0, extra_rows, :]
    )
    R.halves[side, :, part_rows, :] = R.dextra[1:3, :, lane_block(pos)]

    @pl.when(pos // half == side)
    def _():
        R.dproject[0, extra_rows, :] = R.dextra[0, :, lane_block(pos)]

    lower = lax.rem(level, 2)
    level_mate = me + 2 - 4 * lower
    upper_mate = me + 4 - 8 * upper

    def shard(u, bit, other, side_first):
        return row_block(4 * u + (2 * other + bit if side_first else 2 * bit + other), channels)

    def sum_begin(kind, slot, source, span, side_first):
        bit, mate = (side, near) if side_first else (lower, level_mate)
        return [
            send(
                kind,
                2 * u + v,
                R.in_w.at[shard(u, 1 - bit, v, side_first), source],
                R.got_one.at[slot, 2 * u + v, :, span],
                mate,
            )
            for u in range(2)
            for v in range(2)
        ]

    def sum_next(kind, slot, source, span, side_first, copies):
        wait(copies)
        bit, other = (side, lower) if side_first else (lower, side)
        mate = level_mate if side_first else near
        for u in range(2):
            for v in range(2):
                own = R.in_w[shard(u, bit, v, side_first), source]
                got = R.got_one[slot, 2 * u + v, :, span]
                R.sum_one[slot, 2 * u + v, :, span] = (own.astype(f32) + got.astype(f32)).astype(
                    low
                )
        return [
            send(
                kind,
                u,
                R.sum_one.at[slot, 2 * u + 1 - other, :, span],
                R.got_two.at[slot, u, :, span],
                mate,
            )
            for u in range(2)
        ]

    def sum_last(kind, slot, span, side_first, copies):
        wait(copies)
        other = lower if side_first else side
        for u in range(2):
            own = R.sum_one[slot, 2 * u + other, :, span]
            got = R.got_two[slot, u, :, span]
            R.sum_two[slot, u, :, span] = (own.astype(f32) + got.astype(f32)).astype(low)
        return [
            send(
                kind,
                0,
                R.sum_two.at[slot, 1 - upper, :, span],
                R.got_three.at[slot, :, span],
                upper_mate,
            )
        ]

    def summed(slot, copies):
        wait(copies)
        return (R.sum_two[slot, upper].astype(f32) + R.got_three[slot].astype(f32)).astype(low)

    every = slice(0, width)
    in_span, out_span = chunk_of(0), chunk_of(1)
    stores = []

    def store(index, source, target):
        copy = pltpu.make_async_copy(source, target, R.store_sem.at[index])
        copy.start()
        stores.append(copy)

    share_forward(10, lanes_of(R.two_all), two_copies)
    share_forward(7, lanes_of(R.hidden_all), hidden_copies)
    blocks = length // size

    def main_back(block):
        span = query_span(block, size)
        parts = attend_back(
            R.main, R.gmain[:, span], span, block, R.att_main[:, span], R.lse_main[:, span]
        )
        R.dmain[0, :, span] = parts[0].astype(low)
        R.dkey[...] += parts[1]
        R.dvalue[...] += parts[2]

    R.dkey[...] = jnp.zeros_like(R.dkey)
    R.dvalue[...] = jnp.zeros_like(R.dvalue)
    pl.loop(0, blocks // 2)(main_back)
    wait(two_copies)
    wait(act_copies)
    product = matmul_turned(R.act_all[...].reshape(width, -1), R.two_all[...])
    R.in_w[:, out_span] = product.astype(low)
    out_copies = sum_begin(18, 1, out_span, every, False)
    pl.loop(blocks // 2, blocks)(main_back)
    R.dmain[1] = R.dkey[...].astype(low)
    R.dmain[2] = R.dvalue[...].astype(low)
    copies += to_places(
        16, lambda p: R.dmain.at[:, :, lane_block(p)], R.dproject.at[0:3, own_rows, :]
    )
    R.dproject[0:3, own_rows, :] = R.dmain[:, :, lane_block(pos)]
    wait(hidden_copies)
    wait(pre_copies)
    R.in_w[:, in_span] = matmul_turned(R.hidden_all[...], R.pre_all[...]).astype(low)
    in_copies = sum_begin(17, 0, in_span, every, True)
    wait(copies)
    wait_some(pending)
    first = half * head_dim
    for which in range(2):
        total = R.halves[0, which].astype(f32) + R.halves[1, which].astype(f32)
        R.dproject[1 + which, width - first :, :] = total.astype(low)

    late = to_rows(19, lambda p: R.dproject.at[p], R.late_right.at[:, lane_block(row)])
    R.late_right[:, lane_block(row)] = R.dproject[row]
    grad_mixed = R.mixed[...]
    for part in range(3):
        block = R.dproject[part].astype(f32).T
        if part != 1:
            R.small[1 + part // 2, :] = jnp.sum(block, axis=0)
        grad_mixed = grad_mixed + matmul_turned(block.astype(low), R.qkv_w[:, chunk_of(part)])
    R.mixed_here[...] = grad_mixed.astype(low)
    grad_conv = (grad_mixed * R.slope[...]).astype(low)
    R.conv_turned[...] = turned(grad_conv)
    conv_pending = from_level(
        20, lambda b: R.conv_turned.at[row_block(b, channels), :], R.gcol.at[:, lane_block(pos + 1)]
    )
    R.small[0, :] = jnp.sum(grad_conv.astype(f32), axis=0)
    small_copy = send(21, 0, R.small, R.small_got.at[0], twin, "dp")
    out_copies = sum_next(23, 1, out_span, every, False, out_copies)
    in_copies = sum_next(22, 0, in_span, every, True, in_copies)
    mixed_pending = move(36, R.mixed_here, R.mixed_got, from_level_device)
    wait_some(conv_pending)
    @pl.loop(0, groups)
    def _(group):
        rows = row_block(group, group_width)
        spread_taps(R.gcol[rows, :].astype(f32), LANES // 2, -1, R.stage, R.taps.at[group])
        product = dot(R.mix_back[group], R.taps[group])
        total = product[:group_width, LANES:]
        for a in range(1, steps):
            part = product[a * group_width : (a + 1) * group_width, :]
            total = total + pltpu.roll(part, a * TAP_STEP, 1)[:, LANES:]
        R.result[rows, :] = total.astype(low)
    back = to_blocks(
        24, lambda p: R.result.at[:, lane_block(p)], R.back_home.at[row_block(me, channels), :]
    )
    R.back_home[row_block(me, channels), :] = R.result[:, lane_block(me)]

    wait(late)
    wait_some(left_pending)
    product = matmul_turned(R.late_left[...], R.late_right[...])
    R.in_w[:, chunk_of(2)] = product.astype(low)
    middle = width // 2
    parts = (
        (26, slice(2 * width, 2 * width + middle), slice(0, middle), True),
        (28, slice(2 * width + middle, 3 * width), slice(middle, width), False),
    )
    att_copies = [sum_begin(kind, 2, source, span, first) for kind, source, span, first in parts]
    out_copies = sum_last(37, 1, every, False, out_copies)
    quarter = channels // rows_count
    @pl.loop(0, groups)
    def _(group):
        grad = matmul_turned(R.shifted[group], R.taps[group])
        for block in range(group_width // steps):
            span = slice(block * LANES, (block + 1) * LANES)
            tiles = [
                grad[a * group_width : (a + 1) * group_width, span] for a in range(steps)
            ]
            for u, tile in enumerate(swap_blocks(tiles, TAP_STEP)):
                channel = block * steps + u
                R.conv_part[group, channel // quarter, channel % quarter] = tile.astype(low)
    conv_copy = send(25, 0, R.conv_part.at[:, 1 - core], R.conv_got, twin, "dp")
    small_copy.wait()
    R.small_sum[0] = R.small[...] + R.small_got[0]
    small_copy = send(21, 1, R.small_sum.at[0], R.small_got.at[1], across, "dp")
    in_copies = sum_last(38, 0, every, True, in_copies)
    att_copies = [
        sum_next(kind + 1, 2, source, span, first, copies)
        for (kind, source, span, first), copies in zip(parts, att_copies)
    ]
    conv_copy.wait()
    for part in range(2):
        R.conv_sum[part] = (
            R.conv_part[part, core].astype(f32) + R.conv_got[part].astype(f32)
        ).astype(low)
    conv_copy = send(25, 1, R.conv_sum.at[1 - row // 2], R.conv_far, across, "dp")
    small_copy.wait()
    R.small_sum[1] = R.small_sum[0] + R.small_got[1]
    small_copy = send(21, 2, R.small_sum.at[1], R.small_got.at[2], near)

    def slots_of(ref):
        return lambda index: ref.at[index]

    def part_of(ref, which):
        return lambda index: ref.at[index, which]

    R.ffn_sums[row, 1] = summed(1, out_copies)
    out_share = share_start(43, part_of(R.ffn_sums, 1))
    R.ffn_sums[row, 0] = summed(0, in_copies)
    in_share = share_start(40, part_of(R.ffn_sums, 0))
    att_copies = [
        sum_last(kind + 13, 2, span, first, copies)
        for (kind, source, span, first), copies in zip(parts, att_copies)
    ]
    wait(back)
    wait_some(mixed_pending)
    R.frames_done[...] = (
        R.mixed_got[...].astype(f32) + (R.back_home[...].astype(f32) * valid).T
    ).astype(low)
    store(0, R.frames_done, R.frames_out)
    wait_some(layer_pending)
    store(1, R.layer_got, R.layer_out)
    conv_copy.wait()
    R.conv_sums[row] = (
        R.conv_sum[row // 2].astype(f32) + R.conv_far[...].astype(f32)
    ).astype(low)
    conv_share = share_start(42, slots_of(R.conv_sums))
    small_copy.wait()
    R.small_far[level] = R.small_sum[1] + R.small_got[2]
    smalls = []
    for step in range(1, levels):
        target = 2 * peer(level, step, levels) + side
        smalls.append(
            send(30, step, R.small_far.at[level], R.small_far.at[level], target)
        )
    share_forward(43, part_of(R.ffn_sums, 1), out_share)
    share_forward(40, part_of(R.ffn_sums, 0), in_share)
    R.attn_sums[row] = summed(2, att_copies[0] + att_copies[1])
    att_share = share_start(31, slots_of(R.attn_sums))
    share_forward(42, slots_of(R.conv_sums), conv_share)
    wait(smalls)
    R.small_done[...] = sum_parts(R.small_far)
    store(2, R.small_done, R.small_out)
    wait(out_share)
    wait(in_share)
    store(3, R.ffn_sums, R.ffn_out)
    wait(conv_share)
    store(4, R.conv_sums, R.conv_out)
    share_forward(31, slots_of(R.attn_sums), att_share)
    wait(att_share)
    store(5, R.attn_sums, R.attn_out)
    for copy in stores:
        copy.wait()


VECTORS = (
    "conv_bias",
    "qv_bias",
    "out_bias",
    "gain_one",
    "shift_one",
    "in_bias",
    "back_bias",
    "gain_two",
    "shift_two",
)


def layer(count, rows_count, head_dim, named):
    low, f32 = jnp.bfloat16, jnp.float32
    tokens, width = named["frames"].shape
    wide = named["in_hbm"].shape[1]
    _, group_width, kernel = named["conv_hbm"].shape
    channels = width // count
    groups = channels // group_width
    length = count * LANES
    span = length + LANES
    steps = kernel // TAP_STEP
    taps = group_width * TAP_STEP
    every = rows_count * tokens
    piece = channels // rows_count
    extras = count // 2 * head_dim
    levels = count // 2
    outs = {
        "layer_out": ((tokens, width), low),
        "frames_out": ((tokens, width), low),
        "conv_out": ((rows_count, piece, group_width, kernel), low),
        "ffn_out": ((rows_count, 2, channels, width), low),
        "attn_out": ((rows_count, channels, width), low),
        "small_out": ((16, width), f32),
    }
    scratch = {
        "qkv_w": (named["qkv_hbm"].shape, low),
        "out_w": (named["out_hbm"].shape, low),
        "in_w": (named["in_hbm"].shape, low),
        "back_w": (named["back_hbm"].shape, low),
        "table": ((16, width), f32),
        "small": ((16, width), f32),
        "small_got": ((3, 16, width), f32),
        "small_sum": ((2, 16, width), f32),
        "small_far": ((levels, 16, width), f32),
        "turned": ((width, tokens), low),
        "conv_turned": ((width, tokens), low),
        "column": ((channels, span + LANES), low),
        "gcol": ((channels, span + LANES), low),
        "segs": ((count, 1, LANES), jnp.int32),
        "clip": ((length, LANES), f32),
        "stage": ((span // LANES * taps, LANES), f32),
        "own_weight": ((channels, group_width, kernel), low),
        "frames_home": ((tokens, width), low),
        "cotangent_home": ((tokens, width), low),
        "layer_here": ((tokens, width), low),
        "mixed_here": ((tokens, width), low),
        "mixed_got": ((tokens, width), low),
        "taps": ((groups, taps, span), low),
        "mix": ((groups, steps * group_width, taps), low),
        "mix_back": ((groups, steps * group_width, taps), low),
        "shifted": ((groups, steps * group_width, span), low),
        "result": ((channels, length), low),
        "conv_home": ((width, tokens), low),
        "back_home": ((width, tokens), low),
        "slope": ((tokens, width), f32),
        "mixed": ((tokens, width), f32),
        "project": ((3, width, tokens), low),
        "main": ((3, head_dim, length), low),
        "extra": ((3, head_dim, length), low),
        "att_main": ((head_dim, length), f32),
        "att_extra": ((head_dim, length // 2), f32),
        "low_main": ((head_dim, length), low),
        "low_extra": ((head_dim, length), low),
        "lse_main": ((1, length), f32),
        "lse_extra": ((1, length // 2), f32),
        "att_home": ((width, tokens), low),
        "keep": ((tokens, wide), f32),
        "total": ((tokens, width), f32),
        "dkey": ((head_dim, length), f32),
        "dvalue": ((head_dim, length), f32),
        "left": ((2, width, tokens), low),
        "act_turned": ((count, rows_count, wide // (count * rows_count), tokens), low),
        "pre_turned": ((rows_count, width, tokens), low),
        "hidden_all": ((width, every), low),
        "two_all": ((width, every), low),
        "pre_all": ((width, every), low),
        "act_all": ((count, wide // (count * rows_count), every), low),
        "late_left": ((width, every), low),
        "late_right": ((width, every), low),
        "gmain": ((head_dim, length), low),
        "gextra": ((head_dim, length), low),
        "dmain": ((3, head_dim, length), low),
        "dextra": ((3, head_dim, length), low),
        "dproject": ((4, width, tokens), low),
        "halves": ((2, 2, extras, tokens), low),
        "got_one": ((3, 4, channels, width), low),
        "sum_one": ((3, 4, channels, width), low),
        "got_two": ((3, 2, channels, width), low),
        "sum_two": ((3, 2, channels, width), low),
        "got_three": ((3, channels, width), low),
        "layer_got": ((tokens, width), low),
        "frames_done": ((tokens, width), low),
        "small_done": ((16, width), f32),
        "ffn_sums": ((rows_count, 2, channels, width), low),
        "conv_sums": ((rows_count, piece, group_width, kernel), low),
        "attn_sums": ((rows_count, channels, width), low),
        "conv_part": ((2, 2, piece, group_width, kernel), low),
        "conv_got": ((2, piece, group_width, kernel), low),
        "conv_sum": ((2, piece, group_width, kernel), low),
        "conv_far": ((piece, group_width, kernel), low),
    }
    hbm = pl.BlockSpec(memory_space=pl.ANY)
    names = (*named, *outs, *scratch, "out_sem", "in_sem", "load_sem", "store_sem")
    return pl.pallas_call(
        functools.partial(layer_kernel, names, count, rows_count, head_dim),
        out_shape=tuple(jax.ShapeDtypeStruct(*out) for out in outs.values()),
        in_specs=[hbm if name.endswith("_hbm") else VMEM for name in named],
        out_specs=(hbm,) * len(outs),
        scratch_shapes=[pltpu.VMEM(*item) for item in scratch.values()]
        + [
            pltpu.SemaphoreType.DMA((44, count)),
            pltpu.SemaphoreType.DMA((44, count)),
            pltpu.SemaphoreType.DMA((3 + 2 * (wide // width),)),
            pltpu.SemaphoreType.DMA((len(outs),)),
        ],
        compiler_params=pltpu.CompilerParams(
            collective_id=0, has_side_effects=True, vmem_limit_bytes=62 * 2**20
        ),
        name="layer",
    )(*named.values())


def unpack_kernel(
    count,
    layer_hbm,
    frames_hbm,
    conv_hbm,
    ffn_hbm,
    attn_hbm,
    small_hbm,
    layer_out,
    frames_out,
    conv_out,
    conv_bias,
    qkv_out,
    qv_bias,
    out_out,
    out_bias,
    gain_one,
    shift_one,
    in_out,
    in_bias,
    back_out,
    back_bias,
    gain_two,
    shift_two,
    conv_wide,
    qkv_wide,
    out_wide,
    in_wide,
    back_wide,
    conv_ref,
    ffn_ref,
    attn_ref,
    small_ref,
    layer_ref,
    frames_ref,
    spare,
    sems,
):
    f32 = jnp.float32
    me = lax.axis_index("blk")
    rows_count, channels, width = attn_ref.shape
    piece = conv_ref.shape[1]
    copies = []

    def start(source, target):
        copy = pltpu.make_async_copy(source, target, sems.at[len(copies)])
        copy.start()
        copies.append(copy)

    loads = [
        pltpu.make_async_copy(source, target, sems.at[6 + rows_count + i])
        for i, (source, target) in enumerate(
            (
                (conv_hbm, conv_ref),
                (ffn_hbm, ffn_ref),
                (attn_hbm, attn_ref),
                (small_hbm, small_ref),
                (layer_hbm, layer_ref),
                (frames_hbm, frames_ref),
            )
        )
    ]
    for load in loads:
        load.start()
    loads[0].wait()
    for row in range(rows_count):
        part = slice(row * piece, (row + 1) * piece)
        conv_wide[part] = conv_ref[row].astype(f32)
        start(conv_wide.at[part], conv_out.at[part])
    loads[1].wait()
    loads[2].wait()
    for row in range(rows_count):
        part = slice(row * channels, (row + 1) * channels)
        span = slice(row * width, (row + 1) * width)
        in_wide[:, span] = ffn_ref[row, 0].astype(f32)
        back_wide[part, :] = ffn_ref[row, 1].astype(f32)
        if row < rows_count - 1:
            qkv_wide[:, span] = attn_ref[row].astype(f32)
        else:
            out_wide[...] = attn_ref[row].astype(f32)
    start(in_wide, in_out)
    start(back_wide, back_out)
    start(qkv_wide, qkv_out)
    start(out_wide, out_out)
    loads[4].wait()
    start(layer_ref, layer_out)
    loads[5].wait()
    start(frames_ref, frames_out)
    loads[3].wait()
    small = small_ref[...]
    own = pltpu.roll(small, lax.rem(width - channels * me, width), 1)
    for place, ref in (
        (0, conv_bias),
        (3, out_bias),
        (4, gain_one),
        (5, shift_one),
        (10, back_bias),
        (11, gain_two),
        (12, shift_two),
    ):
        ref[...] = own[place, :channels]
    for first, parts, ref in ((1, 2, qv_bias), (6, rows_count, in_bias)):
        size = parts * channels
        inside = count // parts
        spare[...] = pltpu.roll(small, lax.rem(width - size * lax.rem(me, inside), width), 1)
        ref[...] = spare[pl.ds(first + me // inside, 1), :][0, :size]
    for copy in copies:
        copy.wait()


def unpack(count, layer_out, frames_out, conv, ffn, attn, small):
    rows_count, channels, width = attn.shape
    piece, group_width, kernel = conv.shape[1:]
    f32 = jnp.float32
    hbm = pl.BlockSpec(memory_space=pl.ANY)
    vector = jax.ShapeDtypeStruct((channels,), f32)
    conv_type = jax.ShapeDtypeStruct((rows_count * piece, group_width, kernel), f32)
    qkv_type = jax.ShapeDtypeStruct((channels, (rows_count - 1) * width), f32)
    out_type = jax.ShapeDtypeStruct((channels, width), f32)
    in_type = jax.ShapeDtypeStruct((channels, rows_count * width), f32)
    back_type = jax.ShapeDtypeStruct((rows_count * channels, width), f32)
    results = pl.pallas_call(
        functools.partial(unpack_kernel, count),
        out_shape=(
            jax.ShapeDtypeStruct(layer_out.shape, layer_out.dtype),
            jax.ShapeDtypeStruct(frames_out.shape, frames_out.dtype),
            conv_type,
            vector,
            qkv_type,
            jax.ShapeDtypeStruct((2 * channels,), f32),
            out_type,
            vector,
            vector,
            vector,
            in_type,
            jax.ShapeDtypeStruct((rows_count * channels,), f32),
            back_type,
            vector,
            vector,
            vector,
        ),
        in_specs=[hbm] * 6,
        out_specs=(
            hbm,
            hbm,
            hbm,
            VMEM,
            hbm,
            VMEM,
            hbm,
            VMEM,
            VMEM,
            VMEM,
            hbm,
            VMEM,
            hbm,
            VMEM,
            VMEM,
            VMEM,
        ),
        scratch_shapes=[
            pltpu.VMEM(item.shape, f32)
            for item in (conv_type, qkv_type, out_type, in_type, back_type)
        ]
        + [pltpu.VMEM(item.shape, item.dtype) for item in (conv, ffn, attn, small, layer_out, frames_out)]
        + [pltpu.VMEM(small.shape, f32), pltpu.SemaphoreType.DMA((12 + rows_count,))],
        compiler_params=pltpu.CompilerParams(vmem_limit_bytes=62 * 2**20),
        name="unpack",
    )(layer_out, frames_out, conv, ffn, attn, small)
    return (results[0][None], results[1][None], *results[2:])


def shards(sizes, *arrays):
    frames, segment, conv_weight = arrays[:3]
    row_count, block_len, model_width = frames.shape
    group_width, kernel = conv_weight.shape[1:]
    count = sizes["blk"]
    head_dim = model_width // HEADS
    channels = model_width // count
    fits = (
        row_count == 1
        and block_len == LANES
        and kernel == LANES
        and channels % group_width == 0
        and group_width % TAP_STEP == 0
        and count % 4 == 0
        and 2 * HEADS == 3 * count
        and head_dim % TAP_STEP == 0
        and sizes["dp"] == 4
        and count % sizes["dp"] == 0
        and arrays[10].shape[1] == 4 * model_width
    )
    if fits:
        return swap_shards(count, sizes["dp"], *arrays)
    return ring_shards(*arrays)


def swap_shards(
    count,
    rows_count,
    frames,
    segment,
    conv_weight,
    conv_bias,
    qkv_weight,
    qv_bias,
    out_weight,
    out_bias,
    norm1_gain,
    norm1_bias,
    ffn_in,
    ffn_in_bias,
    ffn_out,
    ffn_out_bias,
    norm2_gain,
    norm2_bias,
    cotangent,
):
    named = {
        "frames": frames[0],
        "segment": segment,
        "cotangent": cotangent[0],
        "conv_bias": conv_bias,
        "qv_bias": qv_bias,
        "out_bias": out_bias,
        "gain_one": norm1_gain,
        "shift_one": norm1_bias,
        "in_bias": ffn_in_bias,
        "back_bias": ffn_out_bias,
        "gain_two": norm2_gain,
        "shift_two": norm2_bias,
        "conv_hbm": conv_weight,
        "qkv_hbm": qkv_weight,
        "out_hbm": out_weight,
        "in_hbm": ffn_in,
        "back_hbm": ffn_out,
    }
    width = frames.shape[2]
    results = layer(count, rows_count, width // HEADS, named)
    return unpack(count, *results)


def solution(mesh):
    return jax.shard_map(
        functools.partial(shards, mesh.shape),
        mesh=mesh,
        in_specs=(
            P("dp", "blk", None),
            P("dp", "blk"),
            P(),
            P(),
            P(),
            P(),
            P(),
            P(),
            P(),
            P(),
            P(),
            P(),
            P(),
            P(),
            P(),
            P(),
            P("dp", "blk", None),
        ),
        out_specs=(
            P("dp", "blk", None),
            P("dp", "blk", None),
            P("blk", None, None),
            P("blk"),
            P("blk", None),
            P("blk"),
            P("blk", None),
            P("blk"),
            P("blk"),
            P("blk"),
            P("blk", None),
            P("blk"),
            P("blk", None),
            P("blk"),
            P("blk"),
            P("blk"),
        ),
        check_vma=False,
    )
```

```python
import functools
import math
import types

import jax
import jax.numpy as jnp
from jax import lax
from jax.experimental import pallas as pl
from jax.experimental.pallas import tpu as pltpu
from jax.sharding import PartitionSpec as P

HEADS = 12
GROUPS = 16


EPS = 1e-05
ROOT_HALF = 0.7071067811865476
DENSITY_CONST = 0.3989422804014327


def with_halo(x, sides, width):
    for axis, dim in sides:
        size, length = (lax.axis_size(axis), x.shape[dim])
        up = [(i, (i + 1) % size) for i in range(size - 1)]
        down = [(j, i) for i, j in up]
        last = lax.slice_in_dim(x, length - width, length, axis=dim)
        initial = lax.slice_in_dim(x, 0, width, axis=dim)
        before = lax.ppermute(last, axis, up)
        after = lax.ppermute(initial, axis, down)
        x = jnp.concatenate([before, x, after], axis=dim)
    return x


def from_behind(value, axis, steps):
    count = lax.axis_size(axis)
    pairs = [(source, (source + steps) % count) for source in range(count)]
    return lax.ppermute(value, axis, pairs)


def gelu_value(signal):
    return 0.5 * signal * (1.0 + lax.erf(signal * ROOT_HALF))


def gelu_slope(signal):
    return (
        0.5 * (1.0 + lax.erf(signal * ROOT_HALF))
        + signal * jnp.exp(-0.5 * signal * signal) * DENSITY_CONST
    )


def norm_forward(signal, gain_vec, shift_vec):
    average = jnp.mean(signal, axis=-1, keepdims=True)
    centred = signal - average
    inv_std = lax.rsqrt(jnp.mean(centred * centred, axis=-1, keepdims=True) + EPS)
    normed = centred * inv_std
    return (normed * gain_vec + shift_vec, normed, inv_std)


def norm_backward(grad_in, normed, inv_std, gain_vec):
    scaled = grad_in * gain_vec
    result = inv_std * (
        scaled
        - jnp.mean(scaled, axis=-1, keepdims=True)
        - normed * jnp.mean(scaled * normed, axis=-1, keepdims=True)
    )
    return (result, jnp.sum(grad_in * normed, axis=0), jnp.sum(grad_in, axis=0))


def block_grads(
    query_h, dout_h, query_seg, log_tot, row_delta, key_h, value_h, key_seg, score_scale
):
    scores = (
        jnp.einsum("rqhc,rkhc->rhqk", query_h, key_h, preferred_element_type=jnp.float32)
        * score_scale
    )
    same_seg = (query_seg[:, :, None] == key_seg[:, None, :])[:, None]
    weights_f = jnp.where(same_seg, jnp.exp(scores - log_tot[..., None]), 0.0)
    grad_prob = jnp.einsum("rqhc,rkhc->rhqk", dout_h, value_h, preferred_element_type=jnp.float32)
    grad_score = (weights_f * (grad_prob - row_delta[..., None])).astype(jnp.bfloat16)
    query_part = score_scale * jnp.einsum(
        "rhqk,rkhc->rqhc", grad_score, key_h, preferred_element_type=jnp.float32
    )
    key_part = score_scale * jnp.einsum(
        "rhqk,rqhc->rkhc", grad_score, query_h, preferred_element_type=jnp.float32
    )
    value_part = jnp.einsum(
        "rhqk,rqhc->rkhc",
        weights_f.astype(jnp.bfloat16),
        dout_h,
        preferred_element_type=jnp.float32,
    )
    return (query_part, key_part, value_part)


def ring_shards(
    frames,
    segment,
    conv_weight,
    conv_bias,
    qkv_weight,
    qv_bias,
    out_weight,
    out_bias,
    norm1_gain,
    norm1_bias,
    ffn_in,
    ffn_in_bias,
    ffn_out,
    ffn_out_bias,
    norm2_gain,
    norm2_bias,
    cotangent,
):
    row_count, block_len, model_width = frames.shape
    token_count = row_count * block_len
    group_width = conv_weight.shape[1]
    kernel = conv_weight.shape[2]
    half_kernel = kernel // 2
    head_dim = model_width // HEADS
    score_scale = head_dim ** (-0.5)
    cycle_len = lax.axis_size("blk")
    is_valid = segment >= 0
    masked = jnp.where(is_valid[..., None], frames, jnp.zeros_like(frames))
    padded = with_halo(masked, (("blk", 1),), half_kernel)
    conv_out = lax.conv_general_dilated(
        padded,
        conv_weight,
        (1,),
        "VALID",
        dimension_numbers=("NWC", "OIW", "NWC"),
        feature_group_count=GROUPS,
        preferred_element_type=jnp.float32,
    )
    pre_conv = conv_out[:, :block_len].reshape(token_count, model_width) + conv_bias.astype(
        jnp.float32
    )
    mixed_in = frames.reshape(token_count, model_width).astype(jnp.float32) + gelu_value(pre_conv)
    mixed_low = mixed_in.astype(jnp.bfloat16)
    pair_bias = qv_bias.astype(jnp.float32)
    zero_bias = jnp.zeros((model_width,), jnp.float32)
    full_bias = jnp.concatenate([pair_bias[:model_width], zero_bias, pair_bias[model_width:]])
    project = (
        jnp.dot(mixed_low, qkv_weight, preferred_element_type=jnp.float32) + full_bias
    ).astype(jnp.bfloat16)
    project = project.reshape(row_count, block_len, 3 * model_width)
    query_heads = project[..., :model_width].reshape(row_count, block_len, HEADS, head_dim)
    keys_local = project[..., model_width : 2 * model_width]
    values_local = project[..., 2 * model_width :]
    key_heads = keys_local.reshape(row_count, block_len, HEADS, head_dim)
    value_heads = values_local.reshape(row_count, block_len, HEADS, head_dim)
    query_seg = segment.astype(jnp.bfloat16)
    start_carry = (
        jnp.full((row_count, HEADS, block_len), -1e30, jnp.float32),
        jnp.zeros((row_count, HEADS, block_len), jnp.float32),
        jnp.zeros((row_count, HEADS, block_len, head_dim), jnp.float32),
    )
    key_piece = lax.all_gather(keys_local, "blk", axis=1, tiled=True)
    value_piece = lax.all_gather(values_local, "blk", axis=1, tiled=True)
    seg_piece = lax.all_gather(query_seg, "blk", axis=1, tiled=True)
    piece_len = key_piece.shape[1]
    block_size = math.gcd(piece_len, 512)

    def one_block(block_index, inner_carry):
        running_max, denominator, numerator = inner_carry
        offset = block_index * block_size
        key_block = lax.dynamic_slice_in_dim(key_piece, offset, block_size, 1).reshape(
            row_count, block_size, HEADS, head_dim
        )
        value_block = lax.dynamic_slice_in_dim(value_piece, offset, block_size, 1).reshape(
            row_count, block_size, HEADS, head_dim
        )
        seg_block = lax.dynamic_slice_in_dim(seg_piece, offset, block_size, 1)
        scores = (
            jnp.einsum(
                "rqhc,rkhc->rhqk", query_heads, key_block, preferred_element_type=jnp.float32
            )
            * score_scale
        )
        same_seg = (query_seg[:, :, None] == seg_block[:, None, :])[:, None]
        masked_scores = jnp.where(same_seg, scores, -1e30)
        new_max = jnp.maximum(running_max, jnp.max(masked_scores, axis=-1))
        weights_f = jnp.where(same_seg, jnp.exp(masked_scores - new_max[..., None]), 0.0)
        rescale = jnp.exp(running_max - new_max)
        denominator = denominator * rescale + jnp.sum(weights_f, axis=-1)
        numerator = numerator * rescale[..., None] + jnp.einsum(
            "rhqk,rkhc->rhqc",
            weights_f.astype(jnp.bfloat16),
            value_block,
            preferred_element_type=jnp.float32,
        )
        return (new_max, denominator, numerator)

    running_max, denominator, numerator = lax.fori_loop(
        0, piece_len // block_size, one_block, start_carry
    )
    log_total = running_max + jnp.log(denominator)
    attended_heads = (numerator / denominator[..., None]).transpose(0, 2, 1, 3)
    attended = attended_heads.reshape(token_count, model_width)
    attn_low = attended.astype(jnp.bfloat16)
    branch = jnp.dot(attn_low, out_weight, preferred_element_type=jnp.float32) + out_bias.astype(
        jnp.float32
    )
    gain_one = norm1_gain.astype(jnp.float32)
    hidden_norm, normed_one, inv_one = norm_forward(
        mixed_in + branch, gain_one, norm1_bias.astype(jnp.float32)
    )
    hidden_low = hidden_norm.astype(jnp.bfloat16)
    ffn_pre = jnp.dot(hidden_low, ffn_in, preferred_element_type=jnp.float32) + ffn_in_bias.astype(
        jnp.float32
    )
    ffn_act = gelu_value(ffn_pre).astype(jnp.bfloat16)
    ffn_branch = jnp.dot(
        ffn_act, ffn_out, preferred_element_type=jnp.float32
    ) + ffn_out_bias.astype(jnp.float32)
    gain_two = norm2_gain.astype(jnp.float32)
    layer_out, normed_two, inv_two = norm_forward(
        hidden_norm + ffn_branch, gain_two, norm2_bias.astype(jnp.float32)
    )
    grad_top = cotangent.reshape(token_count, model_width).astype(jnp.float32)
    grad_second, norm2_gain_grad, norm2_bias_grad = norm_backward(
        grad_top, normed_two, inv_two, gain_two
    )
    grad_branch_two = grad_second.astype(jnp.bfloat16)
    ffn_out_grad = jnp.einsum(
        "nf,nd->fd", ffn_act, grad_branch_two, preferred_element_type=jnp.float32
    )
    ffn_out_bias_grad = jnp.sum(grad_branch_two.astype(jnp.float32), axis=0)
    grad_act = jnp.einsum("nd,fd->nf", grad_branch_two, ffn_out, preferred_element_type=jnp.float32)
    grad_pre = (grad_act * gelu_slope(ffn_pre)).astype(jnp.bfloat16)
    ffn_in_grad = jnp.einsum("nd,nf->df", hidden_low, grad_pre, preferred_element_type=jnp.float32)
    ffn_in_bias_grad = jnp.sum(grad_pre.astype(jnp.float32), axis=0)
    grad_hidden = grad_second + jnp.einsum(
        "nf,df->nd", grad_pre, ffn_in, preferred_element_type=jnp.float32
    )
    grad_first, norm1_gain_grad, norm1_bias_grad = norm_backward(
        grad_hidden, normed_one, inv_one, gain_one
    )
    grad_branch = grad_first.astype(jnp.bfloat16)
    out_weight_grad = jnp.einsum(
        "ne,nd->ed", attn_low, grad_branch, preferred_element_type=jnp.float32
    )
    out_bias_grad = jnp.sum(grad_branch.astype(jnp.float32), axis=0)
    grad_att = jnp.einsum("nd,ed->ne", grad_branch, out_weight, preferred_element_type=jnp.float32)
    grad_heads = grad_att.astype(jnp.bfloat16).reshape(row_count, block_len, HEADS, head_dim)
    row_delta = jnp.einsum("rqhc,rqhc->rhq", grad_heads.astype(jnp.float32), attended_heads)
    zero_heads = jnp.zeros((row_count, block_len, HEADS, head_dim), jnp.float32)

    def key_step(carried):
        key_block, value_block, seg_block, key_grad, value_grad, query_grad = carried
        query_part, key_part, value_part = block_grads(
            query_heads,
            grad_heads,
            query_seg,
            log_total,
            row_delta,
            key_block,
            value_block,
            seg_block,
            score_scale,
        )
        query_grad = query_grad + query_part
        key_grad = key_grad + key_part
        value_grad = value_grad + value_part
        key_block, value_block, seg_block = from_behind(
            (key_block, value_block, seg_block), "blk", 1
        )
        key_grad, value_grad = (
            from_behind(key_grad.astype(jnp.bfloat16), "blk", 1).astype(key_grad.dtype),
            from_behind(value_grad.astype(jnp.bfloat16), "blk", 1).astype(value_grad.dtype),
        )
        return (key_block, value_block, seg_block, key_grad, value_grad, query_grad)

    def four_steps(turn_index, carried):
        for repeat in range(4):
            carried = key_step(carried)
        return carried

    final_state = lax.fori_loop(
        0,
        cycle_len // 4,
        four_steps,
        (key_heads, value_heads, query_seg, zero_heads, zero_heads, zero_heads),
    )
    key_grad, value_grad, query_grad = (final_state[3], final_state[4], final_state[5])
    grad_project = jnp.concatenate(
        [
            query_grad.reshape(token_count, model_width),
            key_grad.reshape(token_count, model_width),
            value_grad.reshape(token_count, model_width),
        ],
        axis=1,
    ).astype(jnp.bfloat16)
    qkv_weight_grad = jnp.einsum(
        "nd,ne->de", mixed_low, grad_project, preferred_element_type=jnp.float32
    )
    bias_sums = jnp.sum(grad_project.astype(jnp.float32), axis=0)
    qv_bias_grad = jnp.concatenate([bias_sums[:model_width], bias_sums[2 * model_width :]])
    grad_mixed = grad_first + jnp.einsum(
        "ne,de->nd", grad_project, qkv_weight, preferred_element_type=jnp.float32
    )
    grad_conv = (grad_mixed * gelu_slope(pre_conv)).astype(jnp.bfloat16)
    conv_bias_grad = jnp.sum(grad_conv.astype(jnp.float32), axis=0)
    grad_conv_rows = grad_conv.reshape(row_count, block_len, model_width)
    grad_padded = with_halo(grad_conv_rows, (("blk", 1),), half_kernel)
    flipped = conv_weight.reshape(GROUPS, group_width, group_width, kernel).transpose(0, 2, 1, 3)
    flipped = flipped.reshape(model_width, group_width, kernel)[:, :, ::-1]
    back_conv = lax.conv_general_dilated(
        grad_padded,
        flipped,
        (1,),
        "VALID",
        dimension_numbers=("NWC", "OIW", "NWC"),
        feature_group_count=GROUPS,
        preferred_element_type=jnp.float32,
    )[:, 1:]
    frames_grad = (
        grad_mixed.reshape(row_count, block_len, model_width)
        + jnp.where(is_valid[..., None], back_conv, 0.0)
    ).astype(jnp.bfloat16)
    conv_weight_grad = lax.conv_general_dilated(
        padded,
        grad_conv_rows,
        (1,),
        "VALID",
        dimension_numbers=("CWN", "IWO", "CNW"),
        batch_group_count=GROUPS,
        preferred_element_type=jnp.float32,
    )[:, :, :kernel]
    (
        conv_weight_part,
        conv_bias_part,
        qkv_weight_part,
        qv_bias_part,
        out_weight_part,
        out_bias_part,
        gain_one_part,
        shift_one_part,
        ffn_in_part,
        ffn_in_bias_part,
        ffn_out_part,
        ffn_out_bias_part,
        gain_two_part,
        shift_two_part,
    ) = (
        lax.psum_scatter(conv_weight_grad, "blk", scatter_dimension=0, tiled=True),
        lax.psum_scatter(conv_bias_grad, "blk", scatter_dimension=0, tiled=True),
        lax.psum_scatter(qkv_weight_grad, "blk", scatter_dimension=0, tiled=True),
        lax.psum_scatter(qv_bias_grad, "blk", scatter_dimension=0, tiled=True),
        lax.psum_scatter(out_weight_grad, "blk", scatter_dimension=0, tiled=True),
        lax.psum_scatter(out_bias_grad, "blk", scatter_dimension=0, tiled=True),
        lax.psum_scatter(norm1_gain_grad, "blk", scatter_dimension=0, tiled=True),
        lax.psum_scatter(norm1_bias_grad, "blk", scatter_dimension=0, tiled=True),
        lax.psum_scatter(ffn_in_grad, "blk", scatter_dimension=0, tiled=True),
        lax.psum_scatter(ffn_in_bias_grad, "blk", scatter_dimension=0, tiled=True),
        lax.psum_scatter(ffn_out_grad, "blk", scatter_dimension=0, tiled=True),
        lax.psum_scatter(ffn_out_bias_grad, "blk", scatter_dimension=0, tiled=True),
        lax.psum_scatter(norm2_gain_grad, "blk", scatter_dimension=0, tiled=True),
        lax.psum_scatter(norm2_bias_grad, "blk", scatter_dimension=0, tiled=True),
    )
    totals = (
        lax.psum(conv_weight_part.astype(jnp.bfloat16), "dp").astype(jnp.float32),
        lax.psum(conv_bias_part.astype(jnp.bfloat16), "dp").astype(jnp.float32),
        lax.psum(qkv_weight_part.astype(jnp.bfloat16), "dp").astype(jnp.float32),
        lax.psum(qv_bias_part.astype(jnp.bfloat16), "dp").astype(jnp.float32),
        lax.psum(out_weight_part.astype(jnp.bfloat16), "dp").astype(jnp.float32),
        lax.psum(out_bias_part.astype(jnp.bfloat16), "dp").astype(jnp.float32),
        lax.psum(gain_one_part.astype(jnp.bfloat16), "dp").astype(jnp.float32),
        lax.psum(shift_one_part.astype(jnp.bfloat16), "dp").astype(jnp.float32),
        lax.psum(ffn_in_part.astype(jnp.bfloat16), "dp").astype(jnp.float32),
        lax.psum(ffn_in_bias_part.astype(jnp.bfloat16), "dp").astype(jnp.float32),
        lax.psum(ffn_out_part.astype(jnp.bfloat16), "dp").astype(jnp.float32),
        lax.psum(ffn_out_bias_part.astype(jnp.bfloat16), "dp").astype(jnp.float32),
        lax.psum(gain_two_part.astype(jnp.bfloat16), "dp").astype(jnp.float32),
        lax.psum(shift_two_part.astype(jnp.bfloat16), "dp").astype(jnp.float32),
    )
    return (
        layer_out.reshape(row_count, block_len, model_width).astype(jnp.bfloat16),
        frames_grad,
        totals[0],
        totals[1],
        totals[2],
        totals[3],
        totals[4],
        totals[5],
        totals[6],
        totals[7],
        totals[8],
        totals[9],
        totals[10],
        totals[11],
        totals[12],
        totals[13],
    )


MESH = pl.DeviceIdType.MESH
LANES = 128
TAP_STEP = 16
VMEM = pl.BlockSpec(memory_space=pltpu.VMEM)


def peer(me, step, count):
    return lax.rem(me + step, count)


def greet(index, count, rows):
    barrier = pltpu.get_barrier_semaphore()
    for step in range(1, count * rows):
        other = lax.rem(index + step, count * rows)
        pl.semaphore_signal(
            barrier,
            inc=1,
            device_id={"dp": other // count, "blk": lax.rem(other, count)},
            device_id_type=MESH,
        )


def greet_wait(count, rows):
    pl.semaphore_wait(pltpu.get_barrier_semaphore(), count * rows - 1)


def remote(src, dst, send_sem, recv_sem, target, axis="blk"):
    copy = pltpu.make_async_remote_copy(
        src_ref=src,
        dst_ref=dst,
        send_sem=send_sem,
        recv_sem=recv_sem,
        device_id=target if isinstance(target, dict) else {axis: target},
        device_id_type=MESH,
    )
    copy.start()
    return copy


def turned(value):
    return value.astype(jnp.float32).T.astype(jnp.bfloat16)


def matmul_turned(left, right):
    return lax.dot_general(
        left, right, (((1,), (1,)), ((), ())), preferred_element_type=jnp.float32
    )


def sum_parts(parts_ref):
    total = parts_ref[0].astype(jnp.float32)
    for part in range(1, parts_ref.shape[0]):
        total = total + parts_ref[part].astype(jnp.float32)
    return total


def lane_block(index):
    return pl.ds(pl.multiple_of(index * LANES, LANES), LANES)


def row_block(index, size):
    return pl.ds(pl.multiple_of(index * size, size), size)


def swap_blocks(tiles, width):
    count = len(tiles)
    lane = lax.broadcasted_iota(jnp.int32, tiles[0].shape, 1) // width
    tiles = list(tiles)
    step = count // 2
    while step:
        low = (lane & step) == 0
        for u in range(count):
            if u & step == 0:
                one, two = tiles[u], tiles[u + step]
                tiles[u] = jnp.where(low, one, pltpu.roll(two, step * width, 1))
                tiles[u + step] = jnp.where(low, pltpu.roll(one, LANES - step * width, 1), two)
        step //= 2
    return tiles


def spread_taps(source, offset, direction, stage_ref, out_ref):
    rows, length = source.shape
    blocks = out_ref.shape[1] // LANES
    for tap in range(TAP_STEP):
        shift = (length - offset - direction * tap) % length
        moved = pltpu.roll(source, shift, 1)
        for block in range(blocks):
            first = block * rows * TAP_STEP + tap
            stage_ref[pl.ds(first, rows, stride=TAP_STEP), :] = moved[
                :, block * LANES : (block + 1) * LANES
            ]
    size = rows * TAP_STEP
    for block in range(blocks):
        out_ref[:, block * LANES : (block + 1) * LANES] = stage_ref[
            block * size : (block + 1) * size, :
        ].astype(jnp.bfloat16)


def query_span(index, size):
    return pl.ds(pl.multiple_of(index * size, size), size)


def same_clip(column_ref, seg_row):
    column = column_ref[...]
    parts = [
        column == seg_row[:, start : start + LANES]
        for start in range(0, seg_row.shape[1], LANES)
    ]
    return jnp.concatenate(parts, axis=1)


def clip_column(count, segs_ref, column_ref):
    for block in range(count):
        row = segs_ref[block].astype(jnp.float32)
        column_ref[block * LANES : (block + 1) * LANES, :] = jnp.broadcast_to(
            row, (LANES, LANES)
        ).T


def clip_row(segs_ref, first, size):
    parts = [segs_ref[first + i].astype(jnp.float32) for i in range(size // LANES)]
    return jnp.concatenate(parts, axis=1)


def layer_kernel(names, count, rows_count, head_dim, *refs):
    R = types.SimpleNamespace(**dict(zip(names, refs)))
    low, f32 = jnp.bfloat16, jnp.float32
    me, row = lax.axis_index("blk"), lax.axis_index("dp")
    level, side = me // 2, lax.rem(me, 2)
    levels = count // 2
    half = count // 2
    near = me + 1 - 2 * side
    core = lax.rem(row, 2)
    twin = row + 1 - 2 * core
    upper = level // 2
    pos = 4 * core + 2 * lax.rem(level, 2) + side
    home_row = 2 * (row // 2) + upper
    at_home = core == upper
    east = row // 2
    corner = 2 * side + core
    facing = peer(corner, 2, 4)
    across = peer(row, 2, rows_count)
    tokens, width = R.frames.shape
    channels = width // count
    length = count * LANES
    group_width = R.own_weight.shape[1]
    groups = channels // group_width
    steps = LANES // TAP_STEP
    scale = head_dim ** (-0.5)
    chunks = R.in_hbm.shape[1] // width

    def send(kind, step, source, target_ref, target, axis="blk"):
        return remote(
            source, target_ref, R.out_sem.at[kind, step], R.in_sem.at[kind, step], target, axis
        )

    def wait(copies):
        for copy in copies:
            copy.wait()

    def to_blocks(kind, source, target_ref):
        copies = []
        for step in range(1, count):
            target = peer(me, step, count)
            copies.append(send(kind, step, source(target), target_ref, target))
        return copies

    def device_at(place, part):
        return {"dp": 2 * (row // 2) + place // 4, "blk": 4 * part + lax.rem(place, 4)}

    def to_places(kind, source, target_ref):
        copies = []
        for step in range(1, count):
            target = peer(pos, step, count)
            copies.append(send(kind, step, source(target), target_ref, device_at(target, upper)))
        return copies

    def move(kind, source, target_ref, device):
        copy = pltpu.make_async_remote_copy(
            src_ref=source,
            dst_ref=target_ref,
            send_sem=R.out_sem.at[kind, 0],
            recv_sem=R.in_sem.at[kind, 0],
            device_id=device,
            device_id_type=MESH,
        )
        away = jnp.logical_not(at_home)
        pl.when(away)(copy.start)

        @pl.when(at_home)
        def _():
            target_ref[...] = source[...]

        return [(away, away, copy)]

    def shift_all(kind, first, own, device_of, source, target_ref):
        pending = []
        for step in range(count):
            target = peer(first, step, count)
            away = jnp.logical_not(jnp.logical_and(at_home, target == own))
            copy = pltpu.make_async_remote_copy(
                src_ref=source(target),
                dst_ref=target_ref,
                send_sem=R.out_sem.at[kind, step],
                recv_sem=R.in_sem.at[kind, step],
                device_id=device_of(target),
                device_id_type=MESH,
            )
            pl.when(away)(copy.start)
            pending.append((away, away, copy))

        @pl.when(at_home)
        def _():
            target_ref[...] = source(own)[...]

        return pending

    def to_level(kind, source, target_ref):
        return shift_all(
            kind, me, pos, lambda place: device_at(place, core), source, target_ref
        )

    def from_level(kind, source, target_ref):
        return shift_all(
            kind, pos, me, lambda block: {"dp": home_row, "blk": block}, source, target_ref
        )

    def wait_some(pending):
        for sends, comes, copy in pending:
            pl.when(sends)(copy.wait_send)
            pl.when(comes)(copy.wait_recv)

    def chunk_of(index):
        return slice(index * width, (index + 1) * width)

    def table(index):
        return R.table[index : index + 1, :]

    def dot(left, right):
        return jnp.dot(left, right, preferred_element_type=f32)

    greet(row * count + me, count, rows_count)

    loads = [pltpu.make_async_copy(R.qkv_hbm, R.qkv_w, R.load_sem.at[0])]
    loads.append(pltpu.make_async_copy(R.out_hbm, R.out_w, R.load_sem.at[1]))
    for chunk in range(chunks):
        span = chunk_of(chunk)
        loads.append(
            pltpu.make_async_copy(
                R.in_hbm.at[:, span], R.in_w.at[:, span], R.load_sem.at[2 + 2 * chunk]
            )
        )
        loads.append(
            pltpu.make_async_copy(
                R.back_hbm.at[span], R.back_w.at[span], R.load_sem.at[3 + 2 * chunk]
            )
        )
    for load in loads:
        load.start()
    own_load = pltpu.make_async_copy(
        R.conv_hbm.at[row_block(me, channels)], R.own_weight, R.load_sem.at[2 + 2 * chunks]
    )
    own_load.start()
    valid = (R.segment[...] >= 0).astype(f32)
    R.turned[...] = (R.frames[...].astype(f32).T * valid).astype(low)
    to_level_device = device_at(me, core)
    from_level_device = {"dp": home_row, "blk": pos}

    R.table[...] = jnp.zeros_like(R.table)
    R.small[...] = jnp.zeros_like(R.small)
    place = 0
    for vector in VECTORS:
        ref = getattr(R, vector)
        for part in range(ref.shape[0] // width):
            R.table[place, :] = ref[chunk_of(part)].astype(f32)
            place += 1

    def mix_taps(mix, tile_rows):
        @pl.loop(0, group_width // steps)
        def _(block):
            for group in range(groups):
                tiles = [
                    R.stage[tile_rows(group, block * steps + u), :] for u in range(steps)
                ]
                for a, tile in enumerate(swap_blocks(tiles, TAP_STEP)):
                    rows = slice(a * group_width, (a + 1) * group_width)
                    mix[group, rows, lane_block(block)] = tile.astype(low)

    square = group_width * group_width
    own_load.wait()
    total_rows = channels * group_width
    R.stage[:total_rows, :] = R.own_weight[...].astype(f32).reshape(total_rows, LANES)
    mix_taps(R.mix, lambda g, i: pl.ds(g * square + i, group_width, stride=group_width))
    greet_wait(count, rows_count)

    copies = to_blocks(
        0, lambda p: R.turned.at[row_block(p, channels), :], R.column.at[:, lane_block(me + 1)]
    )
    brought = move(33, R.frames, R.frames_home, to_level_device)
    seg_pending = to_level(1, lambda p: R.segment, R.segs.at[me])
    R.column[:, lane_block(me + 1)] = R.turned[row_block(me, channels), :]
    for ref in (R.column, R.gcol):
        ref[:, :LANES] = jnp.zeros((channels, LANES), low)
        ref[:, length + LANES :] = jnp.zeros((channels, LANES), low)
    mix_taps(R.mix_back, lambda g, c: pl.ds(g * square + c * group_width, group_width))
    wait(copies)

    @pl.loop(0, groups)
    def _(group):
        rows = row_block(group, group_width)
        spread_taps(R.column[rows, :].astype(f32), LANES // 2, 1, R.stage, R.taps.at[group])
        product = dot(R.mix[group], R.taps[group])
        total = product[:group_width, :length]
        for a in range(1, steps):
            part = product[a * group_width : (a + 1) * group_width, :]
            part = pltpu.roll(part, product.shape[1] - a * TAP_STEP, 1)
            total = total + part[:, :length]
        R.result[rows, :] = total.astype(low)
    pending = to_level(
        2, lambda p: R.result.at[:, lane_block(p)], R.conv_home.at[row_block(me, channels), :]
    )
    @pl.loop(0, groups)
    def _(group):
        source = R.column[row_block(group, group_width), :].astype(f32)
        span = R.shifted.shape[2]
        for a in range(steps):
            moved = pltpu.roll(source, (span + LANES - a * TAP_STEP) % (span + LANES), 1)
            R.shifted[group, a * group_width : (a + 1) * group_width, :] = moved[:, :span].astype(
                low
            )
    wait_some(seg_pending)
    clip_column(count, R.segs, R.clip)
    wait_some(brought)
    wait_some(pending)
    brought = move(34, R.cotangent, R.cotangent_home, to_level_device)

    pre = R.conv_home[...].astype(f32).T + table(0)
    share = 0.5 * (1.0 + lax.erf(pre * ROOT_HALF))
    R.slope[...] = share + pre * jnp.exp(-0.5 * pre * pre) * DENSITY_CONST
    mixed = R.frames_home[...].astype(f32) + pre * share
    R.mixed[...] = mixed
    mixed_low = mixed.astype(low)
    loads[0].wait()
    for part in range(3):
        block = dot(mixed_low, R.qkv_w[:, chunk_of(part)])
        if part != 1:
            block = block + table(1 + part // 2)
        block = block.astype(low).astype(f32)
        if part == 0:
            block = block * scale
        R.project[part] = block.T.astype(low)
    extra_copies = to_places(
        4,
        lambda p: R.project.at[:, row_block(count + p // 2, head_dim), :],
        R.extra.at[:, :, lane_block(pos)],
    )
    copies = to_places(
        3,
        lambda p: R.project.at[:, row_block(p, head_dim), :],
        R.main.at[:, :, lane_block(pos)],
    )
    R.main[:, :, lane_block(pos)] = R.project[:, row_block(pos, head_dim), :]
    R.extra[:, :, lane_block(pos)] = R.project[:, row_block(count + pos // 2, head_dim), :]
    R.left[0] = turned(mixed_low)
    last_row = rows_count - 1

    def to_some_rows(kind, source, sends_to, comes_to):
        pending = []
        for step in range(1, rows_count):
            target = peer(row, step, rows_count)
            copy = pltpu.make_async_remote_copy(
                src_ref=source,
                dst_ref=R.late_left.at[:, lane_block(row)],
                send_sem=R.out_sem.at[kind, step],
                recv_sem=R.in_sem.at[kind, step],
                device_id={"dp": target},
                device_id_type=MESH,
            )
            sends = sends_to(target)
            pl.when(sends)(copy.start)
            pending.append((sends, comes_to, copy))
        return pending

    left_pending = to_some_rows(8, R.left.at[0], lambda p: p != last_row, row != last_row)
    wait(extra_copies)

    size = 2 * LANES
    halves = half * LANES // size

    def scores_of(held, start, seg_row):
        scores = lax.dot_general(
            held[1], held[0, :, start], (((0,), (0,)), ((), ())), preferred_element_type=f32
        )
        return jnp.where(same_clip(R.clip, seg_row), scores, -1e30)

    def attend(held, start, index, att_ref, low_ref, lse_ref, place):
        scores = scores_of(held, start, clip_row(R.segs, index * 2, size))
        top = jnp.max(scores, axis=0, keepdims=True)
        weights = jnp.exp(scores - top)
        total = jnp.sum(weights, axis=0, keepdims=True)
        mean = dot(held[2], weights.astype(low)) / total
        att_ref[:, place] = mean
        low_ref[:, start] = mean.astype(low)
        lse_ref[:, place] = top + jnp.log(total)

    own_rows = row_block(pos, head_dim)
    extra_rows = row_block(count + pos // 2, head_dim)

    def to_half(kind, source, target_ref):
        pending = []
        for step in range(1, count):
            target, origin = peer(pos, step, count), peer(pos, count - step, count)
            copy = pltpu.make_async_remote_copy(
                src_ref=source(target),
                dst_ref=target_ref,
                send_sem=R.out_sem.at[kind, step],
                recv_sem=R.in_sem.at[kind, step],
                device_id=device_at(target, upper),
                device_id_type=MESH,
            )
            sends, comes = target // half == side, pos // half == lax.rem(origin, 2)
            pl.when(sends)(copy.start)
            pending.append((sends, comes, copy))
        return pending

    @pl.loop(0, halves)
    def _(block):
        index = side * halves + block
        place = query_span(block, size)
        attend(
            R.extra,
            query_span(index, size),
            index,
            R.att_extra,
            R.low_extra,
            R.lse_extra,
            place,
        )
    pending = to_half(5, lambda p: R.low_extra.at[:, lane_block(p)], R.att_home.at[extra_rows, :])

    @pl.when(pos // half == side)
    def _():
        R.att_home[extra_rows, :] = R.low_extra[:, lane_block(pos)]

    wait(copies)

    @pl.loop(0, length // size)
    def _(block):
        span = query_span(block, size)
        attend(R.main, span, block, R.att_main, R.low_main, R.lse_main, span)

    copies = to_places(6, lambda p: R.low_main.at[:, lane_block(p)], R.att_home.at[own_rows, :])
    R.att_home[own_rows, :] = R.low_main[:, lane_block(pos)]
    wait(copies)
    wait_some(pending)

    def to_rows(kind, source, target_ref):
        return [
            send(kind, step, source(peer(row, step, rows_count)), target_ref, target, "dp")
            for step, target in ((n, peer(row, n, rows_count)) for n in range(1, rows_count))
        ]

    def share_start(kind, part, index=row, mate={"dp": across}):
        own = part(index)
        return [send(kind, 2, own, own, mate), send(kind, 1, own, own, twin, "dp")]

    def share_forward(kind, part, copies, index=across):
        copies[0].wait()
        got = part(index)
        copies[0] = send(kind, 3, got, got, twin, "dp")

    def lanes_of(ref):
        return lambda index: ref.at[:, lane_block(index)]

    R.left[1] = R.att_home[...]
    att = R.att_home[...].astype(f32).T.astype(low)
    loads[1].wait()
    branch = dot(att, R.out_w[...]) + table(3)
    hidden, normed_one, inv_one = norm_forward(R.mixed[...] + branch, table(4), table(5))
    hidden_low = hidden.astype(low)
    R.hidden_all[:, lane_block(corner)] = turned(hidden_low)
    hidden_copies = share_start(7, lanes_of(R.hidden_all), corner, {"blk": near})
    left_pending += to_some_rows(32, R.left.at[1], lambda p: p == last_row, row == last_row)
    R.late_left[:, lane_block(row)] = R.left[row // last_row]
    pieces = count // chunks
    for load in loads[2:]:
        load.wait()
    R.total[...] = hidden + table(10)

    @pl.loop(0, chunks)
    def _(chunk):
        span = query_span(chunk, width)
        pre = dot(hidden_low, R.in_w[:, span]) + R.table[pl.ds(6 + chunk, 1), :]
        share = 0.5 * (1.0 + lax.erf(pre * ROOT_HALF))
        act = (pre * share).astype(low)
        R.keep[:, span] = share + pre * jnp.exp(-0.5 * pre * pre) * DENSITY_CONST
        R.act_turned[pl.ds(chunk * pieces, pieces)] = turned(act).reshape(
            pieces, rows_count, -1, LANES
        )
        R.total[...] += dot(act, R.back_w[row_block(chunk, width), :])

    act_copies = to_rows(9, lambda p: R.act_turned.at[:, p], R.act_all.at[:, :, lane_block(row)])
    R.act_all[:, :, lane_block(row)] = R.act_turned[:, row]
    layer, normed_two, inv_two = norm_forward(R.total[...], table(11), table(12))
    R.layer_here[...] = layer.astype(low)
    layer_pending = move(35, R.layer_here, R.layer_got, from_level_device)
    wait_some(brought)
    grad_second, gain_sum, shift_sum = norm_backward(
        R.cotangent_home[...].astype(f32), normed_two, inv_two, table(11)
    )
    R.small[11, :] = gain_sum
    R.small[12, :] = shift_sum
    grad_two = grad_second.astype(low)
    R.two_all[:, lane_block(row)] = turned(grad_two)
    two_copies = share_start(10, lanes_of(R.two_all))
    R.small[10, :] = jnp.sum(grad_two.astype(f32), axis=0)
    R.total[...] = grad_second

    @pl.loop(0, chunks)
    def _(chunk):
        span = query_span(chunk, width)
        grad_pre = matmul_turned(grad_two, R.back_w[row_block(chunk, width), :]) * R.keep[:, span]
        grad_pre = grad_pre.astype(low)
        R.pre_turned[chunk] = turned(grad_pre)
        R.small[pl.ds(6 + chunk, 1), :] = jnp.sum(grad_pre.astype(f32), axis=0, keepdims=True)
        R.total[...] += matmul_turned(grad_pre, R.in_w[:, span])

    grad_first, gain_sum, shift_sum = norm_backward(R.total[...], normed_one, inv_one, table(4))
    R.small[4, :] = gain_sum
    R.small[5, :] = shift_sum
    R.mixed[...] = grad_first
    grad_branch = grad_first.astype(low)
    R.small[3, :] = jnp.sum(grad_branch.astype(f32), axis=0)
    R.turned[...] = turned(matmul_turned(grad_branch, R.out_w[...]).astype(low))

    extra_copies = to_places(
        12,
        lambda p: R.turned.at[row_block(count + p // 2, head_dim), :],
        R.gextra.at[:, lane_block(pos)],
    )
    copies = to_places(
        11, lambda p: R.turned.at[row_block(p, head_dim), :], R.gmain.at[:, lane_block(pos)]
    )
    R.gmain[:, lane_block(pos)] = R.turned[row_block(pos, head_dim), :]
    R.gextra[:, lane_block(pos)] = R.turned[row_block(count + pos // 2, head_dim), :]
    pre_copies = []
    for step in range(1, 4):
        target = peer(corner, step, 4)
        device = {"dp": 2 * east + lax.rem(target, 2), "blk": 2 * level + target // 2}
        pre_copies.append(
            send(13, step, R.pre_turned.at[target], R.pre_all.at[:, lane_block(corner)], device)
        )
    R.pre_all[:, lane_block(corner)] = R.pre_turned[corner]
    R.dproject[3] = turned(grad_branch)
    wait(extra_copies)

    def attend_back(held, grads, start, index, att, lse):
        queries = held[0, :, start]
        weights = jnp.exp(scores_of(held, start, clip_row(R.segs, index * 2, size)) - lse)
        grad_prob = lax.dot_general(
            held[2], grads, (((0,), (0,)), ((), ())), preferred_element_type=f32
        )
        delta = jnp.sum(grads.astype(f32) * att, axis=0, keepdims=True)
        grad_score = (weights * (grad_prob - delta)).astype(low)
        return (
            dot(held[1], grad_score) * scale,
            matmul_turned(queries, grad_score),
            matmul_turned(grads, weights.astype(low)),
        )

    R.dkey[...] = jnp.zeros_like(R.dkey)
    R.dvalue[...] = jnp.zeros_like(R.dvalue)

    @pl.loop(0, halves)
    def _(block):
        index = side * halves + block
        span = query_span(index, size)
        place = query_span(block, size)
        parts = attend_back(
            R.extra, R.gextra[:, span], span, index, R.att_extra[:, place], R.lse_extra[:, place]
        )
        R.dextra[0, :, span] = parts[0].astype(low)
        R.dkey[...] += parts[1]
        R.dvalue[...] += parts[2]

    R.dextra[1] = R.dkey[...].astype(low)
    R.dextra[2] = R.dvalue[...].astype(low)
    part_rows = row_block(pos // 2, head_dim)
    wait(copies)
    copies = to_places(
        14, lambda p: R.dextra.at[1:3, :, lane_block(p)], R.halves.at[side, :, part_rows, :]
    )
    pending = to_half(
        15, lambda p: R.dextra.at[0, :, lane_block(p)], R.dproject.at[0, extra_rows, :]
    )
    R.halves[side, :, part_rows, :] = R.dextra[1:3, :, lane_block(pos)]

    @pl.when(pos // half == side)
    def _():
        R.dproject[0, extra_rows, :] = R.dextra[0, :, lane_block(pos)]

    lower = lax.rem(level, 2)
    level_mate = me + 2 - 4 * lower
    upper_mate = me + 4 - 8 * upper

    modes = {
        "side": (side, {"blk": near}, lower, {"blk": level_mate}),
        "east": (east, {"dp": across}, lower, {"blk": level_mate}),
        "level": (lower, {"blk": level_mate}, side, {"blk": near}),
    }

    def shard(u, bit, other, mode):
        return row_block(4 * u + (2 * bit + other if mode == "level" else 2 * other + bit), channels)

    def sum_begin(kind, slot, source, span, mode):
        bit, mate, _, _ = modes[mode]
        return [
            send(
                kind,
                2 * u + v,
                R.in_w.at[shard(u, 1 - bit, v, mode), source],
                R.got_one.at[slot, 2 * u + v, :, span],
                mate,
            )
            for u in range(2)
            for v in range(2)
        ]

    def sum_next(kind, slot, source, span, mode, copies):
        wait(copies)
        bit, _, other, mate = modes[mode]
        for u in range(2):
            for v in range(2):
                own = R.in_w[shard(u, bit, v, mode), source]
                got = R.got_one[slot, 2 * u + v, :, span]
                R.sum_one[slot, 2 * u + v, :, span] = (own.astype(f32) + got.astype(f32)).astype(
                    low
                )
        return [
            send(
                kind,
                u,
                R.sum_one.at[slot, 2 * u + 1 - other, :, span],
                R.got_two.at[slot, u, :, span],
                mate,
            )
            for u in range(2)
        ]

    def sum_last(kind, slot, span, mode, copies):
        wait(copies)
        other = modes[mode][2]
        for u in range(2):
            own = R.sum_one[slot, 2 * u + other, :, span]
            got = R.got_two[slot, u, :, span]
            R.sum_two[slot, u, :, span] = (own.astype(f32) + got.astype(f32)).astype(low)
        return [
            send(
                kind,
                0,
                R.sum_two.at[slot, 1 - upper, :, span],
                R.got_three.at[slot, :, span],
                upper_mate,
            )
        ]

    def summed(slot, copies):
        wait(copies)
        return (R.sum_two[slot, upper].astype(f32) + R.got_three[slot].astype(f32)).astype(low)

    every = slice(0, width)
    in_span, out_span = chunk_of(0), chunk_of(1)
    stores = []

    def store(index, source, target):
        copy = pltpu.make_async_copy(source, target, R.store_sem.at[index])
        copy.start()
        stores.append(copy)

    share_forward(10, lanes_of(R.two_all), two_copies)
    share_forward(7, lanes_of(R.hidden_all), hidden_copies, facing)
    blocks = length // size

    def main_back(block):
        span = query_span(block, size)
        parts = attend_back(
            R.main, R.gmain[:, span], span, block, R.att_main[:, span], R.lse_main[:, span]
        )
        R.dmain[0, :, span] = parts[0].astype(low)
        for place in range(size // LANES):
            target = block * (size // LANES) + place
            pl.when(target != pos)(query_copy(target).start)
        R.dkey[...] += parts[1]
        R.dvalue[...] += parts[2]

    def query_copy(target):
        step = lax.rem(target - pos + count, count)
        return pltpu.make_async_remote_copy(
            src_ref=R.dmain.at[0, :, lane_block(target)],
            dst_ref=R.dproject.at[0, own_rows, :],
            send_sem=R.out_sem.at[16, step],
            recv_sem=R.in_sem.at[16, step],
            device_id=device_at(target, upper),
            device_id_type=MESH,
        )

    R.dkey[...] = jnp.zeros_like(R.dkey)
    R.dvalue[...] = jnp.zeros_like(R.dvalue)
    pl.loop(0, blocks // 2)(main_back)
    wait(two_copies)
    wait(act_copies)
    product = matmul_turned(R.act_all[...].reshape(width, -1), R.two_all[...])
    R.in_w[:, out_span] = product.astype(low)
    out_copies = sum_begin(18, 1, out_span, every, "level")
    wait(hidden_copies)
    wait(pre_copies)
    R.in_w[:, in_span] = matmul_turned(R.hidden_all[...], R.pre_all[...]).astype(low)
    in_copies = sum_begin(17, 0, in_span, every, "east")
    pl.loop(blocks // 2, blocks)(main_back)
    R.dmain[1] = R.dkey[...].astype(low)
    R.dmain[2] = R.dvalue[...].astype(low)
    copies += to_places(
        44, lambda p: R.dmain.at[1:3, :, lane_block(p)], R.dproject.at[1:3, own_rows, :]
    )
    copies += [query_copy(peer(pos, step, count)) for step in range(1, count)]
    R.dproject[0:3, own_rows, :] = R.dmain[:, :, lane_block(pos)]
    in_copies = sum_next(22, 0, in_span, every, "east", in_copies)
    wait(copies)
    wait_some(pending)
    first = half * head_dim
    for which in range(2):
        total = R.halves[0, which].astype(f32) + R.halves[1, which].astype(f32)
        R.dproject[1 + which, width - first :, :] = total.astype(low)

    late = to_rows(19, lambda p: R.dproject.at[p], R.late_right.at[:, lane_block(row)])
    R.late_right[:, lane_block(row)] = R.dproject[row]
    grad_mixed = R.mixed[...]
    for part in range(3):
        block = R.dproject[part].astype(f32).T
        if part != 1:
            R.small[1 + part // 2, :] = jnp.sum(block, axis=0)
        grad_mixed = grad_mixed + matmul_turned(block.astype(low), R.qkv_w[:, chunk_of(part)])
    R.mixed_here[...] = grad_mixed.astype(low)
    grad_conv = (grad_mixed * R.slope[...]).astype(low)
    R.conv_turned[...] = turned(grad_conv)
    conv_pending = from_level(
        20, lambda b: R.conv_turned.at[row_block(b, channels), :], R.gcol.at[:, lane_block(pos + 1)]
    )
    R.small[0, :] = jnp.sum(grad_conv.astype(f32), axis=0)
    small_copy = send(21, 0, R.small, R.small_got.at[0], twin, "dp")
    out_copies = sum_next(23, 1, out_span, every, "level", out_copies)
    in_copies = sum_last(38, 0, every, "east", in_copies)
    mixed_pending = move(36, R.mixed_here, R.mixed_got, from_level_device)
    wait_some(conv_pending)
    @pl.loop(0, groups)
    def _(group):
        rows = row_block(group, group_width)
        spread_taps(R.gcol[rows, :].astype(f32), LANES // 2, -1, R.stage, R.taps.at[group])
        product = dot(R.mix_back[group], R.taps[group])
        total = product[:group_width, LANES:]
        for a in range(1, steps):
            part = product[a * group_width : (a + 1) * group_width, :]
            total = total + pltpu.roll(part, a * TAP_STEP, 1)[:, LANES:]
        R.result[rows, :] = total.astype(low)
    back = to_blocks(
        24, lambda p: R.result.at[:, lane_block(p)], R.back_home.at[row_block(me, channels), :]
    )
    R.back_home[row_block(me, channels), :] = R.result[:, lane_block(me)]

    out_copies = sum_last(37, 1, every, "level", out_copies)

    wait(late)
    wait_some(left_pending)
    product = matmul_turned(R.late_left[...], R.late_right[...])
    R.in_w[:, chunk_of(2)] = product.astype(low)
    middle = width // 2
    parts = (
        (26, slice(2 * width, 2 * width + middle), slice(0, middle), "side"),
        (28, slice(2 * width + middle, 3 * width), slice(middle, width), "level"),
    )
    att_copies = [sum_begin(kind, 2, source, span, first) for kind, source, span, first in parts]
    def slots_of(ref):
        return lambda index: ref.at[index]

    settled = side == east
    R.in_part[...] = summed(0, in_copies)

    def in_send(step, source, slot, device):
        return pltpu.make_async_remote_copy(
            src_ref=source,
            dst_ref=R.in_sums.at[slot],
            send_sem=R.out_sem.at[40, step],
            recv_sem=R.in_sem.at[40, step],
            device_id=device,
            device_id_type=MESH,
        )

    in_near = in_send(0, R.in_part, corner, {"blk": near})
    in_far = [
        in_send(1 + n, R.in_sums.at[slot], slot, {"dp": across})
        for n, slot in enumerate((corner, facing))
    ]

    @pl.when(jnp.logical_not(settled))
    def _():
        in_near.start()

    @pl.when(settled)
    def _():
        R.in_sums[corner] = R.in_part[...]
        in_far[0].start()

    quarter = channels // rows_count

    @pl.loop(0, groups)
    def _(group):
        grad = matmul_turned(R.shifted[group], R.taps[group])
        for block in range(group_width // steps):
            span = slice(block * LANES, (block + 1) * LANES)
            tiles = [
                grad[a * group_width : (a + 1) * group_width, span] for a in range(steps)
            ]
            for u, tile in enumerate(swap_blocks(tiles, TAP_STEP)):
                channel = block * steps + u
                R.conv_part[group, channel // quarter, channel % quarter] = tile.astype(low)
    conv_copy = send(25, 0, R.conv_part.at[:, 1 - core], R.conv_got, twin, "dp")
    small_copy.wait()
    R.small_sum[0] = R.small[...] + R.small_got[0]
    small_copy = send(21, 1, R.small_sum.at[0], R.small_got.at[1], across, "dp")
    conv_copy.wait()
    for part in range(2):
        R.conv_sum[part] = (
            R.conv_part[part, core].astype(f32) + R.conv_got[part].astype(f32)
        ).astype(low)
    conv_copy = send(25, 1, R.conv_sum.at[1 - row // 2], R.conv_far, across, "dp")
    R.out_sums[row] = summed(1, out_copies)
    out_share = share_start(43, slots_of(R.out_sums))
    att_copies = [
        sum_next(kind + 1, 2, source, span, first, copies)
        for (kind, source, span, first), copies in zip(parts, att_copies)
    ]
    @pl.when(settled)
    def _():
        in_near.wait_recv()
        in_far[1].start()

    small_copy.wait()
    R.small_sum[1] = R.small_sum[0] + R.small_got[1]
    small_copy = send(21, 2, R.small_sum.at[1], R.small_got.at[2], near)

    att_copies = [
        sum_last(kind + 13, 2, span, first, copies)
        for (kind, source, span, first), copies in zip(parts, att_copies)
    ]
    share_forward(43, slots_of(R.out_sums), out_share)
    wait(back)
    wait_some(mixed_pending)
    R.frames_done[...] = (
        R.mixed_got[...].astype(f32) + (R.back_home[...].astype(f32) * valid).T
    ).astype(low)
    store(0, R.frames_done, R.frames_out)
    wait_some(layer_pending)
    store(1, R.layer_got, R.layer_out)
    conv_copy.wait()
    R.conv_sums[row] = (
        R.conv_sum[row // 2].astype(f32) + R.conv_far[...].astype(f32)
    ).astype(low)
    conv_share = share_start(42, slots_of(R.conv_sums))
    small_copy.wait()
    R.small_far[level] = R.small_sum[1] + R.small_got[2]
    smalls = []
    for step in range(1, levels):
        target = 2 * peer(level, step, levels) + side
        smalls.append(
            send(30, step, R.small_far.at[level], R.small_far.at[level], target)
        )

    R.attn_sums[row] = summed(2, att_copies[0] + att_copies[1])
    att_share = share_start(31, slots_of(R.attn_sums))
    share_forward(42, slots_of(R.conv_sums), conv_share)
    wait(smalls)
    R.small_done[...] = sum_parts(R.small_far)
    store(2, R.small_done, R.small_out)

    @pl.when(settled)
    def _():
        in_far[0].wait_send()
        in_far[1].wait_send()

    @pl.when(jnp.logical_not(settled))
    def _():
        in_near.wait_send()
        in_far[0].wait_recv()
        in_far[1].wait_recv()

    in_share = [
        send(40, 3 + n, R.in_sums.at[slot], R.in_sums.at[slot], twin, "dp")
        for n, slot in enumerate((corner, facing))
    ]
    wait(out_share)
    store(3, R.out_sums, R.back_out)
    wait(in_share)
    store(6, R.in_sums, R.in_out)
    wait(conv_share)
    store(4, R.conv_sums, R.conv_out)
    share_forward(31, slots_of(R.attn_sums), att_share)
    wait(att_share)
    store(5, R.attn_sums, R.attn_out)
    for copy in stores:
        copy.wait()


VECTORS = (
    "conv_bias",
    "qv_bias",
    "out_bias",
    "gain_one",
    "shift_one",
    "in_bias",
    "back_bias",
    "gain_two",
    "shift_two",
)


def layer(count, rows_count, head_dim, named):
    low, f32 = jnp.bfloat16, jnp.float32
    tokens, width = named["frames"].shape
    wide = named["in_hbm"].shape[1]
    _, group_width, kernel = named["conv_hbm"].shape
    channels = width // count
    groups = channels // group_width
    length = count * LANES
    span = length + LANES
    steps = kernel // TAP_STEP
    taps = group_width * TAP_STEP
    every = rows_count * tokens
    piece = channels // rows_count
    extras = count // 2 * head_dim
    levels = count // 2
    outs = {
        "layer_out": ((tokens, width), low),
        "frames_out": ((tokens, width), low),
        "conv_out": ((rows_count, piece, group_width, kernel), low),
        "in_out": ((rows_count, channels, width), low),
        "back_out": ((rows_count, channels, width), low),
        "attn_out": ((rows_count, channels, width), low),
        "small_out": ((16, width), f32),
    }
    scratch = {
        "qkv_w": (named["qkv_hbm"].shape, low),
        "out_w": (named["out_hbm"].shape, low),
        "in_w": (named["in_hbm"].shape, low),
        "back_w": (named["back_hbm"].shape, low),
        "table": ((16, width), f32),
        "small": ((16, width), f32),
        "small_got": ((3, 16, width), f32),
        "small_sum": ((2, 16, width), f32),
        "small_far": ((levels, 16, width), f32),
        "turned": ((width, tokens), low),
        "conv_turned": ((width, tokens), low),
        "column": ((channels, span + LANES), low),
        "gcol": ((channels, span + LANES), low),
        "segs": ((count, 1, LANES), jnp.int32),
        "clip": ((length, LANES), f32),
        "stage": ((span // LANES * taps, LANES), f32),
        "own_weight": ((channels, group_width, kernel), low),
        "frames_home": ((tokens, width), low),
        "cotangent_home": ((tokens, width), low),
        "layer_here": ((tokens, width), low),
        "mixed_here": ((tokens, width), low),
        "mixed_got": ((tokens, width), low),
        "taps": ((groups, taps, span), low),
        "mix": ((groups, steps * group_width, taps), low),
        "mix_back": ((groups, steps * group_width, taps), low),
        "shifted": ((groups, steps * group_width, span), low),
        "result": ((channels, length), low),
        "conv_home": ((width, tokens), low),
        "back_home": ((width, tokens), low),
        "slope": ((tokens, width), f32),
        "mixed": ((tokens, width), f32),
        "project": ((3, width, tokens), low),
        "main": ((3, head_dim, length), low),
        "extra": ((3, head_dim, length), low),
        "att_main": ((head_dim, length), f32),
        "att_extra": ((head_dim, length // 2), f32),
        "low_main": ((head_dim, length), low),
        "low_extra": ((head_dim, length), low),
        "lse_main": ((1, length), f32),
        "lse_extra": ((1, length // 2), f32),
        "att_home": ((width, tokens), low),
        "keep": ((tokens, wide), f32),
        "total": ((tokens, width), f32),
        "dkey": ((head_dim, length), f32),
        "dvalue": ((head_dim, length), f32),
        "left": ((2, width, tokens), low),
        "act_turned": ((count, rows_count, wide // (count * rows_count), tokens), low),
        "pre_turned": ((rows_count, width, tokens), low),
        "hidden_all": ((width, every), low),
        "two_all": ((width, every), low),
        "pre_all": ((width, every), low),
        "act_all": ((count, wide // (count * rows_count), every), low),
        "late_left": ((width, every), low),
        "late_right": ((width, every), low),
        "gmain": ((head_dim, length), low),
        "gextra": ((head_dim, length), low),
        "dmain": ((3, head_dim, length), low),
        "dextra": ((3, head_dim, length), low),
        "dproject": ((4, width, tokens), low),
        "halves": ((2, 2, extras, tokens), low),
        "got_one": ((3, 4, channels, width), low),
        "sum_one": ((3, 4, channels, width), low),
        "got_two": ((3, 2, channels, width), low),
        "sum_two": ((3, 2, channels, width), low),
        "got_three": ((3, channels, width), low),
        "layer_got": ((tokens, width), low),
        "frames_done": ((tokens, width), low),
        "small_done": ((16, width), f32),
        "in_sums": ((rows_count, channels, width), low),
        "in_part": ((channels, width), low),
        "out_sums": ((rows_count, channels, width), low),
        "conv_sums": ((rows_count, piece, group_width, kernel), low),
        "attn_sums": ((rows_count, channels, width), low),
        "conv_part": ((2, 2, piece, group_width, kernel), low),
        "conv_got": ((2, piece, group_width, kernel), low),
        "conv_sum": ((2, piece, group_width, kernel), low),
        "conv_far": ((piece, group_width, kernel), low),
    }
    hbm = pl.BlockSpec(memory_space=pl.ANY)
    names = (*named, *outs, *scratch, "out_sem", "in_sem", "load_sem", "store_sem")
    return pl.pallas_call(
        functools.partial(layer_kernel, names, count, rows_count, head_dim),
        out_shape=tuple(jax.ShapeDtypeStruct(*out) for out in outs.values()),
        in_specs=[hbm if name.endswith("_hbm") else VMEM for name in named],
        out_specs=(hbm,) * len(outs),
        scratch_shapes=[pltpu.VMEM(*item) for item in scratch.values()]
        + [
            pltpu.SemaphoreType.DMA((45, count)),
            pltpu.SemaphoreType.DMA((45, count)),
            pltpu.SemaphoreType.DMA((3 + 2 * (wide // width),)),
            pltpu.SemaphoreType.DMA((len(outs),)),
        ],
        compiler_params=pltpu.CompilerParams(
            collective_id=0, has_side_effects=True, vmem_limit_bytes=62 * 2**20
        ),
        name="layer",
    )(*named.values())


def unpack_kernel(
    count,
    layer_hbm,
    frames_hbm,
    conv_hbm,
    in_hbm,
    back_hbm,
    attn_hbm,
    small_hbm,
    layer_out,
    frames_out,
    conv_out,
    conv_bias,
    qkv_out,
    qv_bias,
    out_out,
    out_bias,
    gain_one,
    shift_one,
    in_out,
    in_bias,
    back_out,
    back_bias,
    gain_two,
    shift_two,
    conv_wide,
    qkv_wide,
    out_wide,
    in_wide,
    back_wide,
    conv_ref,
    in_ref,
    back_ref,
    attn_ref,
    small_ref,
    layer_ref,
    frames_ref,
    spare,
    sems,
):
    f32 = jnp.float32
    me = lax.axis_index("blk")
    rows_count, channels, width = attn_ref.shape
    piece = conv_ref.shape[1]
    copies = []

    def start(source, target):
        copy = pltpu.make_async_copy(source, target, sems.at[len(copies)])
        copy.start()
        copies.append(copy)

    loads = [
        pltpu.make_async_copy(source, target, sems.at[6 + rows_count + i])
        for i, (source, target) in enumerate(
            (
                (conv_hbm, conv_ref),
                (in_hbm, in_ref),
                (back_hbm, back_ref),
                (attn_hbm, attn_ref),
                (small_hbm, small_ref),
                (layer_hbm, layer_ref),
                (frames_hbm, frames_ref),
            )
        )
    ]
    for load in loads:
        load.start()
    loads[0].wait()
    for row in range(rows_count):
        part = slice(row * piece, (row + 1) * piece)
        conv_wide[part] = conv_ref[row].astype(f32)
        start(conv_wide.at[part], conv_out.at[part])
    loads[1].wait()
    for row in range(rows_count):
        in_wide[:, row * width : (row + 1) * width] = in_ref[row].astype(f32)
    start(in_wide, in_out)
    loads[2].wait()
    for row in range(rows_count):
        back_wide[row * channels : (row + 1) * channels, :] = back_ref[row].astype(f32)
    start(back_wide, back_out)
    loads[3].wait()
    for row in range(rows_count - 1):
        qkv_wide[:, row * width : (row + 1) * width] = attn_ref[row].astype(f32)
    start(qkv_wide, qkv_out)
    out_wide[...] = attn_ref[rows_count - 1].astype(f32)
    start(out_wide, out_out)
    loads[5].wait()
    start(layer_ref, layer_out)
    loads[6].wait()
    start(frames_ref, frames_out)
    loads[4].wait()
    small = small_ref[...]
    own = pltpu.roll(small, lax.rem(width - channels * me, width), 1)
    for place, ref in (
        (0, conv_bias),
        (3, out_bias),
        (4, gain_one),
        (5, shift_one),
        (10, back_bias),
        (11, gain_two),
        (12, shift_two),
    ):
        ref[...] = own[place, :channels]
    for first, parts, ref in ((1, 2, qv_bias), (6, rows_count, in_bias)):
        size = parts * channels
        inside = count // parts
        spare[...] = pltpu.roll(small, lax.rem(width - size * lax.rem(me, inside), width), 1)
        ref[...] = spare[pl.ds(first + me // inside, 1), :][0, :size]
    for copy in copies:
        copy.wait()


def unpack(count, layer_out, frames_out, conv, ffn_in, ffn_out, attn, small):
    rows_count, channels, width = attn.shape
    piece, group_width, kernel = conv.shape[1:]
    f32 = jnp.float32
    hbm = pl.BlockSpec(memory_space=pl.ANY)
    vector = jax.ShapeDtypeStruct((channels,), f32)
    conv_type = jax.ShapeDtypeStruct((rows_count * piece, group_width, kernel), f32)
    qkv_type = jax.ShapeDtypeStruct((channels, (rows_count - 1) * width), f32)
    out_type = jax.ShapeDtypeStruct((channels, width), f32)
    in_type = jax.ShapeDtypeStruct((channels, rows_count * width), f32)
    back_type = jax.ShapeDtypeStruct((rows_count * channels, width), f32)
    results = pl.pallas_call(
        functools.partial(unpack_kernel, count),
        out_shape=(
            jax.ShapeDtypeStruct(layer_out.shape, layer_out.dtype),
            jax.ShapeDtypeStruct(frames_out.shape, frames_out.dtype),
            conv_type,
            vector,
            qkv_type,
            jax.ShapeDtypeStruct((2 * channels,), f32),
            out_type,
            vector,
            vector,
            vector,
            in_type,
            jax.ShapeDtypeStruct((rows_count * channels,), f32),
            back_type,
            vector,
            vector,
            vector,
        ),
        in_specs=[hbm] * 7,
        out_specs=(
            hbm,
            hbm,
            hbm,
            VMEM,
            hbm,
            VMEM,
            hbm,
            VMEM,
            VMEM,
            VMEM,
            hbm,
            VMEM,
            hbm,
            VMEM,
            VMEM,
            VMEM,
        ),
        scratch_shapes=[
            pltpu.VMEM(item.shape, f32)
            for item in (conv_type, qkv_type, out_type, in_type, back_type)
        ]
        + [pltpu.VMEM(item.shape, item.dtype) for item in (conv, ffn_in, ffn_out, attn, small, layer_out, frames_out)]
        + [pltpu.VMEM(small.shape, f32), pltpu.SemaphoreType.DMA((13 + rows_count,))],
        compiler_params=pltpu.CompilerParams(vmem_limit_bytes=62 * 2**20),
        name="unpack",
    )(layer_out, frames_out, conv, ffn_in, ffn_out, attn, small)
    return (results[0][None], results[1][None], *results[2:])


def shards(sizes, *arrays):
    frames, segment, conv_weight = arrays[:3]
    row_count, block_len, model_width = frames.shape
    group_width, kernel = conv_weight.shape[1:]
    count = sizes["blk"]
    head_dim = model_width // HEADS
    channels = model_width // count
    fits = (
        row_count == 1
        and block_len == LANES
        and kernel == LANES
        and channels % group_width == 0
        and group_width % TAP_STEP == 0
        and count % 4 == 0
        and 2 * HEADS == 3 * count
        and head_dim % TAP_STEP == 0
        and sizes["dp"] == 4
        and count % sizes["dp"] == 0
        and arrays[10].shape[1] == 4 * model_width
    )
    if fits:
        return swap_shards(count, sizes["dp"], *arrays)
    return ring_shards(*arrays)


def swap_shards(
    count,
    rows_count,
    frames,
    segment,
    conv_weight,
    conv_bias,
    qkv_weight,
    qv_bias,
    out_weight,
    out_bias,
    norm1_gain,
    norm1_bias,
    ffn_in,
    ffn_in_bias,
    ffn_out,
    ffn_out_bias,
    norm2_gain,
    norm2_bias,
    cotangent,
):
    named = {
        "frames": frames[0],
        "segment": segment,
        "cotangent": cotangent[0],
        "conv_bias": conv_bias,
        "qv_bias": qv_bias,
        "out_bias": out_bias,
        "gain_one": norm1_gain,
        "shift_one": norm1_bias,
        "in_bias": ffn_in_bias,
        "back_bias": ffn_out_bias,
        "gain_two": norm2_gain,
        "shift_two": norm2_bias,
        "conv_hbm": conv_weight,
        "qkv_hbm": qkv_weight,
        "out_hbm": out_weight,
        "in_hbm": ffn_in,
        "back_hbm": ffn_out,
    }
    width = frames.shape[2]
    results = layer(count, rows_count, width // HEADS, named)
    return unpack(count, *results)


def solution(mesh):
    return jax.shard_map(
        functools.partial(shards, mesh.shape),
        mesh=mesh,
        in_specs=(
            P("dp", "blk", None),
            P("dp", "blk"),
            P(),
            P(),
            P(),
            P(),
            P(),
            P(),
            P(),
            P(),
            P(),
            P(),
            P(),
            P(),
            P(),
            P(),
            P("dp", "blk", None),
        ),
        out_specs=(
            P("dp", "blk", None),
            P("dp", "blk", None),
            P("blk", None, None),
            P("blk"),
            P("blk", None),
            P("blk"),
            P("blk", None),
            P("blk"),
            P("blk"),
            P("blk"),
            P("blk", None),
            P("blk"),
            P("blk", None),
            P("blk"),
            P("blk"),
            P("blk"),
        ),
        check_vma=False,
    )
```

```python
import functools
import math
import types

import jax
import jax.numpy as jnp
from jax import lax
from jax.experimental import pallas as pl
from jax.experimental.pallas import tpu as pltpu
from jax.sharding import PartitionSpec as P

HEADS = 12
GROUPS = 16


EPS = 1e-05
ROOT_HALF = 0.7071067811865476
DENSITY_CONST = 0.3989422804014327


def with_halo(x, sides, width):
    for axis, dim in sides:
        size, length = (lax.axis_size(axis), x.shape[dim])
        up = [(i, (i + 1) % size) for i in range(size - 1)]
        down = [(j, i) for i, j in up]
        last = lax.slice_in_dim(x, length - width, length, axis=dim)
        initial = lax.slice_in_dim(x, 0, width, axis=dim)
        before = lax.ppermute(last, axis, up)
        after = lax.ppermute(initial, axis, down)
        x = jnp.concatenate([before, x, after], axis=dim)
    return x


def from_behind(value, axis, steps):
    count = lax.axis_size(axis)
    pairs = [(source, (source + steps) % count) for source in range(count)]
    return lax.ppermute(value, axis, pairs)


def gelu_value(signal):
    return 0.5 * signal * (1.0 + lax.erf(signal * ROOT_HALF))


def gelu_slope(signal):
    return (
        0.5 * (1.0 + lax.erf(signal * ROOT_HALF))
        + signal * jnp.exp(-0.5 * signal * signal) * DENSITY_CONST
    )


def norm_forward(signal, gain_vec, shift_vec):
    average = jnp.mean(signal, axis=-1, keepdims=True)
    centred = signal - average
    inv_std = lax.rsqrt(jnp.mean(centred * centred, axis=-1, keepdims=True) + EPS)
    normed = centred * inv_std
    return (normed * gain_vec + shift_vec, normed, inv_std)


def norm_backward(grad_in, normed, inv_std, gain_vec):
    scaled = grad_in * gain_vec
    result = inv_std * (
        scaled
        - jnp.mean(scaled, axis=-1, keepdims=True)
        - normed * jnp.mean(scaled * normed, axis=-1, keepdims=True)
    )
    return (result, jnp.sum(grad_in * normed, axis=0), jnp.sum(grad_in, axis=0))


def block_grads(
    query_h, dout_h, query_seg, log_tot, row_delta, key_h, value_h, key_seg, score_scale
):
    scores = (
        jnp.einsum("rqhc,rkhc->rhqk", query_h, key_h, preferred_element_type=jnp.float32)
        * score_scale
    )
    same_seg = (query_seg[:, :, None] == key_seg[:, None, :])[:, None]
    weights_f = jnp.where(same_seg, jnp.exp(scores - log_tot[..., None]), 0.0)
    grad_prob = jnp.einsum("rqhc,rkhc->rhqk", dout_h, value_h, preferred_element_type=jnp.float32)
    grad_score = (weights_f * (grad_prob - row_delta[..., None])).astype(jnp.bfloat16)
    query_part = score_scale * jnp.einsum(
        "rhqk,rkhc->rqhc", grad_score, key_h, preferred_element_type=jnp.float32
    )
    key_part = score_scale * jnp.einsum(
        "rhqk,rqhc->rkhc", grad_score, query_h, preferred_element_type=jnp.float32
    )
    value_part = jnp.einsum(
        "rhqk,rqhc->rkhc",
        weights_f.astype(jnp.bfloat16),
        dout_h,
        preferred_element_type=jnp.float32,
    )
    return (query_part, key_part, value_part)


def ring_shards(
    frames,
    segment,
    conv_weight,
    conv_bias,
    qkv_weight,
    qv_bias,
    out_weight,
    out_bias,
    norm1_gain,
    norm1_bias,
    ffn_in,
    ffn_in_bias,
    ffn_out,
    ffn_out_bias,
    norm2_gain,
    norm2_bias,
    cotangent,
):
    row_count, block_len, model_width = frames.shape
    token_count = row_count * block_len
    group_width = conv_weight.shape[1]
    kernel = conv_weight.shape[2]
    half_kernel = kernel // 2
    head_dim = model_width // HEADS
    score_scale = head_dim ** (-0.5)
    cycle_len = lax.axis_size("blk")
    is_valid = segment >= 0
    masked = jnp.where(is_valid[..., None], frames, jnp.zeros_like(frames))
    padded = with_halo(masked, (("blk", 1),), half_kernel)
    conv_out = lax.conv_general_dilated(
        padded,
        conv_weight,
        (1,),
        "VALID",
        dimension_numbers=("NWC", "OIW", "NWC"),
        feature_group_count=GROUPS,
        preferred_element_type=jnp.float32,
    )
    pre_conv = conv_out[:, :block_len].reshape(token_count, model_width) + conv_bias.astype(
        jnp.float32
    )
    mixed_in = frames.reshape(token_count, model_width).astype(jnp.float32) + gelu_value(pre_conv)
    mixed_low = mixed_in.astype(jnp.bfloat16)
    pair_bias = qv_bias.astype(jnp.float32)
    zero_bias = jnp.zeros((model_width,), jnp.float32)
    full_bias = jnp.concatenate([pair_bias[:model_width], zero_bias, pair_bias[model_width:]])
    project = (
        jnp.dot(mixed_low, qkv_weight, preferred_element_type=jnp.float32) + full_bias
    ).astype(jnp.bfloat16)
    project = project.reshape(row_count, block_len, 3 * model_width)
    query_heads = project[..., :model_width].reshape(row_count, block_len, HEADS, head_dim)
    keys_local = project[..., model_width : 2 * model_width]
    values_local = project[..., 2 * model_width :]
    key_heads = keys_local.reshape(row_count, block_len, HEADS, head_dim)
    value_heads = values_local.reshape(row_count, block_len, HEADS, head_dim)
    query_seg = segment.astype(jnp.bfloat16)
    start_carry = (
        jnp.full((row_count, HEADS, block_len), -1e30, jnp.float32),
        jnp.zeros((row_count, HEADS, block_len), jnp.float32),
        jnp.zeros((row_count, HEADS, block_len, head_dim), jnp.float32),
    )
    key_piece = lax.all_gather(keys_local, "blk", axis=1, tiled=True)
    value_piece = lax.all_gather(values_local, "blk", axis=1, tiled=True)
    seg_piece = lax.all_gather(query_seg, "blk", axis=1, tiled=True)
    piece_len = key_piece.shape[1]
    block_size = math.gcd(piece_len, 512)

    def one_block(block_index, inner_carry):
        running_max, denominator, numerator = inner_carry
        offset = block_index * block_size
        key_block = lax.dynamic_slice_in_dim(key_piece, offset, block_size, 1).reshape(
            row_count, block_size, HEADS, head_dim
        )
        value_block = lax.dynamic_slice_in_dim(value_piece, offset, block_size, 1).reshape(
            row_count, block_size, HEADS, head_dim
        )
        seg_block = lax.dynamic_slice_in_dim(seg_piece, offset, block_size, 1)
        scores = (
            jnp.einsum(
                "rqhc,rkhc->rhqk", query_heads, key_block, preferred_element_type=jnp.float32
            )
            * score_scale
        )
        same_seg = (query_seg[:, :, None] == seg_block[:, None, :])[:, None]
        masked_scores = jnp.where(same_seg, scores, -1e30)
        new_max = jnp.maximum(running_max, jnp.max(masked_scores, axis=-1))
        weights_f = jnp.where(same_seg, jnp.exp(masked_scores - new_max[..., None]), 0.0)
        rescale = jnp.exp(running_max - new_max)
        denominator = denominator * rescale + jnp.sum(weights_f, axis=-1)
        numerator = numerator * rescale[..., None] + jnp.einsum(
            "rhqk,rkhc->rhqc",
            weights_f.astype(jnp.bfloat16),
            value_block,
            preferred_element_type=jnp.float32,
        )
        return (new_max, denominator, numerator)

    running_max, denominator, numerator = lax.fori_loop(
        0, piece_len // block_size, one_block, start_carry
    )
    log_total = running_max + jnp.log(denominator)
    attended_heads = (numerator / denominator[..., None]).transpose(0, 2, 1, 3)
    attended = attended_heads.reshape(token_count, model_width)
    attn_low = attended.astype(jnp.bfloat16)
    branch = jnp.dot(attn_low, out_weight, preferred_element_type=jnp.float32) + out_bias.astype(
        jnp.float32
    )
    gain_one = norm1_gain.astype(jnp.float32)
    hidden_norm, normed_one, inv_one = norm_forward(
        mixed_in + branch, gain_one, norm1_bias.astype(jnp.float32)
    )
    hidden_low = hidden_norm.astype(jnp.bfloat16)
    ffn_pre = jnp.dot(hidden_low, ffn_in, preferred_element_type=jnp.float32) + ffn_in_bias.astype(
        jnp.float32
    )
    ffn_act = gelu_value(ffn_pre).astype(jnp.bfloat16)
    ffn_branch = jnp.dot(
        ffn_act, ffn_out, preferred_element_type=jnp.float32
    ) + ffn_out_bias.astype(jnp.float32)
    gain_two = norm2_gain.astype(jnp.float32)
    layer_out, normed_two, inv_two = norm_forward(
        hidden_norm + ffn_branch, gain_two, norm2_bias.astype(jnp.float32)
    )
    grad_top = cotangent.reshape(token_count, model_width).astype(jnp.float32)
    grad_second, norm2_gain_grad, norm2_bias_grad = norm_backward(
        grad_top, normed_two, inv_two, gain_two
    )
    grad_branch_two = grad_second.astype(jnp.bfloat16)
    ffn_out_grad = jnp.einsum(
        "nf,nd->fd", ffn_act, grad_branch_two, preferred_element_type=jnp.float32
    )
    ffn_out_bias_grad = jnp.sum(grad_branch_two.astype(jnp.float32), axis=0)
    grad_act = jnp.einsum("nd,fd->nf", grad_branch_two, ffn_out, preferred_element_type=jnp.float32)
    grad_pre = (grad_act * gelu_slope(ffn_pre)).astype(jnp.bfloat16)
    ffn_in_grad = jnp.einsum("nd,nf->df", hidden_low, grad_pre, preferred_element_type=jnp.float32)
    ffn_in_bias_grad = jnp.sum(grad_pre.astype(jnp.float32), axis=0)
    grad_hidden = grad_second + jnp.einsum(
        "nf,df->nd", grad_pre, ffn_in, preferred_element_type=jnp.float32
    )
    grad_first, norm1_gain_grad, norm1_bias_grad = norm_backward(
        grad_hidden, normed_one, inv_one, gain_one
    )
    grad_branch = grad_first.astype(jnp.bfloat16)
    out_weight_grad = jnp.einsum(
        "ne,nd->ed", attn_low, grad_branch, preferred_element_type=jnp.float32
    )
    out_bias_grad = jnp.sum(grad_branch.astype(jnp.float32), axis=0)
    grad_att = jnp.einsum("nd,ed->ne", grad_branch, out_weight, preferred_element_type=jnp.float32)
    grad_heads = grad_att.astype(jnp.bfloat16).reshape(row_count, block_len, HEADS, head_dim)
    row_delta = jnp.einsum("rqhc,rqhc->rhq", grad_heads.astype(jnp.float32), attended_heads)
    zero_heads = jnp.zeros((row_count, block_len, HEADS, head_dim), jnp.float32)

    def key_step(carried):
        key_block, value_block, seg_block, key_grad, value_grad, query_grad = carried
        query_part, key_part, value_part = block_grads(
            query_heads,
            grad_heads,
            query_seg,
            log_total,
            row_delta,
            key_block,
            value_block,
            seg_block,
            score_scale,
        )
        query_grad = query_grad + query_part
        key_grad = key_grad + key_part
        value_grad = value_grad + value_part
        key_block, value_block, seg_block = from_behind(
            (key_block, value_block, seg_block), "blk", 1
        )
        key_grad, value_grad = (
            from_behind(key_grad.astype(jnp.bfloat16), "blk", 1).astype(key_grad.dtype),
            from_behind(value_grad.astype(jnp.bfloat16), "blk", 1).astype(value_grad.dtype),
        )
        return (key_block, value_block, seg_block, key_grad, value_grad, query_grad)

    def four_steps(turn_index, carried):
        for repeat in range(4):
            carried = key_step(carried)
        return carried

    final_state = lax.fori_loop(
        0,
        cycle_len // 4,
        four_steps,
        (key_heads, value_heads, query_seg, zero_heads, zero_heads, zero_heads),
    )
    key_grad, value_grad, query_grad = (final_state[3], final_state[4], final_state[5])
    grad_project = jnp.concatenate(
        [
            query_grad.reshape(token_count, model_width),
            key_grad.reshape(token_count, model_width),
            value_grad.reshape(token_count, model_width),
        ],
        axis=1,
    ).astype(jnp.bfloat16)
    qkv_weight_grad = jnp.einsum(
        "nd,ne->de", mixed_low, grad_project, preferred_element_type=jnp.float32
    )
    bias_sums = jnp.sum(grad_project.astype(jnp.float32), axis=0)
    qv_bias_grad = jnp.concatenate([bias_sums[:model_width], bias_sums[2 * model_width :]])
    grad_mixed = grad_first + jnp.einsum(
        "ne,de->nd", grad_project, qkv_weight, preferred_element_type=jnp.float32
    )
    grad_conv = (grad_mixed * gelu_slope(pre_conv)).astype(jnp.bfloat16)
    conv_bias_grad = jnp.sum(grad_conv.astype(jnp.float32), axis=0)
    grad_conv_rows = grad_conv.reshape(row_count, block_len, model_width)
    grad_padded = with_halo(grad_conv_rows, (("blk", 1),), half_kernel)
    flipped = conv_weight.reshape(GROUPS, group_width, group_width, kernel).transpose(0, 2, 1, 3)
    flipped = flipped.reshape(model_width, group_width, kernel)[:, :, ::-1]
    back_conv = lax.conv_general_dilated(
        grad_padded,
        flipped,
        (1,),
        "VALID",
        dimension_numbers=("NWC", "OIW", "NWC"),
        feature_group_count=GROUPS,
        preferred_element_type=jnp.float32,
    )[:, 1:]
    frames_grad = (
        grad_mixed.reshape(row_count, block_len, model_width)
        + jnp.where(is_valid[..., None], back_conv, 0.0)
    ).astype(jnp.bfloat16)
    conv_weight_grad = lax.conv_general_dilated(
        padded,
        grad_conv_rows,
        (1,),
        "VALID",
        dimension_numbers=("CWN", "IWO", "CNW"),
        batch_group_count=GROUPS,
        preferred_element_type=jnp.float32,
    )[:, :, :kernel]
    (
        conv_weight_part,
        conv_bias_part,
        qkv_weight_part,
        qv_bias_part,
        out_weight_part,
        out_bias_part,
        gain_one_part,
        shift_one_part,
        ffn_in_part,
        ffn_in_bias_part,
        ffn_out_part,
        ffn_out_bias_part,
        gain_two_part,
        shift_two_part,
    ) = (
        lax.psum_scatter(conv_weight_grad, "blk", scatter_dimension=0, tiled=True),
        lax.psum_scatter(conv_bias_grad, "blk", scatter_dimension=0, tiled=True),
        lax.psum_scatter(qkv_weight_grad, "blk", scatter_dimension=0, tiled=True),
        lax.psum_scatter(qv_bias_grad, "blk", scatter_dimension=0, tiled=True),
        lax.psum_scatter(out_weight_grad, "blk", scatter_dimension=0, tiled=True),
        lax.psum_scatter(out_bias_grad, "blk", scatter_dimension=0, tiled=True),
        lax.psum_scatter(norm1_gain_grad, "blk", scatter_dimension=0, tiled=True),
        lax.psum_scatter(norm1_bias_grad, "blk", scatter_dimension=0, tiled=True),
        lax.psum_scatter(ffn_in_grad, "blk", scatter_dimension=0, tiled=True),
        lax.psum_scatter(ffn_in_bias_grad, "blk", scatter_dimension=0, tiled=True),
        lax.psum_scatter(ffn_out_grad, "blk", scatter_dimension=0, tiled=True),
        lax.psum_scatter(ffn_out_bias_grad, "blk", scatter_dimension=0, tiled=True),
        lax.psum_scatter(norm2_gain_grad, "blk", scatter_dimension=0, tiled=True),
        lax.psum_scatter(norm2_bias_grad, "blk", scatter_dimension=0, tiled=True),
    )
    totals = (
        lax.psum(conv_weight_part.astype(jnp.bfloat16), "dp").astype(jnp.float32),
        lax.psum(conv_bias_part.astype(jnp.bfloat16), "dp").astype(jnp.float32),
        lax.psum(qkv_weight_part.astype(jnp.bfloat16), "dp").astype(jnp.float32),
        lax.psum(qv_bias_part.astype(jnp.bfloat16), "dp").astype(jnp.float32),
        lax.psum(out_weight_part.astype(jnp.bfloat16), "dp").astype(jnp.float32),
        lax.psum(out_bias_part.astype(jnp.bfloat16), "dp").astype(jnp.float32),
        lax.psum(gain_one_part.astype(jnp.bfloat16), "dp").astype(jnp.float32),
        lax.psum(shift_one_part.astype(jnp.bfloat16), "dp").astype(jnp.float32),
        lax.psum(ffn_in_part.astype(jnp.bfloat16), "dp").astype(jnp.float32),
        lax.psum(ffn_in_bias_part.astype(jnp.bfloat16), "dp").astype(jnp.float32),
        lax.psum(ffn_out_part.astype(jnp.bfloat16), "dp").astype(jnp.float32),
        lax.psum(ffn_out_bias_part.astype(jnp.bfloat16), "dp").astype(jnp.float32),
        lax.psum(gain_two_part.astype(jnp.bfloat16), "dp").astype(jnp.float32),
        lax.psum(shift_two_part.astype(jnp.bfloat16), "dp").astype(jnp.float32),
    )
    return (
        layer_out.reshape(row_count, block_len, model_width).astype(jnp.bfloat16),
        frames_grad,
        totals[0],
        totals[1],
        totals[2],
        totals[3],
        totals[4],
        totals[5],
        totals[6],
        totals[7],
        totals[8],
        totals[9],
        totals[10],
        totals[11],
        totals[12],
        totals[13],
    )


MESH = pl.DeviceIdType.MESH
LANES = 128
TAP_STEP = 16
VMEM = pl.BlockSpec(memory_space=pltpu.VMEM)


def peer(me, step, count):
    return lax.rem(me + step, count)


def greet(index, count, rows):
    barrier = pltpu.get_barrier_semaphore()
    for step in range(1, count * rows):
        other = lax.rem(index + step, count * rows)
        pl.semaphore_signal(
            barrier,
            inc=1,
            device_id={"dp": other // count, "blk": lax.rem(other, count)},
            device_id_type=MESH,
        )


def greet_wait(count, rows):
    pl.semaphore_wait(pltpu.get_barrier_semaphore(), count * rows - 1)


def remote(src, dst, send_sem, recv_sem, target, axis="blk"):
    copy = pltpu.make_async_remote_copy(
        src_ref=src,
        dst_ref=dst,
        send_sem=send_sem,
        recv_sem=recv_sem,
        device_id=target if isinstance(target, dict) else {axis: target},
        device_id_type=MESH,
    )
    copy.start()
    return copy


def turned(value):
    return value.astype(jnp.float32).T.astype(jnp.bfloat16)


def matmul_turned(left, right):
    return lax.dot_general(
        left, right, (((1,), (1,)), ((), ())), preferred_element_type=jnp.float32
    )


def sum_parts(parts_ref):
    total = parts_ref[0].astype(jnp.float32)
    for part in range(1, parts_ref.shape[0]):
        total = total + parts_ref[part].astype(jnp.float32)
    return total


def lane_block(index):
    return pl.ds(pl.multiple_of(index * LANES, LANES), LANES)


def row_block(index, size):
    return pl.ds(pl.multiple_of(index * size, size), size)


def swap_blocks(tiles, width):
    count = len(tiles)
    lane = lax.broadcasted_iota(jnp.int32, tiles[0].shape, 1) // width
    tiles = list(tiles)
    step = count // 2
    while step:
        low = (lane & step) == 0
        for u in range(count):
            if u & step == 0:
                one, two = tiles[u], tiles[u + step]
                tiles[u] = jnp.where(low, one, pltpu.roll(two, step * width, 1))
                tiles[u + step] = jnp.where(low, pltpu.roll(one, LANES - step * width, 1), two)
        step //= 2
    return tiles


def spread_taps(source, offset, direction, stage_ref, out_ref):
    rows, length = source.shape
    blocks = out_ref.shape[1] // LANES
    for tap in range(TAP_STEP):
        shift = (length - offset - direction * tap) % length
        moved = pltpu.roll(source, shift, 1)
        for block in range(blocks):
            first = block * rows * TAP_STEP + tap
            stage_ref[pl.ds(first, rows, stride=TAP_STEP), :] = moved[
                :, block * LANES : (block + 1) * LANES
            ]
    size = rows * TAP_STEP
    for block in range(blocks):
        out_ref[:, block * LANES : (block + 1) * LANES] = stage_ref[
            block * size : (block + 1) * size, :
        ].astype(jnp.bfloat16)


def query_span(index, size):
    return pl.ds(pl.multiple_of(index * size, size), size)


def same_clip(column_ref, seg_row):
    column = column_ref[...]
    parts = [
        column == seg_row[:, start : start + LANES]
        for start in range(0, seg_row.shape[1], LANES)
    ]
    return jnp.concatenate(parts, axis=1)


def clip_column(count, segs_ref, column_ref):
    for block in range(count):
        row = segs_ref[block].astype(jnp.float32)
        column_ref[block * LANES : (block + 1) * LANES, :] = jnp.broadcast_to(
            row, (LANES, LANES)
        ).T


def clip_row(segs_ref, first, size):
    parts = [segs_ref[first + i].astype(jnp.float32) for i in range(size // LANES)]
    return jnp.concatenate(parts, axis=1)


def layer_kernel(names, count, rows_count, head_dim, *refs):
    R = types.SimpleNamespace(**dict(zip(names, refs)))
    low, f32 = jnp.bfloat16, jnp.float32
    me, row = lax.axis_index("blk"), lax.axis_index("dp")
    level, side = me // 2, lax.rem(me, 2)
    levels = count // 2
    half = count // 2
    near = me + 1 - 2 * side
    core = lax.rem(row, 2)
    twin = row + 1 - 2 * core
    upper = level // 2
    pos = 4 * core + 2 * lax.rem(level, 2) + side
    home_row = 2 * (row // 2) + upper
    at_home = core == upper
    east = row // 2
    corner = 2 * side + core
    facing = peer(corner, 2, 4)
    across = peer(row, 2, rows_count)
    tokens, width = R.frames_hbm.shape
    channels = width // count
    length = count * LANES
    group_width = R.own_weight.shape[1]
    groups = channels // group_width
    steps = LANES // TAP_STEP
    scale = head_dim ** (-0.5)
    chunks = R.in_hbm.shape[1] // width

    def send(kind, step, source, target_ref, target, axis="blk"):
        return remote(
            source, target_ref, R.out_sem.at[kind, step], R.in_sem.at[kind, step], target, axis
        )

    def wait(copies):
        for copy in copies:
            copy.wait()

    def to_blocks(kind, source, target_ref):
        copies = []
        for step in range(1, count):
            target = peer(me, step, count)
            copies.append(send(kind, step, source(target), target_ref, target))
        return copies

    def device_at(place, part):
        return {"dp": 2 * (row // 2) + place // 4, "blk": 4 * part + lax.rem(place, 4)}

    def to_places(kind, source, target_ref):
        copies = []
        for step in range(1, count):
            target = peer(pos, step, count)
            copies.append(send(kind, step, source(target), target_ref, device_at(target, upper)))
        return copies

    def move(kind, source, target_ref, device):
        copy = pltpu.make_async_remote_copy(
            src_ref=source,
            dst_ref=target_ref,
            send_sem=R.out_sem.at[kind, 0],
            recv_sem=R.in_sem.at[kind, 0],
            device_id=device,
            device_id_type=MESH,
        )
        away = jnp.logical_not(at_home)
        pl.when(away)(copy.start)

        @pl.when(at_home)
        def _():
            target_ref[...] = source[...]

        return [(away, away, copy)]

    def shift_all(kind, first, own, device_of, source, target_ref):
        pending = []
        for step in range(count):
            target = peer(first, step, count)
            away = jnp.logical_not(jnp.logical_and(at_home, target == own))
            copy = pltpu.make_async_remote_copy(
                src_ref=source(target),
                dst_ref=target_ref,
                send_sem=R.out_sem.at[kind, step],
                recv_sem=R.in_sem.at[kind, step],
                device_id=device_of(target),
                device_id_type=MESH,
            )
            pl.when(away)(copy.start)
            pending.append((away, away, copy))

        @pl.when(at_home)
        def _():
            target_ref[...] = source(own)[...]

        return pending

    def to_level(kind, source, target_ref):
        return shift_all(
            kind, me, pos, lambda place: device_at(place, core), source, target_ref
        )

    def from_level(kind, source, target_ref):
        return shift_all(
            kind, pos, me, lambda block: {"dp": home_row, "blk": block}, source, target_ref
        )

    def wait_some(pending):
        for sends, comes, copy in pending:
            pl.when(sends)(copy.wait_send)
            pl.when(comes)(copy.wait_recv)

    def chunk_of(index):
        return slice(index * width, (index + 1) * width)

    def table(index):
        return R.table[index : index + 1, :]

    def dot(left, right):
        return jnp.dot(left, right, preferred_element_type=f32)

    greet(row * count + me, count, rows_count)

    loads = [pltpu.make_async_copy(R.qkv_hbm, R.qkv_w, R.load_sem.at[0])]
    loads.append(pltpu.make_async_copy(R.out_hbm, R.out_w, R.load_sem.at[1]))
    for chunk in range(chunks):
        span = chunk_of(chunk)
        loads.append(
            pltpu.make_async_copy(
                R.in_hbm.at[:, span], R.in_w.at[:, span], R.load_sem.at[2 + 2 * chunk]
            )
        )
        loads.append(
            pltpu.make_async_copy(
                R.back_hbm.at[span], R.back_w.at[span], R.load_sem.at[3 + 2 * chunk]
            )
        )
    for load in loads:
        load.start()
    own_load = pltpu.make_async_copy(
        R.conv_hbm.at[row_block(me, channels)], R.own_weight, R.load_sem.at[2 + 2 * chunks]
    )
    own_load.start()
    first_loads = [
        pltpu.make_async_copy(source, target, R.first_sem.at[index])
        for index, (source, target) in enumerate(
            ((R.frames_hbm, R.frames), (R.cotangent_hbm, R.cotangent))
        )
    ]
    for load in first_loads:
        load.start()
    first_loads[0].wait()
    valid = (R.segment[...] >= 0).astype(f32)
    R.turned[...] = (R.frames[...].astype(f32).T * valid).astype(low)
    to_level_device = device_at(me, core)
    from_level_device = {"dp": home_row, "blk": pos}

    R.table[...] = jnp.zeros_like(R.table)
    R.small[...] = jnp.zeros_like(R.small)
    place = 0
    for vector in VECTORS:
        ref = getattr(R, vector)
        for part in range(ref.shape[0] // width):
            R.table[place, :] = ref[chunk_of(part)].astype(f32)
            place += 1

    def mix_taps(mix, tile_rows):
        @pl.loop(0, group_width // steps)
        def _(block):
            for group in range(groups):
                tiles = [
                    R.stage[tile_rows(group, block * steps + u), :] for u in range(steps)
                ]
                for a, tile in enumerate(swap_blocks(tiles, TAP_STEP)):
                    rows = slice(a * group_width, (a + 1) * group_width)
                    mix[group, rows, lane_block(block)] = tile.astype(low)

    square = group_width * group_width
    own_load.wait()
    total_rows = channels * group_width
    R.stage[:total_rows, :] = R.own_weight[...].astype(f32).reshape(total_rows, LANES)
    mix_taps(R.mix, lambda g, i: pl.ds(g * square + i, group_width, stride=group_width))
    greet_wait(count, rows_count)

    copies = to_blocks(
        0, lambda p: R.turned.at[row_block(p, channels), :], R.column.at[:, lane_block(me + 1)]
    )
    R.column[:, lane_block(me + 1)] = R.turned[row_block(me, channels), :]
    for ref in (R.column, R.gcol):
        ref[:, :LANES] = jnp.zeros((channels, LANES), low)
        ref[:, length + LANES :] = jnp.zeros((channels, LANES), low)
    mix_taps(R.mix_back, lambda g, c: pl.ds(g * square + c * group_width, group_width))
    wait(copies)
    brought = move(33, R.frames, R.frames_home, to_level_device)
    seg_pending = to_level(1, lambda p: R.segment, R.segs.at[me])

    @pl.loop(0, groups)
    def _(group):
        rows = row_block(group, group_width)
        spread_taps(R.column[rows, :].astype(f32), LANES // 2, 1, R.stage, R.taps.at[group])
        product = dot(R.mix[group], R.taps[group])
        total = product[:group_width, :length]
        for a in range(1, steps):
            part = product[a * group_width : (a + 1) * group_width, :]
            part = pltpu.roll(part, product.shape[1] - a * TAP_STEP, 1)
            total = total + part[:, :length]
        R.result[rows, :] = total.astype(low)
    pending = to_level(
        2, lambda p: R.result.at[:, lane_block(p)], R.conv_home.at[row_block(me, channels), :]
    )
    @pl.loop(0, groups)
    def _(group):
        source = R.column[row_block(group, group_width), :].astype(f32)
        span = R.shifted.shape[2]
        for a in range(steps):
            moved = pltpu.roll(source, (span + LANES - a * TAP_STEP) % (span + LANES), 1)
            R.shifted[group, a * group_width : (a + 1) * group_width, :] = moved[:, :span].astype(
                low
            )
    wait_some(seg_pending)
    clip_column(count, R.segs, R.clip)
    wait_some(brought)
    wait_some(pending)

    pre = R.conv_home[...].astype(f32).T + table(0)
    share = 0.5 * (1.0 + lax.erf(pre * ROOT_HALF))
    R.slope[...] = share + pre * jnp.exp(-0.5 * pre * pre) * DENSITY_CONST
    mixed = R.frames_home[...].astype(f32) + pre * share
    R.mixed[...] = mixed
    mixed_low = mixed.astype(low)
    loads[0].wait()
    for part in range(3):
        block = dot(mixed_low, R.qkv_w[:, chunk_of(part)])
        if part != 1:
            block = block + table(1 + part // 2)
        block = block.astype(low).astype(f32)
        if part == 0:
            block = block * scale
        R.project[part] = block.T.astype(low)
    extra_copies = to_places(
        4,
        lambda p: R.project.at[:, row_block(count + p // 2, head_dim), :],
        R.extra.at[:, :, lane_block(pos)],
    )
    copies = to_places(
        3,
        lambda p: R.project.at[:, row_block(p, head_dim), :],
        R.main.at[:, :, lane_block(pos)],
    )
    R.main[:, :, lane_block(pos)] = R.project[:, row_block(pos, head_dim), :]
    R.extra[:, :, lane_block(pos)] = R.project[:, row_block(count + pos // 2, head_dim), :]
    R.left[0] = turned(mixed_low)
    last_row = rows_count - 1

    def to_some_rows(kind, source, sends_to, comes_to):
        pending = []
        for step in range(1, rows_count):
            target = peer(row, step, rows_count)
            copy = pltpu.make_async_remote_copy(
                src_ref=source,
                dst_ref=R.late_left.at[:, lane_block(row)],
                send_sem=R.out_sem.at[kind, step],
                recv_sem=R.in_sem.at[kind, step],
                device_id={"dp": target},
                device_id_type=MESH,
            )
            sends = sends_to(target)
            pl.when(sends)(copy.start)
            pending.append((sends, comes_to, copy))
        return pending

    left_pending = to_some_rows(8, R.left.at[0], lambda p: p != last_row, row != last_row)
    wait(extra_copies)

    size = 2 * LANES
    halves = half * LANES // size

    def scores_of(held, start, seg_row):
        scores = lax.dot_general(
            held[1], held[0, :, start], (((0,), (0,)), ((), ())), preferred_element_type=f32
        )
        return jnp.where(same_clip(R.clip, seg_row), scores, -1e30)

    def attend(held, start, index, att_ref, low_ref, lse_ref, place):
        scores = scores_of(held, start, clip_row(R.segs, index * 2, size))
        top = jnp.max(scores, axis=0, keepdims=True)
        weights = jnp.exp(scores - top)
        total = jnp.sum(weights, axis=0, keepdims=True)
        mean = dot(held[2], weights.astype(low)) / total
        att_ref[:, place] = mean
        low_ref[:, start] = mean.astype(low)
        lse_ref[:, place] = top + jnp.log(total)

    own_rows = row_block(pos, head_dim)
    extra_rows = row_block(count + pos // 2, head_dim)

    def to_half(kind, source, target_ref):
        pending = []
        for step in range(1, count):
            target, origin = peer(pos, step, count), peer(pos, count - step, count)
            copy = pltpu.make_async_remote_copy(
                src_ref=source(target),
                dst_ref=target_ref,
                send_sem=R.out_sem.at[kind, step],
                recv_sem=R.in_sem.at[kind, step],
                device_id=device_at(target, upper),
                device_id_type=MESH,
            )
            sends, comes = target // half == side, pos // half == lax.rem(origin, 2)
            pl.when(sends)(copy.start)
            pending.append((sends, comes, copy))
        return pending

    @pl.loop(0, halves)
    def _(block):
        index = side * halves + block
        place = query_span(block, size)
        attend(
            R.extra,
            query_span(index, size),
            index,
            R.att_extra,
            R.low_extra,
            R.lse_extra,
            place,
        )
    pending = to_half(5, lambda p: R.low_extra.at[:, lane_block(p)], R.att_home.at[extra_rows, :])

    @pl.when(pos // half == side)
    def _():
        R.att_home[extra_rows, :] = R.low_extra[:, lane_block(pos)]

    wait(copies)
    first_loads[1].wait()
    brought = move(34, R.cotangent, R.cotangent_home, to_level_device)

    @pl.loop(0, length // size)
    def _(block):
        span = query_span(block, size)
        attend(R.main, span, block, R.att_main, R.low_main, R.lse_main, span)

    copies = to_places(6, lambda p: R.low_main.at[:, lane_block(p)], R.att_home.at[own_rows, :])
    R.att_home[own_rows, :] = R.low_main[:, lane_block(pos)]
    wait(copies)
    wait_some(pending)

    def to_rows(kind, source, target_ref):
        return [
            send(kind, step, source(peer(row, step, rows_count)), target_ref, target, "dp")
            for step, target in ((n, peer(row, n, rows_count)) for n in range(1, rows_count))
        ]

    def share_start(kind, part, index=row, mate={"dp": across}):
        own = part(index)
        return [send(kind, 2, own, own, mate), send(kind, 1, own, own, twin, "dp")]

    def share_forward(kind, part, copies, index=across):
        copies[0].wait()
        got = part(index)
        copies[0] = send(kind, 3, got, got, twin, "dp")

    def lanes_of(ref):
        return lambda index: ref.at[:, lane_block(index)]

    R.left[1] = R.att_home[...]
    att = R.att_home[...].astype(f32).T.astype(low)
    loads[1].wait()
    branch = dot(att, R.out_w[...]) + table(3)
    hidden, normed_one, inv_one = norm_forward(R.mixed[...] + branch, table(4), table(5))
    hidden_low = hidden.astype(low)
    R.hidden_all[:, lane_block(corner)] = turned(hidden_low)
    hidden_copies = share_start(7, lanes_of(R.hidden_all), corner, {"blk": near})
    left_pending += to_some_rows(32, R.left.at[1], lambda p: p == last_row, row == last_row)
    R.late_left[:, lane_block(row)] = R.left[row // last_row]
    pieces = count // chunks
    for load in loads[2:]:
        load.wait()
    R.total[...] = hidden + table(10)

    @pl.loop(0, chunks)
    def _(chunk):
        span = query_span(chunk, width)
        pre = dot(hidden_low, R.in_w[:, span]) + R.table[pl.ds(6 + chunk, 1), :]
        share = 0.5 * (1.0 + lax.erf(pre * ROOT_HALF))
        act = (pre * share).astype(low)
        R.keep[:, span] = share + pre * jnp.exp(-0.5 * pre * pre) * DENSITY_CONST
        R.act_turned[pl.ds(chunk * pieces, pieces)] = turned(act).reshape(
            pieces, rows_count, -1, LANES
        )
        R.total[...] += dot(act, R.back_w[row_block(chunk, width), :])

    act_copies = to_rows(9, lambda p: R.act_turned.at[:, p], R.act_all.at[:, :, lane_block(row)])
    R.act_all[:, :, lane_block(row)] = R.act_turned[:, row]
    layer, normed_two, inv_two = norm_forward(R.total[...], table(11), table(12))
    R.layer_here[...] = layer.astype(low)
    wait_some(brought)
    grad_second, gain_sum, shift_sum = norm_backward(
        R.cotangent_home[...].astype(f32), normed_two, inv_two, table(11)
    )
    R.small[11, :] = gain_sum
    R.small[12, :] = shift_sum
    grad_two = grad_second.astype(low)
    R.two_all[:, lane_block(row)] = turned(grad_two)
    two_copies = share_start(10, lanes_of(R.two_all))
    R.small[10, :] = jnp.sum(grad_two.astype(f32), axis=0)
    R.total[...] = grad_second

    @pl.loop(0, chunks)
    def _(chunk):
        span = query_span(chunk, width)
        grad_pre = matmul_turned(grad_two, R.back_w[row_block(chunk, width), :]) * R.keep[:, span]
        grad_pre = grad_pre.astype(low)
        R.pre_turned[chunk] = turned(grad_pre)
        R.small[pl.ds(6 + chunk, 1), :] = jnp.sum(grad_pre.astype(f32), axis=0, keepdims=True)
        R.total[...] += matmul_turned(grad_pre, R.in_w[:, span])

    grad_first, gain_sum, shift_sum = norm_backward(R.total[...], normed_one, inv_one, table(4))
    R.small[4, :] = gain_sum
    R.small[5, :] = shift_sum
    R.mixed[...] = grad_first
    grad_branch = grad_first.astype(low)
    R.small[3, :] = jnp.sum(grad_branch.astype(f32), axis=0)
    R.turned[...] = turned(matmul_turned(grad_branch, R.out_w[...]).astype(low))

    extra_copies = to_places(
        12,
        lambda p: R.turned.at[row_block(count + p // 2, head_dim), :],
        R.gextra.at[:, lane_block(pos)],
    )
    copies = to_places(
        11, lambda p: R.turned.at[row_block(p, head_dim), :], R.gmain.at[:, lane_block(pos)]
    )
    R.gmain[:, lane_block(pos)] = R.turned[row_block(pos, head_dim), :]
    R.gextra[:, lane_block(pos)] = R.turned[row_block(count + pos // 2, head_dim), :]
    pre_copies = []
    for step in range(1, 4):
        target = peer(corner, step, 4)
        device = {"dp": 2 * east + lax.rem(target, 2), "blk": 2 * level + target // 2}
        pre_copies.append(
            send(13, step, R.pre_turned.at[target], R.pre_all.at[:, lane_block(corner)], device)
        )
    R.pre_all[:, lane_block(corner)] = R.pre_turned[corner]
    R.dproject[3] = turned(grad_branch)
    wait(extra_copies)
    layer_pending = move(35, R.layer_here, R.layer_got, from_level_device)
    share_forward(10, lanes_of(R.two_all), two_copies)

    def attend_back(held, grads, start, index, att, lse):
        queries = held[0, :, start]
        weights = jnp.exp(scores_of(held, start, clip_row(R.segs, index * 2, size)) - lse)
        grad_prob = lax.dot_general(
            held[2], grads, (((0,), (0,)), ((), ())), preferred_element_type=f32
        )
        delta = jnp.sum(grads.astype(f32) * att, axis=0, keepdims=True)
        grad_score = (weights * (grad_prob - delta)).astype(low)
        return (
            dot(held[1], grad_score) * scale,
            matmul_turned(queries, grad_score),
            matmul_turned(grads, weights.astype(low)),
        )

    R.dkey[...] = jnp.zeros_like(R.dkey)
    R.dvalue[...] = jnp.zeros_like(R.dvalue)

    @pl.loop(0, halves)
    def _(block):
        index = side * halves + block
        span = query_span(index, size)
        place = query_span(block, size)
        parts = attend_back(
            R.extra, R.gextra[:, span], span, index, R.att_extra[:, place], R.lse_extra[:, place]
        )
        R.dextra[0, :, span] = parts[0].astype(low)
        R.dkey[...] += parts[1]
        R.dvalue[...] += parts[2]

    R.dextra[1] = R.dkey[...].astype(low)
    R.dextra[2] = R.dvalue[...].astype(low)
    part_rows = row_block(pos // 2, head_dim)
    wait(copies)
    copies = to_places(
        14, lambda p: R.dextra.at[1:3, :, lane_block(p)], R.halves.at[side, :, part_rows, :]
    )
    pending = to_half(
        15, lambda p: R.dextra.at[0, :, lane_block(p)], R.dproject.at[0, extra_rows, :]
    )
    R.halves[side, :, part_rows, :] = R.dextra[1:3, :, lane_block(pos)]

    @pl.when(pos // half == side)
    def _():
        R.dproject[0, extra_rows, :] = R.dextra[0, :, lane_block(pos)]

    lower = lax.rem(level, 2)
    level_mate = me + 2 - 4 * lower
    upper_mate = me + 4 - 8 * upper

    modes = {
        "side": (side, {"blk": near}, lower, {"blk": level_mate}),
        "east": (east, {"dp": across}, lower, {"blk": level_mate}),
        "level": (lower, {"blk": level_mate}, side, {"blk": near}),
    }

    def shard(u, bit, other, mode):
        return row_block(4 * u + (2 * bit + other if mode == "level" else 2 * other + bit), channels)

    def sum_begin(kind, slot, source, span, mode):
        bit, mate, _, _ = modes[mode]
        return [
            send(
                kind,
                2 * u + v,
                R.in_w.at[shard(u, 1 - bit, v, mode), source],
                R.got_one.at[slot, 2 * u + v, :, span],
                mate,
            )
            for u in range(2)
            for v in range(2)
        ]

    def sum_next(kind, slot, source, span, mode, copies):
        wait(copies)
        bit, _, other, mate = modes[mode]
        for u in range(2):
            for v in range(2):
                own = R.in_w[shard(u, bit, v, mode), source]
                got = R.got_one[slot, 2 * u + v, :, span]
                R.sum_one[slot, 2 * u + v, :, span] = (own.astype(f32) + got.astype(f32)).astype(
                    low
                )
        return [
            send(
                kind,
                u,
                R.sum_one.at[slot, 2 * u + 1 - other, :, span],
                R.got_two.at[slot, u, :, span],
                mate,
            )
            for u in range(2)
        ]

    def sum_last(kind, slot, span, mode, copies):
        wait(copies)
        other = modes[mode][2]
        for u in range(2):
            own = R.sum_one[slot, 2 * u + other, :, span]
            got = R.got_two[slot, u, :, span]
            R.sum_two[slot, u, :, span] = (own.astype(f32) + got.astype(f32)).astype(low)
        return [
            send(
                kind,
                0,
                R.sum_two.at[slot, 1 - upper, :, span],
                R.got_three.at[slot, :, span],
                upper_mate,
            )
        ]

    def summed(slot, copies):
        wait(copies)
        return (R.sum_two[slot, upper].astype(f32) + R.got_three[slot].astype(f32)).astype(low)

    every = slice(0, width)
    in_span, out_span = chunk_of(0), chunk_of(1)
    stores = []

    def store(index, source, target):
        copy = pltpu.make_async_copy(source, target, R.store_sem.at[index])
        copy.start()
        stores.append(copy)

    blocks = length // size

    def main_back(block):
        span = query_span(block, size)
        parts = attend_back(
            R.main, R.gmain[:, span], span, block, R.att_main[:, span], R.lse_main[:, span]
        )
        R.dmain[0, :, span] = parts[0].astype(low)
        for place in range(size // LANES):
            target = block * (size // LANES) + place
            pl.when(target != pos)(query_copy(target).start)
        R.dkey[...] += parts[1]
        R.dvalue[...] += parts[2]

    def query_copy(target):
        step = lax.rem(target - pos + count, count)
        return pltpu.make_async_remote_copy(
            src_ref=R.dmain.at[0, :, lane_block(target)],
            dst_ref=R.dproject.at[0, own_rows, :],
            send_sem=R.out_sem.at[16, step],
            recv_sem=R.in_sem.at[16, step],
            device_id=device_at(target, upper),
            device_id_type=MESH,
        )

    R.dkey[...] = jnp.zeros_like(R.dkey)
    R.dvalue[...] = jnp.zeros_like(R.dvalue)
    share_forward(7, lanes_of(R.hidden_all), hidden_copies, facing)
    wait(two_copies)
    wait(act_copies)
    product = matmul_turned(R.act_all[...].reshape(width, -1), R.two_all[...])
    R.in_w[:, out_span] = product.astype(low)
    out_copies = sum_begin(18, 1, out_span, every, "level")
    pl.loop(0, blocks // 2)(main_back)
    wait(hidden_copies)
    wait(pre_copies)
    R.in_w[:, in_span] = matmul_turned(R.hidden_all[...], R.pre_all[...]).astype(low)
    in_copies = sum_begin(17, 0, in_span, every, "east")
    pl.loop(blocks // 2, blocks)(main_back)
    R.dmain[1] = R.dkey[...].astype(low)
    R.dmain[2] = R.dvalue[...].astype(low)
    copies += to_places(
        44, lambda p: R.dmain.at[1:3, :, lane_block(p)], R.dproject.at[1:3, own_rows, :]
    )
    copies += [query_copy(peer(pos, step, count)) for step in range(1, count)]
    R.dproject[0:3, own_rows, :] = R.dmain[:, :, lane_block(pos)]
    out_copies = sum_next(23, 1, out_span, every, "level", out_copies)
    wait(copies)
    wait_some(pending)
    first = half * head_dim
    for which in range(2):
        total = R.halves[0, which].astype(f32) + R.halves[1, which].astype(f32)
        R.dproject[1 + which, width - first :, :] = total.astype(low)

    late = to_rows(19, lambda p: R.dproject.at[p], R.late_right.at[:, lane_block(row)])
    R.late_right[:, lane_block(row)] = R.dproject[row]
    grad_mixed = R.mixed[...]
    for part in range(3):
        block = R.dproject[part].astype(f32).T
        if part != 1:
            R.small[1 + part // 2, :] = jnp.sum(block, axis=0)
        grad_mixed = grad_mixed + matmul_turned(block.astype(low), R.qkv_w[:, chunk_of(part)])
    R.mixed_here[...] = grad_mixed.astype(low)
    grad_conv = (grad_mixed * R.slope[...]).astype(low)
    R.conv_turned[...] = turned(grad_conv)
    conv_pending = from_level(
        20, lambda b: R.conv_turned.at[row_block(b, channels), :], R.gcol.at[:, lane_block(pos + 1)]
    )
    R.small[0, :] = jnp.sum(grad_conv.astype(f32), axis=0)
    small_copy = send(21, 0, R.small, R.small_got.at[0], twin, "dp")
    in_copies = sum_next(22, 0, in_span, every, "east", in_copies)
    out_copies = sum_last(37, 1, every, "level", out_copies)
    wait(late)
    wait_some(left_pending)
    product = matmul_turned(R.late_left[...], R.late_right[...])
    R.in_w[:, chunk_of(2)] = product.astype(low)
    middle = width // 2
    parts = (
        (26, slice(2 * width, 2 * width + middle), slice(0, middle), "side"),
        (28, slice(2 * width + middle, 3 * width), slice(middle, width), "level"),
    )
    att_copies = [sum_begin(kind, 2, source, span, first) for kind, source, span, first in parts]
    wait_some(conv_pending)
    mixed_pending = move(36, R.mixed_here, R.mixed_got, from_level_device)

    @pl.loop(0, groups)
    def _(group):
        rows = row_block(group, group_width)
        spread_taps(R.gcol[rows, :].astype(f32), LANES // 2, -1, R.stage, R.taps.at[group])

    quarter = channels // rows_count

    @pl.loop(0, groups)
    def _(group):
        grad = matmul_turned(R.shifted[group], R.taps[group])
        for block in range(group_width // steps):
            span = slice(block * LANES, (block + 1) * LANES)
            tiles = [
                grad[a * group_width : (a + 1) * group_width, span] for a in range(steps)
            ]
            for u, tile in enumerate(swap_blocks(tiles, TAP_STEP)):
                channel = block * steps + u
                R.conv_part[group, channel // quarter, channel % quarter] = tile.astype(low)
    conv_copy = send(25, 0, R.conv_part.at[:, 1 - core], R.conv_got, twin, "dp")
    in_copies = sum_last(38, 0, every, "east", in_copies)
    def slots_of(ref):
        return lambda index: ref.at[index]

    R.out_sums[row] = summed(1, out_copies)
    out_share = share_start(43, slots_of(R.out_sums))
    @pl.loop(0, groups)
    def _(group):
        rows = row_block(group, group_width)
        product = dot(R.mix_back[group], R.taps[group])
        total = product[:group_width, LANES:]
        for a in range(1, steps):
            part = product[a * group_width : (a + 1) * group_width, :]
            total = total + pltpu.roll(part, a * TAP_STEP, 1)[:, LANES:]
        R.result[rows, :] = total.astype(low)
    back = to_blocks(
        24, lambda p: R.result.at[:, lane_block(p)], R.back_home.at[row_block(me, channels), :]
    )
    R.back_home[row_block(me, channels), :] = R.result[:, lane_block(me)]
    conv_copy.wait()
    for part in range(2):
        R.conv_sum[part] = (
            R.conv_part[part, core].astype(f32) + R.conv_got[part].astype(f32)
        ).astype(low)
    conv_copy = send(25, 1, R.conv_sum.at[1 - row // 2], R.conv_far, across, "dp")
    att_copies = [
        sum_next(kind + 1, 2, source, span, first, copies)
        for (kind, source, span, first), copies in zip(parts, att_copies)
    ]
    small_copy.wait()
    R.small_sum[0] = R.small[...] + R.small_got[0]
    small_copy = send(21, 1, R.small_sum.at[0], R.small_got.at[1], across, "dp")
    settled = side == east
    R.in_part[...] = summed(0, in_copies)

    def in_send(step, source, slot, device):
        return pltpu.make_async_remote_copy(
            src_ref=source,
            dst_ref=R.in_sums.at[slot],
            send_sem=R.out_sem.at[40, step],
            recv_sem=R.in_sem.at[40, step],
            device_id=device,
            device_id_type=MESH,
        )

    in_near = in_send(0, R.in_part, corner, {"blk": near})
    in_far = [
        in_send(1 + n, R.in_sums.at[slot], slot, {"dp": across})
        for n, slot in enumerate((corner, facing))
    ]

    @pl.when(jnp.logical_not(settled))
    def _():
        in_near.start()

    @pl.when(settled)
    def _():
        R.in_sums[corner] = R.in_part[...]
        in_far[0].start()

    small_copy.wait()
    R.small_sum[1] = R.small_sum[0] + R.small_got[1]
    small_copy = send(21, 2, R.small_sum.at[1], R.small_got.at[2], near)

    att_copies = [
        sum_last(kind + 13, 2, span, first, copies)
        for (kind, source, span, first), copies in zip(parts, att_copies)
    ]
    share_forward(43, slots_of(R.out_sums), out_share)
    wait(back)
    wait_some(mixed_pending)
    R.frames_done[...] = (
        R.mixed_got[...].astype(f32) + (R.back_home[...].astype(f32) * valid).T
    ).astype(low)
    store(0, R.frames_done, R.frames_out)
    wait_some(layer_pending)
    store(1, R.layer_got, R.layer_out)
    conv_copy.wait()
    R.conv_sums[row] = (
        R.conv_sum[row // 2].astype(f32) + R.conv_far[...].astype(f32)
    ).astype(low)
    conv_share = share_start(42, slots_of(R.conv_sums))
    @pl.when(settled)
    def _():
        in_near.wait_recv()
        in_far[1].start()

    small_copy.wait()
    R.small_far[level] = R.small_sum[1] + R.small_got[2]
    smalls = []
    for step in range(1, levels):
        target = 2 * peer(level, step, levels) + side
        smalls.append(
            send(30, step, R.small_far.at[level], R.small_far.at[level], target)
        )

    R.attn_sums[row] = summed(2, att_copies[0] + att_copies[1])
    att_share = share_start(31, slots_of(R.attn_sums))
    share_forward(42, slots_of(R.conv_sums), conv_share)
    wait(smalls)
    R.small_done[...] = sum_parts(R.small_far)
    store(2, R.small_done, R.small_out)

    @pl.when(settled)
    def _():
        in_far[0].wait_send()
        in_far[1].wait_send()

    @pl.when(jnp.logical_not(settled))
    def _():
        in_near.wait_send()
        in_far[0].wait_recv()
        in_far[1].wait_recv()

    in_share = [
        send(40, 3 + n, R.in_sums.at[slot], R.in_sums.at[slot], twin, "dp")
        for n, slot in enumerate((corner, facing))
    ]
    wait(out_share)
    store(3, R.out_sums, R.back_out)
    wait(in_share)
    store(6, R.in_sums, R.in_out)
    wait(conv_share)
    store(4, R.conv_sums, R.conv_out)
    share_forward(31, slots_of(R.attn_sums), att_share)
    wait(att_share)
    store(5, R.attn_sums, R.attn_out)
    for copy in stores:
        copy.wait()


VECTORS = (
    "conv_bias",
    "qv_bias",
    "out_bias",
    "gain_one",
    "shift_one",
    "in_bias",
    "back_bias",
    "gain_two",
    "shift_two",
)


def layer(count, rows_count, head_dim, named):
    low, f32 = jnp.bfloat16, jnp.float32
    tokens, width = named["frames_hbm"].shape
    wide = named["in_hbm"].shape[1]
    _, group_width, kernel = named["conv_hbm"].shape
    channels = width // count
    groups = channels // group_width
    length = count * LANES
    span = length + LANES
    steps = kernel // TAP_STEP
    taps = group_width * TAP_STEP
    every = rows_count * tokens
    piece = channels // rows_count
    extras = count // 2 * head_dim
    levels = count // 2
    outs = {
        "layer_out": ((tokens, width), low),
        "frames_out": ((tokens, width), low),
        "conv_out": ((rows_count, piece, group_width, kernel), low),
        "in_out": ((rows_count, channels, width), low),
        "back_out": ((rows_count, channels, width), low),
        "attn_out": ((rows_count, channels, width), low),
        "small_out": ((16, width), f32),
    }
    scratch = {
        "qkv_w": (named["qkv_hbm"].shape, low),
        "out_w": (named["out_hbm"].shape, low),
        "in_w": (named["in_hbm"].shape, low),
        "back_w": (named["back_hbm"].shape, low),
        "table": ((16, width), f32),
        "small": ((16, width), f32),
        "small_got": ((3, 16, width), f32),
        "small_sum": ((2, 16, width), f32),
        "small_far": ((levels, 16, width), f32),
        "turned": ((width, tokens), low),
        "conv_turned": ((width, tokens), low),
        "column": ((channels, span + LANES), low),
        "gcol": ((channels, span + LANES), low),
        "segs": ((count, 1, LANES), jnp.int32),
        "clip": ((length, LANES), f32),
        "stage": ((span // LANES * taps, LANES), f32),
        "own_weight": ((channels, group_width, kernel), low),
        "frames_home": ((tokens, width), low),
        "frames": ((tokens, width), low),
        "cotangent": ((tokens, width), low),
        "cotangent_home": ((tokens, width), low),
        "layer_here": ((tokens, width), low),
        "mixed_here": ((tokens, width), low),
        "mixed_got": ((tokens, width), low),
        "taps": ((groups, taps, span), low),
        "mix": ((groups, steps * group_width, taps), low),
        "mix_back": ((groups, steps * group_width, taps), low),
        "shifted": ((groups, steps * group_width, span), low),
        "result": ((channels, length), low),
        "conv_home": ((width, tokens), low),
        "back_home": ((width, tokens), low),
        "slope": ((tokens, width), f32),
        "mixed": ((tokens, width), f32),
        "project": ((3, width, tokens), low),
        "main": ((3, head_dim, length), low),
        "extra": ((3, head_dim, length), low),
        "att_main": ((head_dim, length), f32),
        "att_extra": ((head_dim, length // 2), f32),
        "low_main": ((head_dim, length), low),
        "low_extra": ((head_dim, length), low),
        "lse_main": ((1, length), f32),
        "lse_extra": ((1, length // 2), f32),
        "att_home": ((width, tokens), low),
        "keep": ((tokens, wide), f32),
        "total": ((tokens, width), f32),
        "dkey": ((head_dim, length), f32),
        "dvalue": ((head_dim, length), f32),
        "left": ((2, width, tokens), low),
        "act_turned": ((count, rows_count, wide // (count * rows_count), tokens), low),
        "pre_turned": ((rows_count, width, tokens), low),
        "hidden_all": ((width, every), low),
        "two_all": ((width, every), low),
        "pre_all": ((width, every), low),
        "act_all": ((count, wide // (count * rows_count), every), low),
        "late_left": ((width, every), low),
        "late_right": ((width, every), low),
        "gmain": ((head_dim, length), low),
        "gextra": ((head_dim, length), low),
        "dmain": ((3, head_dim, length), low),
        "dextra": ((3, head_dim, length), low),
        "dproject": ((4, width, tokens), low),
        "halves": ((2, 2, extras, tokens), low),
        "got_one": ((3, 4, channels, width), low),
        "sum_one": ((3, 4, channels, width), low),
        "got_two": ((3, 2, channels, width), low),
        "sum_two": ((3, 2, channels, width), low),
        "got_three": ((3, channels, width), low),
        "layer_got": ((tokens, width), low),
        "frames_done": ((tokens, width), low),
        "small_done": ((16, width), f32),
        "in_sums": ((rows_count, channels, width), low),
        "in_part": ((channels, width), low),
        "out_sums": ((rows_count, channels, width), low),
        "conv_sums": ((rows_count, piece, group_width, kernel), low),
        "attn_sums": ((rows_count, channels, width), low),
        "conv_part": ((2, 2, piece, group_width, kernel), low),
        "conv_got": ((2, piece, group_width, kernel), low),
        "conv_sum": ((2, piece, group_width, kernel), low),
        "conv_far": ((piece, group_width, kernel), low),
    }
    hbm = pl.BlockSpec(memory_space=pl.ANY)
    names = (*named, *outs, *scratch, "out_sem", "in_sem", "load_sem", "store_sem", "first_sem")
    return pl.pallas_call(
        functools.partial(layer_kernel, names, count, rows_count, head_dim),
        out_shape=tuple(jax.ShapeDtypeStruct(*out) for out in outs.values()),
        in_specs=[hbm if name.endswith("_hbm") else VMEM for name in named],
        out_specs=(hbm,) * len(outs),
        scratch_shapes=[pltpu.VMEM(*item) for item in scratch.values()]
        + [
            pltpu.SemaphoreType.DMA((45, count)),
            pltpu.SemaphoreType.DMA((45, count)),
            pltpu.SemaphoreType.DMA((3 + 2 * (wide // width),)),
            pltpu.SemaphoreType.DMA((len(outs),)),
            pltpu.SemaphoreType.DMA((2,)),
        ],
        compiler_params=pltpu.CompilerParams(
            collective_id=0, has_side_effects=True, vmem_limit_bytes=62 * 2**20
        ),
        name="layer",
    )(*named.values())


def unpack_kernel(
    count,
    layer_hbm,
    frames_hbm,
    conv_hbm,
    in_hbm,
    back_hbm,
    attn_hbm,
    small_hbm,
    layer_out,
    frames_out,
    conv_out,
    conv_bias,
    qkv_out,
    qv_bias,
    out_out,
    out_bias,
    gain_one,
    shift_one,
    in_out,
    in_bias,
    back_out,
    back_bias,
    gain_two,
    shift_two,
    conv_wide,
    qkv_wide,
    out_wide,
    in_wide,
    back_wide,
    conv_ref,
    in_ref,
    back_ref,
    attn_ref,
    small_ref,
    layer_ref,
    frames_ref,
    spare,
    sems,
):
    f32 = jnp.float32
    me = lax.axis_index("blk")
    rows_count, channels, width = attn_ref.shape
    piece = conv_ref.shape[1]
    copies = []

    def start(source, target):
        copy = pltpu.make_async_copy(source, target, sems.at[len(copies)])
        copy.start()
        copies.append(copy)

    loads = [
        pltpu.make_async_copy(source, target, sems.at[6 + rows_count + i])
        for i, (source, target) in enumerate(
            (
                (conv_hbm, conv_ref),
                (in_hbm, in_ref),
                (back_hbm, back_ref),
                (attn_hbm, attn_ref),
                (small_hbm, small_ref),
                (layer_hbm, layer_ref),
                (frames_hbm, frames_ref),
            )
        )
    ]
    for load in loads:
        load.start()
    loads[0].wait()
    for row in range(rows_count):
        part = slice(row * piece, (row + 1) * piece)
        conv_wide[part] = conv_ref[row].astype(f32)
        start(conv_wide.at[part], conv_out.at[part])
    loads[1].wait()
    for row in range(rows_count):
        in_wide[:, row * width : (row + 1) * width] = in_ref[row].astype(f32)
    start(in_wide, in_out)
    loads[2].wait()
    for row in range(rows_count):
        back_wide[row * channels : (row + 1) * channels, :] = back_ref[row].astype(f32)
    start(back_wide, back_out)
    loads[3].wait()
    for row in range(rows_count - 1):
        qkv_wide[:, row * width : (row + 1) * width] = attn_ref[row].astype(f32)
    start(qkv_wide, qkv_out)
    out_wide[...] = attn_ref[rows_count - 1].astype(f32)
    start(out_wide, out_out)
    loads[5].wait()
    start(layer_ref, layer_out)
    loads[6].wait()
    start(frames_ref, frames_out)
    loads[4].wait()
    small = small_ref[...]
    own = pltpu.roll(small, lax.rem(width - channels * me, width), 1)
    for place, ref in (
        (0, conv_bias),
        (3, out_bias),
        (4, gain_one),
        (5, shift_one),
        (10, back_bias),
        (11, gain_two),
        (12, shift_two),
    ):
        ref[...] = own[place, :channels]
    for first, parts, ref in ((1, 2, qv_bias), (6, rows_count, in_bias)):
        size = parts * channels
        inside = count // parts
        spare[...] = pltpu.roll(small, lax.rem(width - size * lax.rem(me, inside), width), 1)
        ref[...] = spare[pl.ds(first + me // inside, 1), :][0, :size]
    for copy in copies:
        copy.wait()


def unpack(count, layer_out, frames_out, conv, ffn_in, ffn_out, attn, small):
    rows_count, channels, width = attn.shape
    piece, group_width, kernel = conv.shape[1:]
    f32 = jnp.float32
    hbm = pl.BlockSpec(memory_space=pl.ANY)
    vector = jax.ShapeDtypeStruct((channels,), f32)
    conv_type = jax.ShapeDtypeStruct((rows_count * piece, group_width, kernel), f32)
    qkv_type = jax.ShapeDtypeStruct((channels, (rows_count - 1) * width), f32)
    out_type = jax.ShapeDtypeStruct((channels, width), f32)
    in_type = jax.ShapeDtypeStruct((channels, rows_count * width), f32)
    back_type = jax.ShapeDtypeStruct((rows_count * channels, width), f32)
    results = pl.pallas_call(
        functools.partial(unpack_kernel, count),
        out_shape=(
            jax.ShapeDtypeStruct(layer_out.shape, layer_out.dtype),
            jax.ShapeDtypeStruct(frames_out.shape, frames_out.dtype),
            conv_type,
            vector,
            qkv_type,
            jax.ShapeDtypeStruct((2 * channels,), f32),
            out_type,
            vector,
            vector,
            vector,
            in_type,
            jax.ShapeDtypeStruct((rows_count * channels,), f32),
            back_type,
            vector,
            vector,
            vector,
        ),
        in_specs=[hbm] * 7,
        out_specs=(
            hbm,
            hbm,
            hbm,
            VMEM,
            hbm,
            VMEM,
            hbm,
            VMEM,
            VMEM,
            VMEM,
            hbm,
            VMEM,
            hbm,
            VMEM,
            VMEM,
            VMEM,
        ),
        scratch_shapes=[
            pltpu.VMEM(item.shape, f32)
            for item in (conv_type, qkv_type, out_type, in_type, back_type)
        ]
        + [pltpu.VMEM(item.shape, item.dtype) for item in (conv, ffn_in, ffn_out, attn, small, layer_out, frames_out)]
        + [pltpu.VMEM(small.shape, f32), pltpu.SemaphoreType.DMA((13 + rows_count,))],
        compiler_params=pltpu.CompilerParams(vmem_limit_bytes=62 * 2**20),
        name="unpack",
    )(layer_out, frames_out, conv, ffn_in, ffn_out, attn, small)
    return (results[0][None], results[1][None], *results[2:])


def shards(sizes, *arrays):
    frames, segment, conv_weight = arrays[:3]
    row_count, block_len, model_width = frames.shape
    group_width, kernel = conv_weight.shape[1:]
    count = sizes["blk"]
    head_dim = model_width // HEADS
    channels = model_width // count
    fits = (
        row_count == 1
        and block_len == LANES
        and kernel == LANES
        and channels % group_width == 0
        and group_width % TAP_STEP == 0
        and count % 4 == 0
        and 2 * HEADS == 3 * count
        and head_dim % TAP_STEP == 0
        and sizes["dp"] == 4
        and count % sizes["dp"] == 0
        and arrays[10].shape[1] == 4 * model_width
    )
    if fits:
        return swap_shards(count, sizes["dp"], *arrays)
    return ring_shards(*arrays)


def swap_shards(
    count,
    rows_count,
    frames,
    segment,
    conv_weight,
    conv_bias,
    qkv_weight,
    qv_bias,
    out_weight,
    out_bias,
    norm1_gain,
    norm1_bias,
    ffn_in,
    ffn_in_bias,
    ffn_out,
    ffn_out_bias,
    norm2_gain,
    norm2_bias,
    cotangent,
):
    named = {
        "frames_hbm": frames[0],
        "segment": segment,
        "cotangent_hbm": cotangent[0],
        "conv_bias": conv_bias,
        "qv_bias": qv_bias,
        "out_bias": out_bias,
        "gain_one": norm1_gain,
        "shift_one": norm1_bias,
        "in_bias": ffn_in_bias,
        "back_bias": ffn_out_bias,
        "gain_two": norm2_gain,
        "shift_two": norm2_bias,
        "conv_hbm": conv_weight,
        "qkv_hbm": qkv_weight,
        "out_hbm": out_weight,
        "in_hbm": ffn_in,
        "back_hbm": ffn_out,
    }
    width = frames.shape[2]
    results = layer(count, rows_count, width // HEADS, named)
    return unpack(count, *results)


def solution(mesh):
    return jax.shard_map(
        functools.partial(shards, mesh.shape),
        mesh=mesh,
        in_specs=(
            P("dp", "blk", None),
            P("dp", "blk"),
            P(),
            P(),
            P(),
            P(),
            P(),
            P(),
            P(),
            P(),
            P(),
            P(),
            P(),
            P(),
            P(),
            P(),
            P("dp", "blk", None),
        ),
        out_specs=(
            P("dp", "blk", None),
            P("dp", "blk", None),
            P("blk", None, None),
            P("blk"),
            P("blk", None),
            P("blk"),
            P("blk", None),
            P("blk"),
            P("blk"),
            P("blk"),
            P("blk", None),
            P("blk"),
            P("blk", None),
            P("blk"),
            P("blk"),
            P("blk"),
        ),
        check_vma=False,
    )
```

```python
import functools
import math
import types

import jax
import jax.numpy as jnp
from jax import lax
from jax.experimental import pallas as pl
from jax.experimental.pallas import tpu as pltpu
from jax.sharding import PartitionSpec as P

HEADS = 12
GROUPS = 16


EPS = 1e-05
ROOT_HALF = 0.7071067811865476
DENSITY_CONST = 0.3989422804014327


def with_halo(x, sides, width):
    for axis, dim in sides:
        size, length = (lax.axis_size(axis), x.shape[dim])
        up = [(i, (i + 1) % size) for i in range(size - 1)]
        down = [(j, i) for i, j in up]
        last = lax.slice_in_dim(x, length - width, length, axis=dim)
        initial = lax.slice_in_dim(x, 0, width, axis=dim)
        before = lax.ppermute(last, axis, up)
        after = lax.ppermute(initial, axis, down)
        x = jnp.concatenate([before, x, after], axis=dim)
    return x


def from_behind(value, axis, steps):
    count = lax.axis_size(axis)
    pairs = [(source, (source + steps) % count) for source in range(count)]
    return lax.ppermute(value, axis, pairs)


def gelu_value(signal):
    return 0.5 * signal * (1.0 + lax.erf(signal * ROOT_HALF))


def gelu_slope(signal):
    return (
        0.5 * (1.0 + lax.erf(signal * ROOT_HALF))
        + signal * jnp.exp(-0.5 * signal * signal) * DENSITY_CONST
    )


def norm_forward(signal, gain_vec, shift_vec):
    average = jnp.mean(signal, axis=-1, keepdims=True)
    centred = signal - average
    inv_std = lax.rsqrt(jnp.mean(centred * centred, axis=-1, keepdims=True) + EPS)
    normed = centred * inv_std
    return (normed * gain_vec + shift_vec, normed, inv_std)


def norm_backward(grad_in, normed, inv_std, gain_vec):
    scaled = grad_in * gain_vec
    result = inv_std * (
        scaled
        - jnp.mean(scaled, axis=-1, keepdims=True)
        - normed * jnp.mean(scaled * normed, axis=-1, keepdims=True)
    )
    return (result, jnp.sum(grad_in * normed, axis=0), jnp.sum(grad_in, axis=0))


def block_grads(
    query_h, dout_h, query_seg, log_tot, row_delta, key_h, value_h, key_seg, score_scale
):
    scores = (
        jnp.einsum("rqhc,rkhc->rhqk", query_h, key_h, preferred_element_type=jnp.float32)
        * score_scale
    )
    same_seg = (query_seg[:, :, None] == key_seg[:, None, :])[:, None]
    weights_f = jnp.where(same_seg, jnp.exp(scores - log_tot[..., None]), 0.0)
    grad_prob = jnp.einsum("rqhc,rkhc->rhqk", dout_h, value_h, preferred_element_type=jnp.float32)
    grad_score = (weights_f * (grad_prob - row_delta[..., None])).astype(jnp.bfloat16)
    query_part = score_scale * jnp.einsum(
        "rhqk,rkhc->rqhc", grad_score, key_h, preferred_element_type=jnp.float32
    )
    key_part = score_scale * jnp.einsum(
        "rhqk,rqhc->rkhc", grad_score, query_h, preferred_element_type=jnp.float32
    )
    value_part = jnp.einsum(
        "rhqk,rqhc->rkhc",
        weights_f.astype(jnp.bfloat16),
        dout_h,
        preferred_element_type=jnp.float32,
    )
    return (query_part, key_part, value_part)


def ring_shards(
    frames,
    segment,
    conv_weight,
    conv_bias,
    qkv_weight,
    qv_bias,
    out_weight,
    out_bias,
    norm1_gain,
    norm1_bias,
    ffn_in,
    ffn_in_bias,
    ffn_out,
    ffn_out_bias,
    norm2_gain,
    norm2_bias,
    cotangent,
):
    row_count, block_len, model_width = frames.shape
    token_count = row_count * block_len
    group_width = conv_weight.shape[1]
    kernel = conv_weight.shape[2]
    half_kernel = kernel // 2
    head_dim = model_width // HEADS
    score_scale = head_dim ** (-0.5)
    cycle_len = lax.axis_size("blk")
    is_valid = segment >= 0
    masked = jnp.where(is_valid[..., None], frames, jnp.zeros_like(frames))
    padded = with_halo(masked, (("blk", 1),), half_kernel)
    conv_out = lax.conv_general_dilated(
        padded,
        conv_weight,
        (1,),
        "VALID",
        dimension_numbers=("NWC", "OIW", "NWC"),
        feature_group_count=GROUPS,
        preferred_element_type=jnp.float32,
    )
    pre_conv = conv_out[:, :block_len].reshape(token_count, model_width) + conv_bias.astype(
        jnp.float32
    )
    mixed_in = frames.reshape(token_count, model_width).astype(jnp.float32) + gelu_value(pre_conv)
    mixed_low = mixed_in.astype(jnp.bfloat16)
    pair_bias = qv_bias.astype(jnp.float32)
    zero_bias = jnp.zeros((model_width,), jnp.float32)
    full_bias = jnp.concatenate([pair_bias[:model_width], zero_bias, pair_bias[model_width:]])
    project = (
        jnp.dot(mixed_low, qkv_weight, preferred_element_type=jnp.float32) + full_bias
    ).astype(jnp.bfloat16)
    project = project.reshape(row_count, block_len, 3 * model_width)
    query_heads = project[..., :model_width].reshape(row_count, block_len, HEADS, head_dim)
    keys_local = project[..., model_width : 2 * model_width]
    values_local = project[..., 2 * model_width :]
    key_heads = keys_local.reshape(row_count, block_len, HEADS, head_dim)
    value_heads = values_local.reshape(row_count, block_len, HEADS, head_dim)
    query_seg = segment.astype(jnp.bfloat16)
    start_carry = (
        jnp.full((row_count, HEADS, block_len), -1e30, jnp.float32),
        jnp.zeros((row_count, HEADS, block_len), jnp.float32),
        jnp.zeros((row_count, HEADS, block_len, head_dim), jnp.float32),
    )
    key_piece = lax.all_gather(keys_local, "blk", axis=1, tiled=True)
    value_piece = lax.all_gather(values_local, "blk", axis=1, tiled=True)
    seg_piece = lax.all_gather(query_seg, "blk", axis=1, tiled=True)
    piece_len = key_piece.shape[1]
    block_size = math.gcd(piece_len, 512)

    def one_block(block_index, inner_carry):
        running_max, denominator, numerator = inner_carry
        offset = block_index * block_size
        key_block = lax.dynamic_slice_in_dim(key_piece, offset, block_size, 1).reshape(
            row_count, block_size, HEADS, head_dim
        )
        value_block = lax.dynamic_slice_in_dim(value_piece, offset, block_size, 1).reshape(
            row_count, block_size, HEADS, head_dim
        )
        seg_block = lax.dynamic_slice_in_dim(seg_piece, offset, block_size, 1)
        scores = (
            jnp.einsum(
                "rqhc,rkhc->rhqk", query_heads, key_block, preferred_element_type=jnp.float32
            )
            * score_scale
        )
        same_seg = (query_seg[:, :, None] == seg_block[:, None, :])[:, None]
        masked_scores = jnp.where(same_seg, scores, -1e30)
        new_max = jnp.maximum(running_max, jnp.max(masked_scores, axis=-1))
        weights_f = jnp.where(same_seg, jnp.exp(masked_scores - new_max[..., None]), 0.0)
        rescale = jnp.exp(running_max - new_max)
        denominator = denominator * rescale + jnp.sum(weights_f, axis=-1)
        numerator = numerator * rescale[..., None] + jnp.einsum(
            "rhqk,rkhc->rhqc",
            weights_f.astype(jnp.bfloat16),
            value_block,
            preferred_element_type=jnp.float32,
        )
        return (new_max, denominator, numerator)

    running_max, denominator, numerator = lax.fori_loop(
        0, piece_len // block_size, one_block, start_carry
    )
    log_total = running_max + jnp.log(denominator)
    attended_heads = (numerator / denominator[..., None]).transpose(0, 2, 1, 3)
    attended = attended_heads.reshape(token_count, model_width)
    attn_low = attended.astype(jnp.bfloat16)
    branch = jnp.dot(attn_low, out_weight, preferred_element_type=jnp.float32) + out_bias.astype(
        jnp.float32
    )
    gain_one = norm1_gain.astype(jnp.float32)
    hidden_norm, normed_one, inv_one = norm_forward(
        mixed_in + branch, gain_one, norm1_bias.astype(jnp.float32)
    )
    hidden_low = hidden_norm.astype(jnp.bfloat16)
    ffn_pre = jnp.dot(hidden_low, ffn_in, preferred_element_type=jnp.float32) + ffn_in_bias.astype(
        jnp.float32
    )
    ffn_act = gelu_value(ffn_pre).astype(jnp.bfloat16)
    ffn_branch = jnp.dot(
        ffn_act, ffn_out, preferred_element_type=jnp.float32
    ) + ffn_out_bias.astype(jnp.float32)
    gain_two = norm2_gain.astype(jnp.float32)
    layer_out, normed_two, inv_two = norm_forward(
        hidden_norm + ffn_branch, gain_two, norm2_bias.astype(jnp.float32)
    )
    grad_top = cotangent.reshape(token_count, model_width).astype(jnp.float32)
    grad_second, norm2_gain_grad, norm2_bias_grad = norm_backward(
        grad_top, normed_two, inv_two, gain_two
    )
    grad_branch_two = grad_second.astype(jnp.bfloat16)
    ffn_out_grad = jnp.einsum(
        "nf,nd->fd", ffn_act, grad_branch_two, preferred_element_type=jnp.float32
    )
    ffn_out_bias_grad = jnp.sum(grad_branch_two.astype(jnp.float32), axis=0)
    grad_act = jnp.einsum("nd,fd->nf", grad_branch_two, ffn_out, preferred_element_type=jnp.float32)
    grad_pre = (grad_act * gelu_slope(ffn_pre)).astype(jnp.bfloat16)
    ffn_in_grad = jnp.einsum("nd,nf->df", hidden_low, grad_pre, preferred_element_type=jnp.float32)
    ffn_in_bias_grad = jnp.sum(grad_pre.astype(jnp.float32), axis=0)
    grad_hidden = grad_second + jnp.einsum(
        "nf,df->nd", grad_pre, ffn_in, preferred_element_type=jnp.float32
    )
    grad_first, norm1_gain_grad, norm1_bias_grad = norm_backward(
        grad_hidden, normed_one, inv_one, gain_one
    )
    grad_branch = grad_first.astype(jnp.bfloat16)
    out_weight_grad = jnp.einsum(
        "ne,nd->ed", attn_low, grad_branch, preferred_element_type=jnp.float32
    )
    out_bias_grad = jnp.sum(grad_branch.astype(jnp.float32), axis=0)
    grad_att = jnp.einsum("nd,ed->ne", grad_branch, out_weight, preferred_element_type=jnp.float32)
    grad_heads = grad_att.astype(jnp.bfloat16).reshape(row_count, block_len, HEADS, head_dim)
    row_delta = jnp.einsum("rqhc,rqhc->rhq", grad_heads.astype(jnp.float32), attended_heads)
    zero_heads = jnp.zeros((row_count, block_len, HEADS, head_dim), jnp.float32)

    def key_step(carried):
        key_block, value_block, seg_block, key_grad, value_grad, query_grad = carried
        query_part, key_part, value_part = block_grads(
            query_heads,
            grad_heads,
            query_seg,
            log_total,
            row_delta,
            key_block,
            value_block,
            seg_block,
            score_scale,
        )
        query_grad = query_grad + query_part
        key_grad = key_grad + key_part
        value_grad = value_grad + value_part
        key_block, value_block, seg_block = from_behind(
            (key_block, value_block, seg_block), "blk", 1
        )
        key_grad, value_grad = (
            from_behind(key_grad.astype(jnp.bfloat16), "blk", 1).astype(key_grad.dtype),
            from_behind(value_grad.astype(jnp.bfloat16), "blk", 1).astype(value_grad.dtype),
        )
        return (key_block, value_block, seg_block, key_grad, value_grad, query_grad)

    def four_steps(turn_index, carried):
        for repeat in range(4):
            carried = key_step(carried)
        return carried

    final_state = lax.fori_loop(
        0,
        cycle_len // 4,
        four_steps,
        (key_heads, value_heads, query_seg, zero_heads, zero_heads, zero_heads),
    )
    key_grad, value_grad, query_grad = (final_state[3], final_state[4], final_state[5])
    grad_project = jnp.concatenate(
        [
            query_grad.reshape(token_count, model_width),
            key_grad.reshape(token_count, model_width),
            value_grad.reshape(token_count, model_width),
        ],
        axis=1,
    ).astype(jnp.bfloat16)
    qkv_weight_grad = jnp.einsum(
        "nd,ne->de", mixed_low, grad_project, preferred_element_type=jnp.float32
    )
    bias_sums = jnp.sum(grad_project.astype(jnp.float32), axis=0)
    qv_bias_grad = jnp.concatenate([bias_sums[:model_width], bias_sums[2 * model_width :]])
    grad_mixed = grad_first + jnp.einsum(
        "ne,de->nd", grad_project, qkv_weight, preferred_element_type=jnp.float32
    )
    grad_conv = (grad_mixed * gelu_slope(pre_conv)).astype(jnp.bfloat16)
    conv_bias_grad = jnp.sum(grad_conv.astype(jnp.float32), axis=0)
    grad_conv_rows = grad_conv.reshape(row_count, block_len, model_width)
    grad_padded = with_halo(grad_conv_rows, (("blk", 1),), half_kernel)
    flipped = conv_weight.reshape(GROUPS, group_width, group_width, kernel).transpose(0, 2, 1, 3)
    flipped = flipped.reshape(model_width, group_width, kernel)[:, :, ::-1]
    back_conv = lax.conv_general_dilated(
        grad_padded,
        flipped,
        (1,),
        "VALID",
        dimension_numbers=("NWC", "OIW", "NWC"),
        feature_group_count=GROUPS,
        preferred_element_type=jnp.float32,
    )[:, 1:]
    frames_grad = (
        grad_mixed.reshape(row_count, block_len, model_width)
        + jnp.where(is_valid[..., None], back_conv, 0.0)
    ).astype(jnp.bfloat16)
    conv_weight_grad = lax.conv_general_dilated(
        padded,
        grad_conv_rows,
        (1,),
        "VALID",
        dimension_numbers=("CWN", "IWO", "CNW"),
        batch_group_count=GROUPS,
        preferred_element_type=jnp.float32,
    )[:, :, :kernel]
    (
        conv_weight_part,
        conv_bias_part,
        qkv_weight_part,
        qv_bias_part,
        out_weight_part,
        out_bias_part,
        gain_one_part,
        shift_one_part,
        ffn_in_part,
        ffn_in_bias_part,
        ffn_out_part,
        ffn_out_bias_part,
        gain_two_part,
        shift_two_part,
    ) = (
        lax.psum_scatter(conv_weight_grad, "blk", scatter_dimension=0, tiled=True),
        lax.psum_scatter(conv_bias_grad, "blk", scatter_dimension=0, tiled=True),
        lax.psum_scatter(qkv_weight_grad, "blk", scatter_dimension=0, tiled=True),
        lax.psum_scatter(qv_bias_grad, "blk", scatter_dimension=0, tiled=True),
        lax.psum_scatter(out_weight_grad, "blk", scatter_dimension=0, tiled=True),
        lax.psum_scatter(out_bias_grad, "blk", scatter_dimension=0, tiled=True),
        lax.psum_scatter(norm1_gain_grad, "blk", scatter_dimension=0, tiled=True),
        lax.psum_scatter(norm1_bias_grad, "blk", scatter_dimension=0, tiled=True),
        lax.psum_scatter(ffn_in_grad, "blk", scatter_dimension=0, tiled=True),
        lax.psum_scatter(ffn_in_bias_grad, "blk", scatter_dimension=0, tiled=True),
        lax.psum_scatter(ffn_out_grad, "blk", scatter_dimension=0, tiled=True),
        lax.psum_scatter(ffn_out_bias_grad, "blk", scatter_dimension=0, tiled=True),
        lax.psum_scatter(norm2_gain_grad, "blk", scatter_dimension=0, tiled=True),
        lax.psum_scatter(norm2_bias_grad, "blk", scatter_dimension=0, tiled=True),
    )
    totals = (
        lax.psum(conv_weight_part.astype(jnp.bfloat16), "dp").astype(jnp.float32),
        lax.psum(conv_bias_part.astype(jnp.bfloat16), "dp").astype(jnp.float32),
        lax.psum(qkv_weight_part.astype(jnp.bfloat16), "dp").astype(jnp.float32),
        lax.psum(qv_bias_part.astype(jnp.bfloat16), "dp").astype(jnp.float32),
        lax.psum(out_weight_part.astype(jnp.bfloat16), "dp").astype(jnp.float32),
        lax.psum(out_bias_part.astype(jnp.bfloat16), "dp").astype(jnp.float32),
        lax.psum(gain_one_part.astype(jnp.bfloat16), "dp").astype(jnp.float32),
        lax.psum(shift_one_part.astype(jnp.bfloat16), "dp").astype(jnp.float32),
        lax.psum(ffn_in_part.astype(jnp.bfloat16), "dp").astype(jnp.float32),
        lax.psum(ffn_in_bias_part.astype(jnp.bfloat16), "dp").astype(jnp.float32),
        lax.psum(ffn_out_part.astype(jnp.bfloat16), "dp").astype(jnp.float32),
        lax.psum(ffn_out_bias_part.astype(jnp.bfloat16), "dp").astype(jnp.float32),
        lax.psum(gain_two_part.astype(jnp.bfloat16), "dp").astype(jnp.float32),
        lax.psum(shift_two_part.astype(jnp.bfloat16), "dp").astype(jnp.float32),
    )
    return (
        layer_out.reshape(row_count, block_len, model_width).astype(jnp.bfloat16),
        frames_grad,
        totals[0],
        totals[1],
        totals[2],
        totals[3],
        totals[4],
        totals[5],
        totals[6],
        totals[7],
        totals[8],
        totals[9],
        totals[10],
        totals[11],
        totals[12],
        totals[13],
    )


MESH = pl.DeviceIdType.MESH
LANES = 128
TAP_STEP = 16
VMEM = pl.BlockSpec(memory_space=pltpu.VMEM)


def peer(me, step, count):
    return lax.rem(me + step, count)


def greet(index, count, rows):
    barrier = pltpu.get_barrier_semaphore()
    for step in range(1, count * rows):
        other = lax.rem(index + step, count * rows)
        pl.semaphore_signal(
            barrier,
            inc=1,
            device_id={"dp": other // count, "blk": lax.rem(other, count)},
            device_id_type=MESH,
        )


def greet_wait(count, rows):
    pl.semaphore_wait(pltpu.get_barrier_semaphore(), count * rows - 1)


def remote(src, dst, send_sem, recv_sem, target, axis="blk"):
    copy = pltpu.make_async_remote_copy(
        src_ref=src,
        dst_ref=dst,
        send_sem=send_sem,
        recv_sem=recv_sem,
        device_id=target if isinstance(target, dict) else {axis: target},
        device_id_type=MESH,
    )
    copy.start()
    return copy


def turned(value):
    return value.astype(jnp.float32).T.astype(jnp.bfloat16)


def matmul_turned(left, right):
    return lax.dot_general(
        left, right, (((1,), (1,)), ((), ())), preferred_element_type=jnp.float32
    )


def sum_parts(parts_ref):
    total = parts_ref[0].astype(jnp.float32)
    for part in range(1, parts_ref.shape[0]):
        total = total + parts_ref[part].astype(jnp.float32)
    return total


def lane_block(index):
    return pl.ds(pl.multiple_of(index * LANES, LANES), LANES)


def row_block(index, size):
    return pl.ds(pl.multiple_of(index * size, size), size)


def swap_blocks(tiles, width):
    count = len(tiles)
    lane = lax.broadcasted_iota(jnp.int32, tiles[0].shape, 1) // width
    tiles = list(tiles)
    step = count // 2
    while step:
        low = (lane & step) == 0
        for u in range(count):
            if u & step == 0:
                one, two = tiles[u], tiles[u + step]
                tiles[u] = jnp.where(low, one, pltpu.roll(two, step * width, 1))
                tiles[u + step] = jnp.where(low, pltpu.roll(one, LANES - step * width, 1), two)
        step //= 2
    return tiles


def spread_taps(source, offset, direction, stage_ref, out_ref):
    rows, length = source.shape
    blocks = out_ref.shape[1] // LANES
    for tap in range(TAP_STEP):
        shift = (length - offset - direction * tap) % length
        moved = pltpu.roll(source, shift, 1)
        for block in range(blocks):
            first = block * rows * TAP_STEP + tap
            stage_ref[pl.ds(first, rows, stride=TAP_STEP), :] = moved[
                :, block * LANES : (block + 1) * LANES
            ]
    size = rows * TAP_STEP
    for block in range(blocks):
        out_ref[:, block * LANES : (block + 1) * LANES] = stage_ref[
            block * size : (block + 1) * size, :
        ].astype(jnp.bfloat16)


def query_span(index, size):
    return pl.ds(pl.multiple_of(index * size, size), size)


def same_clip(column_ref, seg_row):
    column = column_ref[...]
    parts = [
        column == seg_row[:, start : start + LANES]
        for start in range(0, seg_row.shape[1], LANES)
    ]
    return jnp.concatenate(parts, axis=1)


def clip_column(count, segs_ref, column_ref):
    for block in range(count):
        row = segs_ref[block].astype(jnp.float32)
        column_ref[block * LANES : (block + 1) * LANES, :] = jnp.broadcast_to(
            row, (LANES, LANES)
        ).T


def clip_row(segs_ref, first, size):
    parts = [segs_ref[first + i].astype(jnp.float32) for i in range(size // LANES)]
    return jnp.concatenate(parts, axis=1)


def layer_kernel(names, count, rows_count, head_dim, *refs):
    R = types.SimpleNamespace(**dict(zip(names, refs)))
    low, f32 = jnp.bfloat16, jnp.float32
    me, row = lax.axis_index("blk"), lax.axis_index("dp")
    level, side = me // 2, lax.rem(me, 2)
    levels = count // 2
    half = count // 2
    near = me + 1 - 2 * side
    core = lax.rem(row, 2)
    twin = row + 1 - 2 * core
    upper = level // 2
    pos = 4 * core + 2 * lax.rem(level, 2) + side
    home_row = 2 * (row // 2) + upper
    at_home = core == upper
    east = row // 2
    corner = 2 * side + core
    facing = peer(corner, 2, 4)
    across = peer(row, 2, rows_count)
    tokens, width = R.frames_hbm.shape
    channels = width // count
    length = count * LANES
    group_width = R.own_weight.shape[1]
    groups = channels // group_width
    steps = LANES // TAP_STEP
    scale = head_dim ** (-0.5)
    chunks = R.in_hbm.shape[1] // width

    def send(kind, step, source, target_ref, target, axis="blk"):
        return remote(
            source, target_ref, R.out_sem.at[kind, step], R.in_sem.at[kind, step], target, axis
        )

    def wait(copies):
        for copy in copies:
            copy.wait()

    def to_blocks(kind, source, target_ref):
        copies = []
        for step in range(1, count):
            target = peer(me, step, count)
            copies.append(send(kind, step, source(target), target_ref, target))
        return copies

    def device_at(place, part):
        return {"dp": 2 * (row // 2) + place // 4, "blk": 4 * part + lax.rem(place, 4)}

    def to_places(kind, source, target_ref):
        copies = []
        for step in range(1, count):
            target = peer(pos, step, count)
            copies.append(send(kind, step, source(target), target_ref, device_at(target, upper)))
        return copies

    def move(kind, source, target_ref, device):
        copy = pltpu.make_async_remote_copy(
            src_ref=source,
            dst_ref=target_ref,
            send_sem=R.out_sem.at[kind, 0],
            recv_sem=R.in_sem.at[kind, 0],
            device_id=device,
            device_id_type=MESH,
        )
        away = jnp.logical_not(at_home)
        pl.when(away)(copy.start)

        @pl.when(at_home)
        def _():
            target_ref[...] = source[...]

        return [(away, away, copy)]

    def shift_all(kind, first, own, device_of, source, target_ref):
        pending = []
        for step in range(count):
            target = peer(first, step, count)
            away = jnp.logical_not(jnp.logical_and(at_home, target == own))
            copy = pltpu.make_async_remote_copy(
                src_ref=source(target),
                dst_ref=target_ref,
                send_sem=R.out_sem.at[kind, step],
                recv_sem=R.in_sem.at[kind, step],
                device_id=device_of(target),
                device_id_type=MESH,
            )
            pl.when(away)(copy.start)
            pending.append((away, away, copy))

        @pl.when(at_home)
        def _():
            target_ref[...] = source(own)[...]

        return pending

    def to_level(kind, source, target_ref):
        return shift_all(
            kind, me, pos, lambda place: device_at(place, core), source, target_ref
        )

    def from_level(kind, source, target_ref):
        return shift_all(
            kind, pos, me, lambda block: {"dp": home_row, "blk": block}, source, target_ref
        )

    def wait_some(pending):
        for sends, comes, copy in pending:
            pl.when(sends)(copy.wait_send)
            pl.when(comes)(copy.wait_recv)

    def chunk_of(index):
        return slice(index * width, (index + 1) * width)

    def table(index):
        return R.table[index : index + 1, :]

    def dot(left, right):
        return jnp.dot(left, right, preferred_element_type=f32)

    greet(row * count + me, count, rows_count)

    loads = [pltpu.make_async_copy(R.qkv_hbm, R.qkv_w, R.load_sem.at[0])]
    loads.append(pltpu.make_async_copy(R.out_hbm, R.out_w, R.load_sem.at[1]))
    for chunk in range(chunks):
        span = chunk_of(chunk)
        loads.append(
            pltpu.make_async_copy(
                R.in_hbm.at[:, span], R.in_w.at[:, span], R.load_sem.at[2 + 2 * chunk]
            )
        )
        loads.append(
            pltpu.make_async_copy(
                R.back_hbm.at[span], R.back_w.at[span], R.load_sem.at[3 + 2 * chunk]
            )
        )
    for load in loads:
        load.start()
    own_load = pltpu.make_async_copy(
        R.conv_hbm.at[row_block(me, channels)], R.own_weight, R.load_sem.at[2 + 2 * chunks]
    )
    own_load.start()
    first_loads = [
        pltpu.make_async_copy(source, target, R.first_sem.at[index])
        for index, (source, target) in enumerate(
            ((R.frames_hbm, R.frames), (R.cotangent_hbm, R.cotangent))
        )
    ]
    for load in first_loads:
        load.start()
    first_loads[0].wait()
    valid = (R.segment[...] >= 0).astype(f32)
    R.turned[...] = (R.frames[...].astype(f32).T * valid).astype(low)
    to_level_device = device_at(me, core)
    from_level_device = {"dp": home_row, "blk": pos}

    R.table[...] = jnp.zeros_like(R.table)
    R.small[...] = jnp.zeros_like(R.small)
    place = 0
    for vector in VECTORS:
        ref = getattr(R, vector)
        for part in range(ref.shape[0] // width):
            R.table[place, :] = ref[chunk_of(part)].astype(f32)
            place += 1

    def mix_taps(mix, tile_rows):
        @pl.loop(0, group_width // steps)
        def _(block):
            for group in range(groups):
                tiles = [
                    R.stage[tile_rows(group, block * steps + u), :] for u in range(steps)
                ]
                for a, tile in enumerate(swap_blocks(tiles, TAP_STEP)):
                    rows = slice(a * group_width, (a + 1) * group_width)
                    mix[group, rows, lane_block(block)] = tile.astype(low)

    square = group_width * group_width
    own_load.wait()
    total_rows = channels * group_width
    R.stage[:total_rows, :] = R.own_weight[...].astype(f32).reshape(total_rows, LANES)
    mix_taps(R.mix, lambda g, i: pl.ds(g * square + i, group_width, stride=group_width))
    greet_wait(count, rows_count)

    copies = to_blocks(
        0, lambda p: R.turned.at[row_block(p, channels), :], R.column.at[:, lane_block(me + 1)]
    )
    R.column[:, lane_block(me + 1)] = R.turned[row_block(me, channels), :]
    for ref in (R.column, R.gcol):
        ref[:, :LANES] = jnp.zeros((channels, LANES), low)
        ref[:, length + LANES :] = jnp.zeros((channels, LANES), low)
    mix_taps(R.mix_back, lambda g, c: pl.ds(g * square + c * group_width, group_width))
    wait(copies)
    brought = move(33, R.frames, R.frames_home, to_level_device)
    seg_pending = to_level(1, lambda p: R.segment, R.segs.at[me])

    @pl.loop(0, groups)
    def _(group):
        rows = row_block(group, group_width)
        spread_taps(R.column[rows, :].astype(f32), LANES // 2, 1, R.stage, R.taps.at[group])
        product = dot(R.mix[group], R.taps[group])
        total = product[:group_width, :length]
        for a in range(1, steps):
            part = product[a * group_width : (a + 1) * group_width, :]
            part = pltpu.roll(part, product.shape[1] - a * TAP_STEP, 1)
            total = total + part[:, :length]
        R.result[rows, :] = total.astype(low)
    pending = to_level(
        2, lambda p: R.result.at[:, lane_block(p)], R.conv_home.at[row_block(me, channels), :]
    )
    @pl.loop(0, groups)
    def _(group):
        source = R.column[row_block(group, group_width), :].astype(f32)
        span = R.shifted.shape[2]
        for a in range(steps):
            moved = pltpu.roll(source, (span + LANES - a * TAP_STEP) % (span + LANES), 1)
            R.shifted[group, a * group_width : (a + 1) * group_width, :] = moved[:, :span].astype(
                low
            )
    wait_some(seg_pending)
    clip_column(count, R.segs, R.clip)
    wait_some(brought)
    wait_some(pending)

    pre = R.conv_home[...].astype(f32).T + table(0)
    share = 0.5 * (1.0 + lax.erf(pre * ROOT_HALF))
    R.slope[...] = share + pre * jnp.exp(-0.5 * pre * pre) * DENSITY_CONST
    mixed = R.frames_home[...].astype(f32) + pre * share
    R.mixed[...] = mixed
    mixed_low = mixed.astype(low)
    loads[0].wait()
    for part in range(3):
        block = dot(mixed_low, R.qkv_w[:, chunk_of(part)])
        if part != 1:
            block = block + table(1 + part // 2)
        block = block.astype(low).astype(f32)
        if part == 0:
            block = block * scale
        R.project[part] = block.T.astype(low)
    extra_copies = to_places(
        4,
        lambda p: R.project.at[:, row_block(count + p // 2, head_dim), :],
        R.extra.at[:, :, lane_block(pos)],
    )
    copies = to_places(
        3,
        lambda p: R.project.at[:, row_block(p, head_dim), :],
        R.main.at[:, :, lane_block(pos)],
    )
    R.main[:, :, lane_block(pos)] = R.project[:, row_block(pos, head_dim), :]
    R.extra[:, :, lane_block(pos)] = R.project[:, row_block(count + pos // 2, head_dim), :]
    R.left[0] = turned(mixed_low)
    last_row = rows_count - 1

    def to_some_rows(kind, source, sends_to, comes_to):
        pending = []
        for step in range(1, rows_count):
            target = peer(row, step, rows_count)
            copy = pltpu.make_async_remote_copy(
                src_ref=source,
                dst_ref=R.late_left.at[:, lane_block(row)],
                send_sem=R.out_sem.at[kind, step],
                recv_sem=R.in_sem.at[kind, step],
                device_id={"dp": target},
                device_id_type=MESH,
            )
            sends = sends_to(target)
            pl.when(sends)(copy.start)
            pending.append((sends, comes_to, copy))
        return pending

    left_pending = to_some_rows(8, R.left.at[0], lambda p: p != last_row, row != last_row)
    wait(extra_copies)

    size = 2 * LANES
    halves = half * LANES // size

    def scores_of(held, start, seg_row):
        scores = lax.dot_general(
            held[1], held[0, :, start], (((0,), (0,)), ((), ())), preferred_element_type=f32
        )
        return jnp.where(same_clip(R.clip, seg_row), scores, -1e30)

    def attend(held, start, index, att_ref, low_ref, lse_ref, place):
        scores = scores_of(held, start, clip_row(R.segs, index * 2, size))
        top = jnp.max(scores, axis=0, keepdims=True)
        weights = jnp.exp(scores - top)
        total = jnp.sum(weights, axis=0, keepdims=True)
        mean = dot(held[2], weights.astype(low)) / total
        att_ref[:, place] = mean
        low_ref[:, start] = mean.astype(low)
        lse_ref[:, place] = top + jnp.log(total)

    own_rows = row_block(pos, head_dim)
    extra_rows = row_block(count + pos // 2, head_dim)

    def to_half(kind, source, target_ref):
        pending = []
        for step in range(1, count):
            target, origin = peer(pos, step, count), peer(pos, count - step, count)
            copy = pltpu.make_async_remote_copy(
                src_ref=source(target),
                dst_ref=target_ref,
                send_sem=R.out_sem.at[kind, step],
                recv_sem=R.in_sem.at[kind, step],
                device_id=device_at(target, upper),
                device_id_type=MESH,
            )
            sends, comes = target // half == side, pos // half == lax.rem(origin, 2)
            pl.when(sends)(copy.start)
            pending.append((sends, comes, copy))
        return pending

    @pl.loop(0, halves)
    def _(block):
        index = side * halves + block
        place = query_span(block, size)
        attend(
            R.extra,
            query_span(index, size),
            index,
            R.att_extra,
            R.low_extra,
            R.lse_extra,
            place,
        )
    pending = to_half(5, lambda p: R.low_extra.at[:, lane_block(p)], R.att_home.at[extra_rows, :])

    @pl.when(pos // half == side)
    def _():
        R.att_home[extra_rows, :] = R.low_extra[:, lane_block(pos)]

    wait(copies)
    first_loads[1].wait()
    brought = move(34, R.cotangent, R.cotangent_home, to_level_device)

    @pl.loop(0, length // size)
    def _(block):
        span = query_span(block, size)
        attend(R.main, span, block, R.att_main, R.low_main, R.lse_main, span)

    copies = to_places(6, lambda p: R.low_main.at[:, lane_block(p)], R.att_home.at[own_rows, :])
    R.att_home[own_rows, :] = R.low_main[:, lane_block(pos)]
    wait(copies)
    wait_some(pending)

    def to_rows(kind, source, target_ref):
        return [
            send(kind, step, source(peer(row, step, rows_count)), target_ref, target, "dp")
            for step, target in ((n, peer(row, n, rows_count)) for n in range(1, rows_count))
        ]

    def share_start(kind, part, index=row, mate={"dp": across}):
        own = part(index)
        return [send(kind, 2, own, own, mate), send(kind, 1, own, own, twin, "dp")]

    def share_forward(kind, part, copies, index=across):
        copies[0].wait()
        got = part(index)
        copies[0] = send(kind, 3, got, got, twin, "dp")

    def lanes_of(ref):
        return lambda index: ref.at[:, lane_block(index)]

    R.left[1] = R.att_home[...]
    att = R.att_home[...].astype(f32).T.astype(low)
    loads[1].wait()
    branch = dot(att, R.out_w[...]) + table(3)
    hidden, normed_one, inv_one = norm_forward(R.mixed[...] + branch, table(4), table(5))
    hidden_low = hidden.astype(low)
    R.hidden_all[:, lane_block(corner)] = turned(hidden_low)
    hidden_copies = share_start(7, lanes_of(R.hidden_all), corner, {"blk": near})
    left_pending += to_some_rows(32, R.left.at[1], lambda p: p == last_row, row == last_row)
    R.late_left[:, lane_block(row)] = R.left[row // last_row]
    pieces = count // chunks
    for load in loads[2:]:
        load.wait()
    R.total[...] = hidden + table(10)

    @pl.loop(0, chunks)
    def _(chunk):
        span = query_span(chunk, width)
        pre = dot(hidden_low, R.in_w[:, span]) + R.table[pl.ds(6 + chunk, 1), :]
        share = 0.5 * (1.0 + lax.erf(pre * ROOT_HALF))
        act = (pre * share).astype(low)
        R.keep[:, span] = share + pre * jnp.exp(-0.5 * pre * pre) * DENSITY_CONST
        R.act_turned[pl.ds(chunk * pieces, pieces)] = turned(act).reshape(
            pieces, rows_count, -1, LANES
        )
        R.total[...] += dot(act, R.back_w[row_block(chunk, width), :])

    act_copies = to_rows(9, lambda p: R.act_turned.at[:, p], R.act_all.at[:, :, lane_block(row)])
    R.act_all[:, :, lane_block(row)] = R.act_turned[:, row]
    layer, normed_two, inv_two = norm_forward(R.total[...], table(11), table(12))
    R.layer_here[...] = layer.astype(low)
    wait_some(brought)
    grad_second, gain_sum, shift_sum = norm_backward(
        R.cotangent_home[...].astype(f32), normed_two, inv_two, table(11)
    )
    R.small[11, :] = gain_sum
    R.small[12, :] = shift_sum
    grad_two = grad_second.astype(low)
    R.two_all[:, lane_block(row)] = turned(grad_two)
    two_copies = share_start(10, lanes_of(R.two_all))
    R.small[10, :] = jnp.sum(grad_two.astype(f32), axis=0)
    R.total[...] = grad_second

    @pl.loop(0, chunks)
    def _(chunk):
        span = query_span(chunk, width)
        grad_pre = matmul_turned(grad_two, R.back_w[row_block(chunk, width), :]) * R.keep[:, span]
        grad_pre = grad_pre.astype(low)
        R.pre_turned[chunk] = turned(grad_pre)
        R.small[pl.ds(6 + chunk, 1), :] = jnp.sum(grad_pre.astype(f32), axis=0, keepdims=True)
        R.total[...] += matmul_turned(grad_pre, R.in_w[:, span])

    grad_first, gain_sum, shift_sum = norm_backward(R.total[...], normed_one, inv_one, table(4))
    R.small[4, :] = gain_sum
    R.small[5, :] = shift_sum
    R.mixed[...] = grad_first
    grad_branch = grad_first.astype(low)
    R.small[3, :] = jnp.sum(grad_branch.astype(f32), axis=0)
    R.turned[...] = turned(matmul_turned(grad_branch, R.out_w[...]).astype(low))

    extra_copies = to_places(
        12,
        lambda p: R.turned.at[row_block(count + p // 2, head_dim), :],
        R.gextra.at[:, lane_block(pos)],
    )
    copies = to_places(
        11, lambda p: R.turned.at[row_block(p, head_dim), :], R.gmain.at[:, lane_block(pos)]
    )
    R.gmain[:, lane_block(pos)] = R.turned[row_block(pos, head_dim), :]
    R.gextra[:, lane_block(pos)] = R.turned[row_block(count + pos // 2, head_dim), :]
    pre_copies = []
    for step in range(1, 4):
        target = peer(corner, step, 4)
        device = {"dp": 2 * east + lax.rem(target, 2), "blk": 2 * level + target // 2}
        pre_copies.append(
            send(13, step, R.pre_turned.at[target], R.pre_all.at[:, lane_block(corner)], device)
        )
    R.pre_all[:, lane_block(corner)] = R.pre_turned[corner]
    R.dproject[3] = turned(grad_branch)
    wait(extra_copies)
    layer_pending = move(35, R.layer_here, R.layer_got, from_level_device)
    share_forward(10, lanes_of(R.two_all), two_copies)

    def attend_back(held, grads, start, index, att, lse):
        queries = held[0, :, start]
        weights = jnp.exp(scores_of(held, start, clip_row(R.segs, index * 2, size)) - lse)
        grad_prob = lax.dot_general(
            held[2], grads, (((0,), (0,)), ((), ())), preferred_element_type=f32
        )
        delta = jnp.sum(grads.astype(f32) * att, axis=0, keepdims=True)
        grad_score = (weights * (grad_prob - delta)).astype(low)
        return (
            dot(held[1], grad_score) * scale,
            matmul_turned(queries, grad_score),
            matmul_turned(grads, weights.astype(low)),
        )

    R.dkey[...] = jnp.zeros_like(R.dkey)
    R.dvalue[...] = jnp.zeros_like(R.dvalue)

    @pl.loop(0, halves)
    def _(block):
        index = side * halves + block
        span = query_span(index, size)
        place = query_span(block, size)
        parts = attend_back(
            R.extra, R.gextra[:, span], span, index, R.att_extra[:, place], R.lse_extra[:, place]
        )
        R.dextra[0, :, span] = parts[0].astype(low)
        R.dkey[...] += parts[1]
        R.dvalue[...] += parts[2]

    R.dextra[1] = R.dkey[...].astype(low)
    R.dextra[2] = R.dvalue[...].astype(low)
    part_rows = row_block(pos // 2, head_dim)
    wait(copies)
    copies = to_places(
        14, lambda p: R.dextra.at[1:3, :, lane_block(p)], R.halves.at[side, :, part_rows, :]
    )
    pending = to_half(
        15, lambda p: R.dextra.at[0, :, lane_block(p)], R.dproject.at[0, extra_rows, :]
    )
    R.halves[side, :, part_rows, :] = R.dextra[1:3, :, lane_block(pos)]

    @pl.when(pos // half == side)
    def _():
        R.dproject[0, extra_rows, :] = R.dextra[0, :, lane_block(pos)]

    lower = lax.rem(level, 2)
    level_mate = me + 2 - 4 * lower
    upper_mate = me + 4 - 8 * upper

    modes = {
        "side": (side, {"blk": near}, lower, {"blk": level_mate}),
        "east": (east, {"dp": across}, lower, {"blk": level_mate}),
        "level": (lower, {"blk": level_mate}, side, {"blk": near}),
    }

    def shard(u, bit, other, mode):
        return row_block(4 * u + (2 * bit + other if mode == "level" else 2 * other + bit), channels)

    def sum_begin(kind, slot, source, span, mode):
        bit, mate, _, _ = modes[mode]
        return [
            send(
                kind,
                2 * u + v,
                R.in_w.at[shard(u, 1 - bit, v, mode), source],
                R.got_one.at[slot, 2 * u + v, :, span],
                mate,
            )
            for u in range(2)
            for v in range(2)
        ]

    def sum_next(kind, slot, source, span, mode, copies):
        wait(copies)
        bit, _, other, mate = modes[mode]
        for u in range(2):
            for v in range(2):
                own = R.in_w[shard(u, bit, v, mode), source]
                got = R.got_one[slot, 2 * u + v, :, span]
                R.sum_one[slot, 2 * u + v, :, span] = (own.astype(f32) + got.astype(f32)).astype(
                    low
                )
        return [
            send(
                kind,
                u,
                R.sum_one.at[slot, 2 * u + 1 - other, :, span],
                R.got_two.at[slot, u, :, span],
                mate,
            )
            for u in range(2)
        ]

    def sum_last(kind, slot, span, mode, copies):
        wait(copies)
        other = modes[mode][2]
        for u in range(2):
            own = R.sum_one[slot, 2 * u + other, :, span]
            got = R.got_two[slot, u, :, span]
            R.sum_two[slot, u, :, span] = (own.astype(f32) + got.astype(f32)).astype(low)
        return [
            send(
                kind,
                0,
                R.sum_two.at[slot, 1 - upper, :, span],
                R.got_three.at[slot, :, span],
                upper_mate,
            )
        ]

    def summed(slot, copies):
        wait(copies)
        return (R.sum_two[slot, upper].astype(f32) + R.got_three[slot].astype(f32)).astype(low)

    every = slice(0, width)
    in_span, out_span = chunk_of(0), chunk_of(1)
    stores = []

    def store(index, source, target):
        copy = pltpu.make_async_copy(source, target, R.store_sem.at[index])
        copy.start()
        stores.append(copy)

    blocks = length // size

    def main_back(block):
        span = query_span(block, size)
        parts = attend_back(
            R.main, R.gmain[:, span], span, block, R.att_main[:, span], R.lse_main[:, span]
        )
        R.dmain[0, :, span] = parts[0].astype(low)
        for place in range(size // LANES):
            target = block * (size // LANES) + place
            pl.when(target != pos)(query_copy(target).start)
        R.dkey[...] += parts[1]
        R.dvalue[...] += parts[2]

    def query_copy(target):
        step = lax.rem(target - pos + count, count)
        return pltpu.make_async_remote_copy(
            src_ref=R.dmain.at[0, :, lane_block(target)],
            dst_ref=R.dproject.at[0, own_rows, :],
            send_sem=R.out_sem.at[16, step],
            recv_sem=R.in_sem.at[16, step],
            device_id=device_at(target, upper),
            device_id_type=MESH,
        )

    R.dkey[...] = jnp.zeros_like(R.dkey)
    R.dvalue[...] = jnp.zeros_like(R.dvalue)
    share_forward(7, lanes_of(R.hidden_all), hidden_copies, facing)
    wait(two_copies)
    wait(act_copies)
    product = matmul_turned(R.act_all[...].reshape(width, -1), R.two_all[...])
    R.in_w[:, out_span] = product.astype(low)
    out_copies = sum_begin(18, 1, out_span, every, "level")
    pl.loop(0, blocks // 2)(main_back)
    wait(hidden_copies)
    wait(pre_copies)
    R.in_w[:, in_span] = matmul_turned(R.hidden_all[...], R.pre_all[...]).astype(low)
    in_copies = sum_begin(17, 0, in_span, every, "east")
    pl.loop(blocks // 2, blocks)(main_back)
    R.dmain[1] = R.dkey[...].astype(low)
    R.dmain[2] = R.dvalue[...].astype(low)
    copies += to_places(
        44, lambda p: R.dmain.at[1:3, :, lane_block(p)], R.dproject.at[1:3, own_rows, :]
    )
    copies += [query_copy(peer(pos, step, count)) for step in range(1, count)]
    R.dproject[0:3, own_rows, :] = R.dmain[:, :, lane_block(pos)]
    out_copies = sum_next(23, 1, out_span, every, "level", out_copies)
    wait(copies)
    wait_some(pending)
    first = half * head_dim
    for which in range(2):
        total = R.halves[0, which].astype(f32) + R.halves[1, which].astype(f32)
        R.dproject[1 + which, width - first :, :] = total.astype(low)

    late = to_rows(19, lambda p: R.dproject.at[p], R.late_right.at[:, lane_block(row)])
    R.late_right[:, lane_block(row)] = R.dproject[row]
    grad_mixed = R.mixed[...]
    for part in range(3):
        block = R.dproject[part].astype(f32).T
        if part != 1:
            R.small[1 + part // 2, :] = jnp.sum(block, axis=0)
        grad_mixed = grad_mixed + matmul_turned(block.astype(low), R.qkv_w[:, chunk_of(part)])
    R.mixed_here[...] = grad_mixed.astype(low)
    grad_conv = (grad_mixed * R.slope[...]).astype(low)
    R.conv_turned[...] = turned(grad_conv)
    conv_pending = from_level(
        20, lambda b: R.conv_turned.at[row_block(b, channels), :], R.gcol.at[:, lane_block(pos + 1)]
    )
    R.small[0, :] = jnp.sum(grad_conv.astype(f32), axis=0)
    small_copy = send(21, 0, R.small, R.small_got.at[0], twin, "dp")
    in_copies = sum_next(22, 0, in_span, every, "east", in_copies)
    out_copies = sum_last(37, 1, every, "level", out_copies)
    wait_some(conv_pending)
    mixed_pending = move(36, R.mixed_here, R.mixed_got, from_level_device)

    @pl.loop(0, groups)
    def _(group):
        rows = row_block(group, group_width)
        spread_taps(R.gcol[rows, :].astype(f32), LANES // 2, -1, R.stage, R.taps.at[group])

    quarter = channels // rows_count

    @pl.loop(0, groups)
    def _(group):
        grad = matmul_turned(R.shifted[group], R.taps[group])
        for block in range(group_width // steps):
            span = slice(block * LANES, (block + 1) * LANES)
            tiles = [
                grad[a * group_width : (a + 1) * group_width, span] for a in range(steps)
            ]
            for u, tile in enumerate(swap_blocks(tiles, TAP_STEP)):
                channel = block * steps + u
                R.conv_part[group, channel // quarter, channel % quarter] = tile.astype(low)
    conv_copy = send(25, 0, R.conv_part.at[:, 1 - core], R.conv_got, twin, "dp")
    wait(late)
    wait_some(left_pending)
    product = matmul_turned(R.late_left[...], R.late_right[...])
    R.in_w[:, chunk_of(2)] = product.astype(low)
    middle = width // 2
    parts = (
        (26, slice(2 * width, 2 * width + middle), slice(0, middle), "side"),
        (28, slice(2 * width + middle, 3 * width), slice(middle, width), "level"),
    )
    att_copies = [sum_begin(kind, 2, source, span, first) for kind, source, span, first in parts]
    in_copies = sum_last(38, 0, every, "east", in_copies)
    def slots_of(ref):
        return lambda index: ref.at[index]

    R.out_sums[row] = summed(1, out_copies)
    out_share = share_start(43, slots_of(R.out_sums))
    @pl.loop(0, groups)
    def _(group):
        rows = row_block(group, group_width)
        product = dot(R.mix_back[group], R.taps[group])
        total = product[:group_width, LANES:]
        for a in range(1, steps):
            part = product[a * group_width : (a + 1) * group_width, :]
            total = total + pltpu.roll(part, a * TAP_STEP, 1)[:, LANES:]
        R.result[rows, :] = total.astype(low)
    back = to_blocks(
        24, lambda p: R.result.at[:, lane_block(p)], R.back_home.at[row_block(me, channels), :]
    )
    R.back_home[row_block(me, channels), :] = R.result[:, lane_block(me)]
    conv_copy.wait()
    for part in range(2):
        R.conv_sum[part] = (
            R.conv_part[part, core].astype(f32) + R.conv_got[part].astype(f32)
        ).astype(low)
    conv_copy = send(25, 1, R.conv_sum.at[1 - row // 2], R.conv_far, across, "dp")
    att_copies = [
        sum_next(kind + 1, 2, source, span, first, copies)
        for (kind, source, span, first), copies in zip(parts, att_copies)
    ]
    small_copy.wait()
    R.small_sum[0] = R.small[...] + R.small_got[0]
    small_copy = send(21, 1, R.small_sum.at[0], R.small_got.at[1], across, "dp")
    settled = side == east
    R.in_part[...] = summed(0, in_copies)

    def in_send(step, source, slot, device):
        return pltpu.make_async_remote_copy(
            src_ref=source,
            dst_ref=R.in_sums.at[slot],
            send_sem=R.out_sem.at[40, step],
            recv_sem=R.in_sem.at[40, step],
            device_id=device,
            device_id_type=MESH,
        )

    in_near = in_send(0, R.in_part, corner, {"blk": near})
    in_far = [
        in_send(1 + n, R.in_sums.at[slot], slot, {"dp": across})
        for n, slot in enumerate((corner, facing))
    ]

    @pl.when(jnp.logical_not(settled))
    def _():
        in_near.start()

    @pl.when(settled)
    def _():
        R.in_sums[corner] = R.in_part[...]
        in_far[0].start()

    small_copy.wait()
    R.small_sum[1] = R.small_sum[0] + R.small_got[1]
    small_copy = send(21, 2, R.small_sum.at[1], R.small_got.at[2], near)

    conv_copy.wait()
    R.conv_sums[row] = (
        R.conv_sum[row // 2].astype(f32) + R.conv_far[...].astype(f32)
    ).astype(low)
    conv_share = share_start(42, slots_of(R.conv_sums))
    att_copies = [
        sum_last(kind + 13, 2, span, first, copies)
        for (kind, source, span, first), copies in zip(parts, att_copies)
    ]
    share_forward(43, slots_of(R.out_sums), out_share)
    wait(back)
    wait_some(mixed_pending)
    R.frames_done[...] = (
        R.mixed_got[...].astype(f32) + (R.back_home[...].astype(f32) * valid).T
    ).astype(low)
    store(0, R.frames_done, R.frames_out)
    wait_some(layer_pending)
    store(1, R.layer_got, R.layer_out)
    @pl.when(settled)
    def _():
        in_near.wait_recv()
        in_far[1].start()

    small_copy.wait()
    R.small_far[level] = R.small_sum[1] + R.small_got[2]
    smalls = []
    for step in range(1, levels):
        target = 2 * peer(level, step, levels) + side
        smalls.append(
            send(30, step, R.small_far.at[level], R.small_far.at[level], target)
        )

    share_forward(42, slots_of(R.conv_sums), conv_share)
    R.attn_sums[row] = summed(2, att_copies[0] + att_copies[1])
    att_share = share_start(31, slots_of(R.attn_sums))
    wait(smalls)
    R.small_done[...] = sum_parts(R.small_far)
    store(2, R.small_done, R.small_out)

    @pl.when(settled)
    def _():
        in_far[0].wait_send()
        in_far[1].wait_send()

    @pl.when(jnp.logical_not(settled))
    def _():
        in_near.wait_send()
        in_far[0].wait_recv()
        in_far[1].wait_recv()

    in_share = [
        send(40, 3 + n, R.in_sums.at[slot], R.in_sums.at[slot], twin, "dp")
        for n, slot in enumerate((corner, facing))
    ]
    wait(out_share)
    store(3, R.out_sums, R.back_out)
    wait(in_share)
    store(6, R.in_sums, R.in_out)
    wait(conv_share)
    store(4, R.conv_sums, R.conv_out)
    share_forward(31, slots_of(R.attn_sums), att_share)
    wait(att_share)
    store(5, R.attn_sums, R.attn_out)
    for copy in stores:
        copy.wait()


VECTORS = (
    "conv_bias",
    "qv_bias",
    "out_bias",
    "gain_one",
    "shift_one",
    "in_bias",
    "back_bias",
    "gain_two",
    "shift_two",
)


def layer(count, rows_count, head_dim, named):
    low, f32 = jnp.bfloat16, jnp.float32
    tokens, width = named["frames_hbm"].shape
    wide = named["in_hbm"].shape[1]
    _, group_width, kernel = named["conv_hbm"].shape
    channels = width // count
    groups = channels // group_width
    length = count * LANES
    span = length + LANES
    steps = kernel // TAP_STEP
    taps = group_width * TAP_STEP
    every = rows_count * tokens
    piece = channels // rows_count
    extras = count // 2 * head_dim
    levels = count // 2
    outs = {
        "layer_out": ((tokens, width), low),
        "frames_out": ((tokens, width), low),
        "conv_out": ((rows_count, piece, group_width, kernel), low),
        "in_out": ((rows_count, channels, width), low),
        "back_out": ((rows_count, channels, width), low),
        "attn_out": ((rows_count, channels, width), low),
        "small_out": ((16, width), f32),
    }
    scratch = {
        "qkv_w": (named["qkv_hbm"].shape, low),
        "out_w": (named["out_hbm"].shape, low),
        "in_w": (named["in_hbm"].shape, low),
        "back_w": (named["back_hbm"].shape, low),
        "table": ((16, width), f32),
        "small": ((16, width), f32),
        "small_got": ((3, 16, width), f32),
        "small_sum": ((2, 16, width), f32),
        "small_far": ((levels, 16, width), f32),
        "turned": ((width, tokens), low),
        "conv_turned": ((width, tokens), low),
        "column": ((channels, span + LANES), low),
        "gcol": ((channels, span + LANES), low),
        "segs": ((count, 1, LANES), jnp.int32),
        "clip": ((length, LANES), f32),
        "stage": ((span // LANES * taps, LANES), f32),
        "own_weight": ((channels, group_width, kernel), low),
        "frames_home": ((tokens, width), low),
        "frames": ((tokens, width), low),
        "cotangent": ((tokens, width), low),
        "cotangent_home": ((tokens, width), low),
        "layer_here": ((tokens, width), low),
        "mixed_here": ((tokens, width), low),
        "mixed_got": ((tokens, width), low),
        "taps": ((groups, taps, span), low),
        "mix": ((groups, steps * group_width, taps), low),
        "mix_back": ((groups, steps * group_width, taps), low),
        "shifted": ((groups, steps * group_width, span), low),
        "result": ((channels, length), low),
        "conv_home": ((width, tokens), low),
        "back_home": ((width, tokens), low),
        "slope": ((tokens, width), f32),
        "mixed": ((tokens, width), f32),
        "project": ((3, width, tokens), low),
        "main": ((3, head_dim, length), low),
        "extra": ((3, head_dim, length), low),
        "att_main": ((head_dim, length), f32),
        "att_extra": ((head_dim, length // 2), f32),
        "low_main": ((head_dim, length), low),
        "low_extra": ((head_dim, length), low),
        "lse_main": ((1, length), f32),
        "lse_extra": ((1, length // 2), f32),
        "att_home": ((width, tokens), low),
        "keep": ((tokens, wide), f32),
        "total": ((tokens, width), f32),
        "dkey": ((head_dim, length), f32),
        "dvalue": ((head_dim, length), f32),
        "left": ((2, width, tokens), low),
        "act_turned": ((count, rows_count, wide // (count * rows_count), tokens), low),
        "pre_turned": ((rows_count, width, tokens), low),
        "hidden_all": ((width, every), low),
        "two_all": ((width, every), low),
        "pre_all": ((width, every), low),
        "act_all": ((count, wide // (count * rows_count), every), low),
        "late_left": ((width, every), low),
        "late_right": ((width, every), low),
        "gmain": ((head_dim, length), low),
        "gextra": ((head_dim, length), low),
        "dmain": ((3, head_dim, length), low),
        "dextra": ((3, head_dim, length), low),
        "dproject": ((4, width, tokens), low),
        "halves": ((2, 2, extras, tokens), low),
        "got_one": ((3, 4, channels, width), low),
        "sum_one": ((3, 4, channels, width), low),
        "got_two": ((3, 2, channels, width), low),
        "sum_two": ((3, 2, channels, width), low),
        "got_three": ((3, channels, width), low),
        "layer_got": ((tokens, width), low),
        "frames_done": ((tokens, width), low),
        "small_done": ((16, width), f32),
        "in_sums": ((rows_count, channels, width), low),
        "in_part": ((channels, width), low),
        "out_sums": ((rows_count, channels, width), low),
        "conv_sums": ((rows_count, piece, group_width, kernel), low),
        "attn_sums": ((rows_count, channels, width), low),
        "conv_part": ((2, 2, piece, group_width, kernel), low),
        "conv_got": ((2, piece, group_width, kernel), low),
        "conv_sum": ((2, piece, group_width, kernel), low),
        "conv_far": ((piece, group_width, kernel), low),
    }
    hbm = pl.BlockSpec(memory_space=pl.ANY)
    names = (*named, *outs, *scratch, "out_sem", "in_sem", "load_sem", "store_sem", "first_sem")
    return pl.pallas_call(
        functools.partial(layer_kernel, names, count, rows_count, head_dim),
        out_shape=tuple(jax.ShapeDtypeStruct(*out) for out in outs.values()),
        in_specs=[hbm if name.endswith("_hbm") else VMEM for name in named],
        out_specs=(hbm,) * len(outs),
        scratch_shapes=[pltpu.VMEM(*item) for item in scratch.values()]
        + [
            pltpu.SemaphoreType.DMA((45, count)),
            pltpu.SemaphoreType.DMA((45, count)),
            pltpu.SemaphoreType.DMA((3 + 2 * (wide // width),)),
            pltpu.SemaphoreType.DMA((len(outs),)),
            pltpu.SemaphoreType.DMA((2,)),
        ],
        compiler_params=pltpu.CompilerParams(
            collective_id=0, has_side_effects=True, vmem_limit_bytes=62 * 2**20
        ),
        name="layer",
    )(*named.values())


def unpack_kernel(
    count,
    layer_hbm,
    frames_hbm,
    conv_hbm,
    in_hbm,
    back_hbm,
    attn_hbm,
    small_hbm,
    layer_out,
    frames_out,
    conv_out,
    conv_bias,
    qkv_out,
    qv_bias,
    out_out,
    out_bias,
    gain_one,
    shift_one,
    in_out,
    in_bias,
    back_out,
    back_bias,
    gain_two,
    shift_two,
    conv_wide,
    qkv_wide,
    out_wide,
    in_wide,
    back_wide,
    conv_ref,
    in_ref,
    back_ref,
    attn_ref,
    small_ref,
    layer_ref,
    frames_ref,
    spare,
    sems,
):
    f32 = jnp.float32
    me = lax.axis_index("blk")
    rows_count, channels, width = attn_ref.shape
    piece = conv_ref.shape[1]
    copies = []

    def start(source, target):
        copy = pltpu.make_async_copy(source, target, sems.at[len(copies)])
        copy.start()
        copies.append(copy)

    loads = [
        pltpu.make_async_copy(source, target, sems.at[6 + rows_count + i])
        for i, (source, target) in enumerate(
            (
                (conv_hbm, conv_ref),
                (in_hbm, in_ref),
                (back_hbm, back_ref),
                (attn_hbm, attn_ref),
                (small_hbm, small_ref),
                (layer_hbm, layer_ref),
                (frames_hbm, frames_ref),
            )
        )
    ]
    for load in loads:
        load.start()
    loads[0].wait()
    for row in range(rows_count):
        part = slice(row * piece, (row + 1) * piece)
        conv_wide[part] = conv_ref[row].astype(f32)
        start(conv_wide.at[part], conv_out.at[part])
    loads[1].wait()
    for row in range(rows_count):
        in_wide[:, row * width : (row + 1) * width] = in_ref[row].astype(f32)
    start(in_wide, in_out)
    loads[2].wait()
    for row in range(rows_count):
        back_wide[row * channels : (row + 1) * channels, :] = back_ref[row].astype(f32)
    start(back_wide, back_out)
    loads[3].wait()
    for row in range(rows_count - 1):
        qkv_wide[:, row * width : (row + 1) * width] = attn_ref[row].astype(f32)
    start(qkv_wide, qkv_out)
    out_wide[...] = attn_ref[rows_count - 1].astype(f32)
    start(out_wide, out_out)
    loads[5].wait()
    start(layer_ref, layer_out)
    loads[6].wait()
    start(frames_ref, frames_out)
    loads[4].wait()
    small = small_ref[...]
    own = pltpu.roll(small, lax.rem(width - channels * me, width), 1)
    for place, ref in (
        (0, conv_bias),
        (3, out_bias),
        (4, gain_one),
        (5, shift_one),
        (10, back_bias),
        (11, gain_two),
        (12, shift_two),
    ):
        ref[...] = own[place, :channels]
    for first, parts, ref in ((1, 2, qv_bias), (6, rows_count, in_bias)):
        size = parts * channels
        inside = count // parts
        spare[...] = pltpu.roll(small, lax.rem(width - size * lax.rem(me, inside), width), 1)
        ref[...] = spare[pl.ds(first + me // inside, 1), :][0, :size]
    for copy in copies:
        copy.wait()


def unpack(count, layer_out, frames_out, conv, ffn_in, ffn_out, attn, small):
    rows_count, channels, width = attn.shape
    piece, group_width, kernel = conv.shape[1:]
    f32 = jnp.float32
    hbm = pl.BlockSpec(memory_space=pl.ANY)
    vector = jax.ShapeDtypeStruct((channels,), f32)
    conv_type = jax.ShapeDtypeStruct((rows_count * piece, group_width, kernel), f32)
    qkv_type = jax.ShapeDtypeStruct((channels, (rows_count - 1) * width), f32)
    out_type = jax.ShapeDtypeStruct((channels, width), f32)
    in_type = jax.ShapeDtypeStruct((channels, rows_count * width), f32)
    back_type = jax.ShapeDtypeStruct((rows_count * channels, width), f32)
    results = pl.pallas_call(
        functools.partial(unpack_kernel, count),
        out_shape=(
            jax.ShapeDtypeStruct(layer_out.shape, layer_out.dtype),
            jax.ShapeDtypeStruct(frames_out.shape, frames_out.dtype),
            conv_type,
            vector,
            qkv_type,
            jax.ShapeDtypeStruct((2 * channels,), f32),
            out_type,
            vector,
            vector,
            vector,
            in_type,
            jax.ShapeDtypeStruct((rows_count * channels,), f32),
            back_type,
            vector,
            vector,
            vector,
        ),
        in_specs=[hbm] * 7,
        out_specs=(
            hbm,
            hbm,
            hbm,
            VMEM,
            hbm,
            VMEM,
            hbm,
            VMEM,
            VMEM,
            VMEM,
            hbm,
            VMEM,
            hbm,
            VMEM,
            VMEM,
            VMEM,
        ),
        scratch_shapes=[
            pltpu.VMEM(item.shape, f32)
            for item in (conv_type, qkv_type, out_type, in_type, back_type)
        ]
        + [pltpu.VMEM(item.shape, item.dtype) for item in (conv, ffn_in, ffn_out, attn, small, layer_out, frames_out)]
        + [pltpu.VMEM(small.shape, f32), pltpu.SemaphoreType.DMA((13 + rows_count,))],
        compiler_params=pltpu.CompilerParams(vmem_limit_bytes=62 * 2**20),
        name="unpack",
    )(layer_out, frames_out, conv, ffn_in, ffn_out, attn, small)
    return (results[0][None], results[1][None], *results[2:])


def shards(sizes, *arrays):
    frames, segment, conv_weight = arrays[:3]
    row_count, block_len, model_width = frames.shape
    group_width, kernel = conv_weight.shape[1:]
    count = sizes["blk"]
    head_dim = model_width // HEADS
    channels = model_width // count
    fits = (
        row_count == 1
        and block_len == LANES
        and kernel == LANES
        and channels % group_width == 0
        and group_width % TAP_STEP == 0
        and count % 4 == 0
        and 2 * HEADS == 3 * count
        and head_dim % TAP_STEP == 0
        and sizes["dp"] == 4
        and count % sizes["dp"] == 0
        and arrays[10].shape[1] == 4 * model_width
    )
    if fits:
        return swap_shards(count, sizes["dp"], *arrays)
    return ring_shards(*arrays)


def swap_shards(
    count,
    rows_count,
    frames,
    segment,
    conv_weight,
    conv_bias,
    qkv_weight,
    qv_bias,
    out_weight,
    out_bias,
    norm1_gain,
    norm1_bias,
    ffn_in,
    ffn_in_bias,
    ffn_out,
    ffn_out_bias,
    norm2_gain,
    norm2_bias,
    cotangent,
):
    named = {
        "frames_hbm": frames[0],
        "segment": segment,
        "cotangent_hbm": cotangent[0],
        "conv_bias": conv_bias,
        "qv_bias": qv_bias,
        "out_bias": out_bias,
        "gain_one": norm1_gain,
        "shift_one": norm1_bias,
        "in_bias": ffn_in_bias,
        "back_bias": ffn_out_bias,
        "gain_two": norm2_gain,
        "shift_two": norm2_bias,
        "conv_hbm": conv_weight,
        "qkv_hbm": qkv_weight,
        "out_hbm": out_weight,
        "in_hbm": ffn_in,
        "back_hbm": ffn_out,
    }
    width = frames.shape[2]
    results = layer(count, rows_count, width // HEADS, named)
    return unpack(count, *results)


def solution(mesh):
    return jax.shard_map(
        functools.partial(shards, mesh.shape),
        mesh=mesh,
        in_specs=(
            P("dp", "blk", None),
            P("dp", "blk"),
            P(),
            P(),
            P(),
            P(),
            P(),
            P(),
            P(),
            P(),
            P(),
            P(),
            P(),
            P(),
            P(),
            P(),
            P("dp", "blk", None),
        ),
        out_specs=(
            P("dp", "blk", None),
            P("dp", "blk", None),
            P("blk", None, None),
            P("blk"),
            P("blk", None),
            P("blk"),
            P("blk", None),
            P("blk"),
            P("blk"),
            P("blk"),
            P("blk", None),
            P("blk"),
            P("blk", None),
            P("blk"),
            P("blk"),
            P("blk"),
        ),
        check_vma=False,
    )
```
